512 devices in a mesh: tm: 32 (over z, core), row: 16 (over y, x).
Axes of the slice: x: 4, y: 4, z: 16, core: 2. Of those that a mesh axis runs over, the one named last changes fastest.
Arguments:
- lower_factor: bfloat16 [64, 1024, 1024], P('tm', 'row'), may hold values from -0.1875 to 0.1875
- arrow_factor: bfloat16 [64, 1024, 512], P('tm', 'row'), may hold values from -0.25 to 0.25
- block_inverse: bfloat16 [64, 1024, 1024], P('tm', 'row'), as said below
- boundary_sigma: bfloat16 [32, 1024, 1024], P('tm', 'row'), as said below
- boundary_tip: bfloat16 [32, 1024, 512], P('tm', 'row'), may hold values from -3 to 3
- tip_inverse: bfloat16 [512, 512], replicated, as said below
- slope_weights: float32 [64, 1024], P('tm', 'row'), may hold values from 0.1 to 1
Outputs:
- sigma_diag: float32 [64, 1024, 1024], P('tm', 'row')
- sigma_lower: float32 [64, 1024, 1024], P('tm', 'row')
- sigma_tip: float32 [64, 1024, 512], P('tm', 'row')
- logdet_slope: float32 [], replicated
The draws below stay inside these ranges and needn't reach their ends.
Inputs may be any that keep to these rules, and one draw needn't show every extreme that they name: `block_inverse`: each block is symmetric with a diagonal part of order one. `boundary_sigma`: each block is symmetric with a diagonal part of order one. `tip_inverse`: symmetric with a diagonal part of order one.
All inputs are finite; a program needn't handle non-finite values.
Results may differ from the reference program's by a relative error of at most 0.0041.
Values may be sent and summed in bfloat16 or wider, within the bound.
No kernel may reach another device: no remote copies, remote signals or barrier semaphores. Data moves between devices by JAX's collectives and lax.ppermute only.
A program may use at most 64 MiB of HBM per device.

```python
import math
import jax
import jax.numpy as jnp
from jax import lax

B = 1024
A = 512
K = 2
PARTITIONS = 32
BLOCKS = 64


def symmetric_blocks(noise, diag_key, count, order, spread):
    scales = jnp.exp(jax.random.uniform(diag_key, (count, order), jnp.float32, jnp.log(0.5), jnp.log(2.0)))
    eye = jnp.eye(order, dtype=jnp.float32)
    return eye[None, :, :] * scales[:, None, :] + (noise + jnp.swapaxes(noise, 1, 2)) * (spread / jnp.sqrt(order * 1.0))


def draw_block_inverse(key, part):
    key = jax.random.fold_in(key, 11)
    noise_key, diag_key = jax.random.split(key)
    noise = jax.random.normal(noise_key, (BLOCKS, B, B), jnp.float32)
    return symmetric_blocks(noise, diag_key, BLOCKS, B, 0.4).astype(jnp.bfloat16)


def draw_boundary_sigma(key, part):
    key = jax.random.fold_in(key, 23)
    noise_key, diag_key = jax.random.split(key)
    noise = jax.random.normal(noise_key, (PARTITIONS, B, B), jnp.float32)
    return symmetric_blocks(noise, diag_key, PARTITIONS, B, 0.4).astype(jnp.bfloat16)


def draw_tip_inverse(key, part):
    key = jax.random.fold_in(key, 37)
    noise_key, diag_key = jax.random.split(key)
    noise = jax.random.normal(noise_key, (1, A, A), jnp.float32)
    return symmetric_blocks(noise, diag_key, 1, A, 0.5)[0].astype(jnp.bfloat16)


def shard_levels(stream_key, dims, cuts, least, high):
    def one(dim, blocks):
        steps = jax.random.uniform(jax.random.fold_in(jax.random.fold_in(stream_key, 6), dim), (blocks,), jnp.float32, least / len(cuts), high / len(cuts))
        return jnp.repeat(jnp.exp(steps), dims[dim] // blocks).reshape((-1,) + (1,) * (len(dims) - dim - 1))

    loudness = one(*cuts[0])
    for cut in cuts[1:]:
        loudness = loudness * one(*cut)
    return loudness


def gaussian(key, extent, scale, most, cuts=(), held_as=jnp.bfloat16):
    factor_of = shard_levels(key, extent, cuts, -0.22, 0.18) if cuts else 1.0
    array = jax.random.normal(key, extent, jnp.float32) * scale * factor_of
    return jnp.minimum(jnp.maximum(array, -most), most).astype(held_as)


def setup_inputs(seed: int = 0) -> dict:
    key_of = jax.random.split(jax.random.key(seed), 8)
    return {
        "lower_factor": gaussian(key_of[0], (BLOCKS, B, B), B ** -0.5, 0.1875, ((0, 32), (1, 16))),
        "arrow_factor": gaussian(key_of[1], (BLOCKS, B, A), A ** -0.5, 0.25, ((0, 32), (1, 16))),
        "block_inverse": draw_block_inverse(jax.random.fold_in(key_of[7], 71), 0),
        "boundary_sigma": draw_boundary_sigma(jax.random.fold_in(key_of[7], 71), 0),
        "boundary_tip": gaussian(key_of[4], (PARTITIONS, B, A), 0.5, 3.0, ((0, 32), (1, 16))),
        "tip_inverse": draw_tip_inverse(jax.random.fold_in(key_of[7], 71), 0),
        "slope_weights": jnp.clip(jnp.exp(math.log(1.0) - 2.3025851 * jax.random.uniform(key_of[6], (BLOCKS, B), jnp.float32) ** shard_levels(key_of[6], (BLOCKS, B), ((0, 32), (1, 16)), -0.2, 0.2)), 0.1, 1.0),
    }


def mult(left, right):
    return jnp.dot(left.astype(jnp.float32), right.astype(jnp.float32), precision=lax.Precision.HIGHEST)


def one_partition(items, tip_full):
    lower, arrow, inverse, start_sigma, start_tip, weights = items
    sigma_state = start_sigma
    tip_state = start_tip
    diag_list = [None] * K
    lower_list = [None] * K
    tip_list = [None] * K
    slope = jnp.float32(0.0)
    for j in reversed(range(K)):
        low = lower[j].astype(jnp.float32)
        arr = arrow[j].astype(jnp.float32)
        lower_c = -(mult(sigma_state, low) + mult(tip_state, arr.T))
        tip_n = -(mult(low.T, tip_state) + mult(arr, tip_full))
        lower_b = lax.optimization_barrier(lower_c.astype(jnp.bfloat16))
        tip_b = lax.optimization_barrier(tip_n.astype(jnp.bfloat16))
        new_sigma = inverse[j].astype(jnp.float32) - mult(low.T, lower_b) - mult(arr, tip_b.astype(jnp.float32).T)
        slope = slope + jnp.sum(weights[j] * jnp.diagonal(new_sigma))
        diag_list[j] = new_sigma
        lower_list[j] = lower_c
        tip_list[j] = tip_n
        sigma_state = lax.optimization_barrier(new_sigma.astype(jnp.bfloat16))
        tip_state = tip_b
    return jnp.stack(diag_list), jnp.stack(lower_list), jnp.stack(tip_list), slope


def reference(lower_factor, arrow_factor, block_inverse, boundary_sigma, boundary_tip, tip_inverse, slope_weights):
    count = boundary_sigma.shape[0]
    next_sigma = jnp.concatenate([boundary_sigma[1:], jnp.zeros_like(boundary_sigma[:1])], axis=0)
    next_tip = jnp.concatenate([boundary_tip[1:], jnp.zeros_like(boundary_tip[:1])], axis=0)
    lower = lower_factor.reshape(count, K, B, B)
    arrow = arrow_factor.reshape(count, K, B, A)
    inverse = block_inverse.reshape(count, K, B, B)
    weights = slope_weights.reshape(count, K, B)
    tip_full = tip_inverse.astype(jnp.float32)
    diag_all, lower_all, tip_all, slopes = lax.map(
        lambda items: one_partition(items, tip_full),
        (lower, arrow, inverse, next_sigma, next_tip, weights))
    return (diag_all.reshape(count * K, B, B), lower_all.reshape(count * K, B, B),
            tip_all.reshape(count * K, B, A), jnp.sum(slopes))
```

```python
import jax
import jax.numpy as jnp
from jax import lax
from jax.experimental import pallas as pl
from jax.experimental.pallas import tpu as pltpu
from jax.sharding import Mesh, PartitionSpec as P

SIDE = 4
ROWS = 64
HALF = 512
BLOCK = 1024
BF = jnp.bfloat16
F32 = jnp.float32
EVERY = ("tm", "y", "x")

S, R, L1, M1, L0, M0, X1 = 0, 2, 3, 5, 6, 8, 9
KEPT = 9 * ROWS
SENT = 11 * ROWS
PANEL = SIDE * KEPT
SHARE = 2 * ROWS
VMEM_BYTES = 48 * 1024 * 1024


def line_groups(partitions, phase):
    groups = []
    for t in range(partitions):
        base = t * SIDE * SIDE
        for i in range(SIDE):
            if (t + phase) % 2 == 0:
                groups.append([base + SIDE * i + x for x in range(SIDE)])
            else:
                groups.append([base + SIDE * y + i for y in range(SIDE)])
    return groups


def height_groups(partitions):
    plane = SIDE * SIDE
    return [
        [t * plane + r for t in range(core, partitions, 2)]
        for core in range(2)
        for r in range(plane)
    ]


def exchange(value, groups):
    return lax.all_to_all(value, EVERY, 0, 0, tiled=True, axis_index_groups=groups)


def dot(left, right):
    return jnp.dot(left, right, preferred_element_type=F32)


def dot_t(left, right):
    return lax.dot_general(left, right, (((1,), (1,)), ((), ())), preferred_element_type=F32)


def split(value):
    high = value.astype(BF)
    return high, (value - high.astype(F32)).astype(BF)


def place():
    core = lax.rem(lax.axis_index("tm"), 2)
    y, x = lax.axis_index("y"), lax.axis_index("x")
    first = jnp.where(core == 0, x, y)
    return core, y * SIDE + x, first


def natural(core, second, first):
    return jnp.where(core == 0, SIDE * second + first, SIDE * first + second)


def columns_t(ref, piece, row):
    half = lax.div(row, 8)
    lane = lax.div(lax.rem(row, 8), 2)
    window = ref[
        :,
        pl.ds(pl.multiple_of((piece + half) * ROWS, ROWS), ROWS),
        pl.ds(pl.multiple_of(lane * 128, 128), 128),
    ]
    window = window.reshape(window.shape[0] * ROWS, 128)
    want = lax.broadcasted_iota(jnp.int32, (ROWS, 128), 0) + lax.rem(row, 2) * ROWS
    pick = jnp.where(lax.broadcasted_iota(jnp.int32, (ROWS, 128), 1) == want, 1.0, 0.0)
    return dot_t(pick.astype(BF), window).astype(BF)


def panel_kernel(got, out, panel, xs, share, sem_in, sem_x, sem_out, sem_share):
    core, _, first = place()
    loads = [
        pltpu.make_async_copy(got.at[j, pl.ds(0, KEPT)], panel.at[j], sem_in.at[j])
        for j in range(SIDE)
    ]
    loads_x = [
        pltpu.make_async_copy(got.at[j, pl.ds(KEPT, SHARE)], xs.at[j], sem_x.at[j])
        for j in range(SIDE)
    ]
    for copy in loads + loads_x:
        copy.start()
    for copy in loads:
        copy.wait()
    stores = [
        pltpu.make_async_copy(
            panel.at[j], out.at[d, pl.ds(j * KEPT, KEPT)], sem_out.at[d * SIDE + j]
        )
        for d in range(SIDE)
        for j in range(SIDE)
    ]
    for copy in stores:
        copy.start()
    cols = [columns_t(panel, L0, natural(core, d, first)) for d in range(SIDE)]
    cols = jnp.concatenate(cols, axis=0)
    for copy in loads_x:
        copy.wait()
    for h in range(2):
        part = dot(cols, xs[:, h * ROWS : (h + 1) * ROWS, :].reshape(SIDE * ROWS, HALF))
        for d in range(SIDE):
            share[d, h * ROWS : (h + 1) * ROWS, :] = part[d * ROWS : (d + 1) * ROWS].astype(BF)
    stores_share = [
        pltpu.make_async_copy(share.at[d], out.at[d, pl.ds(PANEL, SHARE)], sem_share.at[d])
        for d in range(SIDE)
    ]
    for copy in stores_share:
        copy.start()
    for copy in stores + stores_share:
        copy.wait()


def block_kernel(
    got, x_ref, q_ref, weight_ref, diag, lower, tip, slope, mat, shares, sem_in, sem_share
):
    core, row, _ = place()
    loads = []
    for d in range(SIDE):
        for j in range(SIDE):
            loads.append(
                pltpu.make_async_copy(
                    got.at[d, pl.ds(j * KEPT, KEPT)],
                    mat.at[natural(core, d, j)],
                    sem_in.at[d * SIDE + j],
                )
            )
    loads_share = [
        pltpu.make_async_copy(got.at[d, pl.ds(PANEL, SHARE)], shares.at[d], sem_share.at[d])
        for d in range(SIDE)
    ]
    for copy in loads + loads_share:
        copy.start()
    for copy in loads + loads_share:
        copy.wait()

    def piece(k, q):
        return mat[SIDE * q : SIDE * (q + 1), k * ROWS : (k + 1) * ROWS, :].reshape(
            SIDE * ROWS, HALF
        )

    def part(value, q):
        return value[:, q * 256 : (q + 1) * 256]

    def own(k):
        return mat[row, k * ROWS : (k + 1) * ROWS, :]

    def over_rows(left, k):
        total = dot(part(left, 0), piece(k, 0))
        for q in range(1, SIDE):
            total += dot(part(left, q), piece(k, q))
        return total

    def over_columns(left, k):
        return jnp.concatenate([dot_t(left, piece(k, q)) for q in range(SIDE)], axis=1)

    def times_factor(left_rows, left_tip, low, arr):
        both = jnp.concatenate([over_rows(left_rows, low + h) for h in range(2)], axis=1)
        return both + over_columns(left_tip, arr)

    z1 = columns_t(mat, L1, row)
    z0 = columns_t(mat, L0, row)
    z1_tip, z0_tip = own(M1), own(M0)
    u = over_columns(z0[:, :HALF], L1) + over_columns(z0[:, HALF:], L1 + 1)
    u_tip = over_rows(z0, M1) - z0_tip.astype(F32)
    uh, ul = split(u)
    uh_tip, ul_tip = split(u_tip)
    rows_in = jnp.concatenate([z1, uh, ul], axis=0)
    tip_in = jnp.concatenate([z1_tip, uh_tip, ul_tip], axis=0)
    top = jnp.concatenate([over_rows(rows_in, S + h) for h in range(2)], axis=1)
    top = top + over_columns(tip_in, R)
    bottom = over_rows(rows_in, R) + dot(tip_in, q_ref[...])
    p1, a = top[:64], top[64:128] + top[128:]
    p1_tip, a_tip = bottom[:64], bottom[64:128] + bottom[128:]
    tip[1] = -p1_tip
    tip[0] = a_tip
    own_rows = jnp.concatenate([own(S), own(S + 1)], axis=1)
    p1h, p1l = split(p1)
    ah, al = split(a)
    p1h_tip, p1l_tip = split(p1_tip)
    ah_tip, al_tip = split(a_tip)
    out = times_factor(
        jnp.concatenate([p1h, p1l, ah, al, own_rows], axis=0),
        jnp.concatenate([p1h_tip, p1l_tip, ah_tip, al_tip, own(R)], axis=0),
        L1,
        M1,
    )
    lower[1] = -out[256:]
    sigma1 = x_ref[1].astype(F32) + out[:64] + out[64:128]
    diag[1] = sigma1
    carried = shares[0].astype(F32)
    for d in range(1, SIDE):
        carried += shares[d].astype(F32)
    carried = jnp.concatenate([carried[:ROWS], carried[ROWS:]], axis=1)
    p0 = carried + out[128:192] + out[192:256]
    p0h, p0l = split(p0)
    out = times_factor(
        jnp.concatenate([p0h, p0l, sigma1.astype(BF)], axis=0),
        jnp.concatenate([-ah_tip, -al_tip, (-p1_tip).astype(BF)], axis=0),
        L0,
        M0,
    )
    lower[0] = -out[128:]
    sigma0 = x_ref[0].astype(F32) + out[:64] + out[64:128]
    diag[0] = sigma0
    at = lax.broadcasted_iota(jnp.int32, (ROWS, BLOCK), 0) + row * ROWS
    on_diagonal = lax.broadcasted_iota(jnp.int32, (ROWS, BLOCK), 1) == at
    traced = sigma0 * weight_ref[0] + sigma1 * weight_ref[1]
    traced = jnp.sum(jnp.where(on_diagonal, traced, 0.0))
    slope[...] = jnp.full(slope.shape, traced, F32)


def on_device(
    lower_factor,
    arrow_factor,
    block_inverse,
    boundary_sigma,
    boundary_tip,
    tip_inverse,
    slope_weights,
    partitions,
):
    start = jnp.concatenate([boundary_sigma[0], boundary_tip[0]], axis=1)
    start = lax.ppermute(start, "tm", [(p + 1, p) for p in range(partitions - 1)])
    wide = jnp.concatenate(
        [
            start,
            lower_factor[1],
            arrow_factor[1],
            lower_factor[0],
            arrow_factor[0],
            block_inverse[1],
        ],
        axis=1,
    )
    rows = jnp.concatenate([wide[:, HALF * k : HALF * (k + 1)] for k in range(11)], axis=0)
    rows = jnp.broadcast_to(rows[None], (SIDE, SENT, HALF))
    got = exchange(rows, line_groups(partitions, 0))
    anywhere = pl.BlockSpec(memory_space=pl.ANY)
    fast = pl.BlockSpec(memory_space=pltpu.VMEM)
    params = pltpu.CompilerParams(vmem_limit_bytes=VMEM_BYTES)
    sent = pl.pallas_call(
        panel_kernel,
        out_shape=jax.ShapeDtypeStruct((SIDE, PANEL + SHARE, HALF), BF),
        in_specs=[anywhere],
        out_specs=anywhere,
        scratch_shapes=[
            pltpu.VMEM((SIDE, KEPT, HALF), BF),
            pltpu.VMEM((SIDE, SHARE, HALF), BF),
            pltpu.VMEM((SIDE, SHARE, HALF), BF),
            pltpu.SemaphoreType.DMA((SIDE,)),
            pltpu.SemaphoreType.DMA((SIDE,)),
            pltpu.SemaphoreType.DMA((16,)),
            pltpu.SemaphoreType.DMA((SIDE,)),
        ],
        compiler_params=params,
    )(got)
    got = exchange(sent, line_groups(partitions, 1))
    weights = slope_weights[:, :, None]
    diag, lower, tip, slope = pl.pallas_call(
        block_kernel,
        out_shape=(
            jax.ShapeDtypeStruct((2, ROWS, BLOCK), F32),
            jax.ShapeDtypeStruct((2, ROWS, BLOCK), F32),
            jax.ShapeDtypeStruct((2, ROWS, HALF), F32),
            jax.ShapeDtypeStruct((16, 8, 128), F32),
        ),
        in_specs=[anywhere, fast, fast, fast],
        out_specs=(fast, fast, fast, fast),
        scratch_shapes=[
            pltpu.VMEM((16, KEPT, HALF), BF),
            pltpu.VMEM((SIDE, SHARE, HALF), BF),
            pltpu.SemaphoreType.DMA((16,)),
            pltpu.SemaphoreType.DMA((SIDE,)),
        ],
        compiler_params=params,
    )(got, block_inverse, tip_inverse, weights)
    total = jnp.sum(lax.all_to_all(slope, ("y", "x"), 0, 0, tiled=True), axis=0)
    total = jnp.broadcast_to(total[None], (partitions // 2, 8, 128))
    total = jnp.sum(exchange(total, height_groups(partitions)), axis=0)
    other = lax.ppermute(total, "tm", [(p, p ^ 1) for p in range(partitions)])
    return diag, lower, tip, (total + other)[0, 0]


def solution(mesh):
    partitions = mesh.shape["tm"]
    fine = Mesh(mesh.devices.reshape(partitions, SIDE, SIDE), EVERY)
    rows = P("tm", ("y", "x"), None)

    def program(*args):
        return on_device(*args, partitions=partitions)

    return jax.shard_map(
        program,
        mesh=fine,
        in_specs=(rows, rows, rows, rows, rows, P(), P("tm", ("y", "x"))),
        out_specs=(rows, rows, rows, P()),
        check_vma=False,
    )
```

```python
import jax
import jax.numpy as jnp
from jax import lax
from jax.experimental import pallas as pl
from jax.experimental.pallas import tpu as pltpu
from jax.sharding import Mesh, PartitionSpec as P

SIDE = 4
ROWS = 64
HALF = 512
BLOCK = 1024
BF = jnp.bfloat16
F32 = jnp.float32
EVERY = ("tm", "y", "x")

S, R, L1, M1, L0, M0, X1 = 0, 2, 3, 5, 6, 8, 9
EARLY = 6 * ROWS
PART = 3 * ROWS
SENT = 11 * ROWS
SHARE = 2 * ROWS
OWN = SHARE + 32
VMEM_BYTES = 60 * 1024 * 1024


def line_groups(partitions, phase):
    groups = []
    for t in range(partitions):
        base = t * SIDE * SIDE
        for i in range(SIDE):
            if (t + phase) % 2 == 0:
                groups.append([base + SIDE * i + x for x in range(SIDE)])
            else:
                groups.append([base + SIDE * y + i for y in range(SIDE)])
    return groups


def height_groups(partitions):
    plane = SIDE * SIDE
    return [
        [t * plane + r for t in range(core, partitions, 2)]
        for core in range(2)
        for r in range(plane)
    ]


def line_shift(partitions, steps):
    pairs = []
    for t in range(partitions):
        for y in range(SIDE):
            for x in range(SIDE):
                to = ((y + steps) % SIDE, x) if t % 2 == 0 else (y, (x + steps) % SIDE)
                base = t * SIDE * SIDE
                pairs.append((base + SIDE * y + x, base + SIDE * to[0] + to[1]))
    return pairs


def cost(megabytes):
    return pl.CostEstimate(flops=0, bytes_accessed=megabytes * 1_000_000, transcendentals=0)


def exchange(value, groups):
    return lax.all_to_all(value, EVERY, 0, 0, tiled=True, axis_index_groups=groups)


def dot(left, right):
    return jnp.dot(left, right, preferred_element_type=F32)


def dot_t(left, right):
    return lax.dot_general(left, right, (((1,), (1,)), ((), ())), preferred_element_type=F32)


def split(value):
    high = value.astype(BF)
    return high, (value - high.astype(F32)).astype(BF)


def place():
    core = lax.rem(lax.axis_index("tm"), 2)
    y, x = lax.axis_index("y"), lax.axis_index("x")
    first = jnp.where(core == 0, x, y)
    return core, y * SIDE + x, first


def natural(core, second, first):
    return jnp.where(core == 0, SIDE * second + first, SIDE * first + second)


def columns_t(ref, piece, row):
    half = lax.div(row, 8)
    lane = lax.div(lax.rem(row, 8), 2)
    window = ref[
        :,
        pl.ds(pl.multiple_of((piece + half) * ROWS, ROWS), ROWS),
        pl.ds(pl.multiple_of(lane * 128, 128), 128),
    ]
    window = window.reshape(window.shape[0] * ROWS, 128)
    want = lax.broadcasted_iota(jnp.int32, (ROWS, 128), 0) + lax.rem(row, 2) * ROWS
    pick = jnp.where(lax.broadcasted_iota(jnp.int32, (ROWS, 128), 1) == want, 1.0, 0.0)
    return dot_t(pick.astype(BF), window).astype(BF)


def panel_kernel(got, out, out_late, panel, mine, sem_in, sem_out, sem_late, sem_mine):
    core, _, first = place()
    loads = [pltpu.make_async_copy(got.at[j], panel.at[j], sem_in.at[j]) for j in range(SIDE)]
    for copy in loads:
        copy.start()
    stores = []
    for j in range(SIDE):
        loads[j].wait()
        here = [
            pltpu.make_async_copy(
                panel.at[j, pl.ds(0, EARLY)],
                out.at[d, pl.ds(j * EARLY, EARLY)],
                sem_out.at[d * SIDE + j],
            )
            for d in range(SIDE)
        ]
        here += [
            pltpu.make_async_copy(
                panel.at[j, pl.ds(EARLY, PART)],
                out_late.at[pl.ds(j * PART, PART)],
                sem_late.at[j],
            ),
        ]
        for copy in here:
            copy.start()
        stores += here
    cols = [columns_t(panel, L0, natural(core, d, first)) for d in range(SIDE)]
    for d in range(SIDE):
        mine[d, SHARE:, :] = jnp.concatenate([cols[d][:32], cols[d][32:]], axis=1)
    cols = jnp.concatenate(cols, axis=0)
    for h in range(2):
        at = (X1 + h) * ROWS
        part = dot(cols, panel[:, at : at + ROWS, :].reshape(SIDE * ROWS, HALF))
        for d in range(SIDE):
            mine[d, h * ROWS : (h + 1) * ROWS, :] = part[d * ROWS : (d + 1) * ROWS].astype(BF)
    stores_mine = [
        pltpu.make_async_copy(mine.at[d], out.at[d, pl.ds(SIDE * EARLY, OWN)], sem_mine.at[d])
        for d in range(SIDE)
    ]
    for copy in stores_mine:
        copy.start()
    for copy in stores + stores_mine:
        copy.wait()


class Gathered:
    def __init__(self, mat):
        self.mat = mat

    def piece(self, k, q):
        rows = self.mat[SIDE * q : SIDE * (q + 1), k * ROWS : (k + 1) * ROWS, :]
        return rows.reshape(SIDE * ROWS, HALF)

    def over_rows(self, left, k):
        total = dot(left[:, :256], self.piece(k, 0))
        for q in range(1, SIDE):
            total += dot(left[:, q * 256 : (q + 1) * 256], self.piece(k, q))
        return total

    def over_columns(self, left, k):
        return jnp.concatenate([dot_t(left, self.piece(k, q)) for q in range(SIDE)], axis=1)

    def times_factor(self, left_rows, left_tip, k):
        both = jnp.concatenate([self.over_rows(left_rows, k + h) for h in range(2)], axis=1)
        return both + self.over_columns(left_tip, k + 2)


def load_exchanged(got, mat, sem, piece):
    core, _, _ = place()
    return [
        pltpu.make_async_copy(
            got.at[d, pl.ds(j * EARLY + piece * ROWS, PART)],
            mat.at[natural(core, d, j)],
            sem.at[d * SIDE + j],
        )
        for d in range(SIDE)
        for j in range(SIDE)
    ]


def load_shifted(panels, mat, sem):
    core, _, _ = place()
    second = jnp.where(core == 0, lax.axis_index("y"), lax.axis_index("x"))
    return [
        pltpu.make_async_copy(
            panel.at[pl.ds(j * PART, PART)],
            mat.at[natural(core, lax.rem(second + SIDE - k, SIDE), j)],
            sem.at[k * SIDE + j],
        )
        for k, panel in enumerate(panels)
        for j in range(SIDE)
    ]


def trace_kernel(
    got,
    arrow_ref,
    x_ref,
    q_ref,
    weight_ref,
    tip,
    rows_out,
    tip_out,
    slope,
    factor,
    state,
    shares,
    sem_factor,
    sem_state,
    sem_share,
):
    core, row, _ = place()
    load_share = pltpu.make_async_copy(got.at[:, pl.ds(SIDE * EARLY, OWN)], shares, sem_share)
    load_factor = load_exchanged(got, factor, sem_factor, L1)
    load_state = load_exchanged(got, state, sem_state, S)
    for copy in [load_share] + load_factor + load_state:
        copy.start()
    for copy in [load_share] + load_factor:
        copy.wait()
    have = Gathered(factor)
    z1 = columns_t(factor, 0, row)
    z1_tip, z0_tip = arrow_ref[1], arrow_ref[0]
    parts = []
    for d in range(SIDE):
        held = shares[d, SHARE:, :]
        parts.append(jnp.concatenate([held[:, :256], held[:, 256:]], axis=0))
    even = jnp.concatenate(parts, axis=1)
    odd = [parts[d][:, j * 64 : (j + 1) * 64] for j in range(SIDE) for d in range(SIDE)]
    z0 = jnp.where(core == 0, even, jnp.concatenate(odd, axis=1))
    u = have.over_columns(z0[:, :HALF], 0) + have.over_columns(z0[:, HALF:], 1)
    u_tip = have.over_rows(z0, 2) - z0_tip.astype(F32)
    uh, ul = split(u)
    uh_tip, ul_tip = split(u_tip)
    rows_in = jnp.concatenate([z1, uh, ul], axis=0)
    tip_in = jnp.concatenate([z1_tip, uh_tip, ul_tip], axis=0)
    for copy in load_state:
        copy.wait()
    have = Gathered(state)
    top = have.times_factor(rows_in, tip_in, 0)
    bottom = have.over_rows(rows_in, 2) + dot(tip_in, q_ref[...])
    p1, a = top[:64], top[64:128] + top[128:]
    p1_tip, a_tip = bottom[:64], bottom[64:128] + bottom[128:]
    tip[1] = -p1_tip
    tip[0] = a_tip
    rows_out[...] = jnp.concatenate([p1, a], axis=0)
    tip_out[...] = jnp.concatenate([p1_tip, a_tip], axis=0)
    at = lax.broadcasted_iota(jnp.int32, (ROWS, BLOCK), 0) + row * ROWS
    on_diagonal = lax.broadcasted_iota(jnp.int32, (ROWS, BLOCK), 1) == at
    carried = sum_shares(shares)
    traced0 = jnp.where(on_diagonal, x_ref[0].astype(F32), 0.0)
    traced0 += z0.astype(F32) * carried + u * a
    traced1 = jnp.where(on_diagonal, x_ref[1].astype(F32), 0.0) + z1.astype(F32) * p1
    traced = traced0 * weight_ref[0] + traced1 * weight_ref[1]
    tip_traced = u_tip * a_tip * weight_ref[0] + z1_tip.astype(F32) * p1_tip * weight_ref[1]
    slope[...] = jnp.full(slope.shape, jnp.sum(traced) + jnp.sum(tip_traced), F32)


def sum_shares(shares):
    total = shares[0, :SHARE, :].astype(F32)
    for d in range(1, SIDE):
        total += shares[d, :SHARE, :].astype(F32)
    return jnp.concatenate([total[:ROWS], total[ROWS:]], axis=1)


def first_kernel(
    got,
    start_ref,
    x_ref,
    rows_ref,
    tip_ref,
    diag,
    lower,
    next_rows,
    next_tip,
    factor,
    shares,
    sem_factor,
    sem_share,
):
    load_share = pltpu.make_async_copy(
        got.at[:, pl.ds(SIDE * EARLY, SHARE)], shares, sem_share
    )
    loads = load_exchanged(got, factor, sem_factor, L1)
    for copy in loads + [load_share]:
        copy.start()
    p1h, p1l = split(rows_ref[:64])
    ah, al = split(rows_ref[64:])
    p1h_tip, p1l_tip = split(tip_ref[:64])
    ah_tip, al_tip = split(tip_ref[64:])
    own_rows, own_tip = start_ref[:, :BLOCK], start_ref[:, BLOCK:]
    for copy in loads + [load_share]:
        copy.wait()
    out = Gathered(factor).times_factor(
        jnp.concatenate([p1h, p1l, ah, al, own_rows], axis=0),
        jnp.concatenate([p1h_tip, p1l_tip, ah_tip, al_tip, own_tip], axis=0),
        0,
    )
    lower[...] = -out[256:]
    sigma1 = x_ref[1].astype(F32) + out[:64] + out[64:128]
    diag[...] = sigma1
    p0 = sum_shares(shares) + out[128:192] + out[192:256]
    p0h, p0l = split(p0)
    next_rows[...] = jnp.concatenate([p0h, p0l, sigma1.astype(BF)], axis=0)
    next_tip[...] = jnp.concatenate([-ah_tip, -al_tip, -p1h_tip], axis=0)


def last_kernel(
    late0,
    late1,
    late2,
    late3,
    x_ref,
    diag1,
    lower1,
    next_rows,
    next_tip,
    diag,
    lower,
    factor,
    sem,
):
    loads = load_shifted((late0, late1, late2, late3), factor, sem)
    for copy in loads:
        copy.start()
    diag[1] = diag1[...]
    lower[1] = lower1[...]
    for copy in loads:
        copy.wait()
    out = Gathered(factor).times_factor(next_rows[...], next_tip[...], 0)
    lower[0] = -out[128:]
    diag[0] = x_ref[0].astype(F32) + out[:64] + out[64:128]


def on_device(
    lower_factor,
    arrow_factor,
    block_inverse,
    boundary_sigma,
    boundary_tip,
    tip_inverse,
    slope_weights,
    partitions,
):
    start = jnp.concatenate([boundary_sigma[0], boundary_tip[0]], axis=1)
    start = lax.ppermute(start, "tm", [(p + 1, p) for p in range(partitions - 1)])
    wide = jnp.concatenate(
        [
            start,
            lower_factor[1],
            arrow_factor[1],
            lower_factor[0],
            arrow_factor[0],
            block_inverse[1],
        ],
        axis=1,
    )
    rows = jnp.concatenate([wide[:, HALF * k : HALF * (k + 1)] for k in range(11)], axis=0)
    rows = jnp.broadcast_to(rows[None], (SIDE, SENT, HALF))
    got = exchange(rows, line_groups(partitions, 0))
    anywhere = pl.BlockSpec(memory_space=pl.ANY)
    fast = pl.BlockSpec(memory_space=pltpu.VMEM)
    params = pltpu.CompilerParams(vmem_limit_bytes=VMEM_BYTES)
    sent, late = pl.pallas_call(
        panel_kernel,
        out_shape=(
            jax.ShapeDtypeStruct((SIDE, SIDE * EARLY + OWN, HALF), BF),
            jax.ShapeDtypeStruct((SIDE * PART, HALF), BF),
        ),
        in_specs=[anywhere],
        out_specs=(anywhere,) * 2,
        scratch_shapes=[
            pltpu.VMEM((SIDE, SENT, HALF), BF),
            pltpu.VMEM((SIDE, OWN, HALF), BF),
            pltpu.SemaphoreType.DMA((SIDE,)),
            pltpu.SemaphoreType.DMA((16,)),
            pltpu.SemaphoreType.DMA((SIDE,)),
            pltpu.SemaphoreType.DMA((SIDE,)),
        ],
        compiler_params=params,
        cost_estimate=cost(12),
    )(got)
    lates = [late] + [lax.ppermute(late, EVERY, line_shift(partitions, k)) for k in range(1, SIDE)]
    early = exchange(sent, line_groups(partitions, 1))
    weights = slope_weights[:, :, None]
    tip, rows_out, tip_out, slope = pl.pallas_call(
        trace_kernel,
        out_shape=(
            jax.ShapeDtypeStruct((2, ROWS, HALF), F32),
            jax.ShapeDtypeStruct((2 * ROWS, BLOCK), F32),
            jax.ShapeDtypeStruct((2 * ROWS, HALF), F32),
            jax.ShapeDtypeStruct((16, 8, 128), F32),
        ),
        in_specs=[anywhere] + [fast] * 4,
        out_specs=(fast,) * 4,
        scratch_shapes=[
            pltpu.VMEM((16, 3 * ROWS, HALF), BF),
            pltpu.VMEM((16, 3 * ROWS, HALF), BF),
            pltpu.VMEM((SIDE, OWN, HALF), BF),
            pltpu.SemaphoreType.DMA((16,)),
            pltpu.SemaphoreType.DMA((16,)),
            pltpu.SemaphoreType.DMA,
        ],
        compiler_params=params,
        cost_estimate=cost(20),
    )(early, arrow_factor, block_inverse, tip_inverse, weights)
    total = jnp.sum(lax.all_to_all(slope, ("y", "x"), 0, 0, tiled=True), axis=0)
    total = jnp.broadcast_to(total[None], (partitions // 2, 8, 128))
    total = jnp.sum(exchange(total, height_groups(partitions)), axis=0)
    other = lax.ppermute(total, "tm", [(p, p ^ 1) for p in range(partitions)])
    diag1, lower1, next_rows, next_tip = pl.pallas_call(
        first_kernel,
        out_shape=(
            jax.ShapeDtypeStruct((ROWS, BLOCK), F32),
            jax.ShapeDtypeStruct((ROWS, BLOCK), F32),
            jax.ShapeDtypeStruct((3 * ROWS, BLOCK), BF),
            jax.ShapeDtypeStruct((3 * ROWS, HALF), BF),
        ),
        in_specs=[anywhere] + [fast] * 4,
        out_specs=(fast,) * 4,
        scratch_shapes=[
            pltpu.VMEM((16, 3 * ROWS, HALF), BF),
            pltpu.VMEM((SIDE, SHARE, HALF), BF),
            pltpu.SemaphoreType.DMA((16,)),
            pltpu.SemaphoreType.DMA,
        ],
        compiler_params=params,
        cost_estimate=cost(15),
    )(early, start, block_inverse, rows_out, tip_out)
    diag, lower = pl.pallas_call(
        last_kernel,
        out_shape=(
            jax.ShapeDtypeStruct((2, ROWS, BLOCK), F32),
            jax.ShapeDtypeStruct((2, ROWS, BLOCK), F32),
        ),
        in_specs=[anywhere] * 4 + [fast] * 5,
        out_specs=(fast,) * 2,
        scratch_shapes=[
            pltpu.VMEM((16, PART, HALF), BF),
            pltpu.SemaphoreType.DMA((16,)),
        ],
        compiler_params=params,
        cost_estimate=cost(15),
    )(*lates, block_inverse, diag1, lower1, next_rows, next_tip)
    return diag, lower, tip, (total + other)[0, 0]


def solution(mesh):
    partitions = mesh.shape["tm"]
    fine = Mesh(mesh.devices.reshape(partitions, SIDE, SIDE), EVERY)
    rows = P("tm", ("y", "x"), None)

    def program(*args):
        return on_device(*args, partitions=partitions)

    return jax.shard_map(
        program,
        mesh=fine,
        in_specs=(rows, rows, rows, rows, rows, P(), P("tm", ("y", "x"))),
        out_specs=(rows, rows, rows, P()),
        check_vma=False,
    )
```

```python
import functools

import jax
import jax.numpy as jnp
from jax import lax
from jax.experimental import pallas as pl
from jax.experimental.pallas import tpu as pltpu
from jax.sharding import Mesh, PartitionSpec as P

SIDE = 4
ROWS = 64
HALF = 512
BLOCK = 1024
BF = jnp.bfloat16
F32 = jnp.float32
EVERY = ("tm", "y", "x")

L1, M1, L0, M0, X1 = 0, 2, 3, 5, 6
PART = 3 * ROWS
EARLY = 2 * PART
SENT = 8 * ROWS
SHARE = 2 * ROWS
OWN = SHARE + 32
VMEM_BYTES = 127 * 512 * 1024


def line_groups(partitions, phase):
    groups = []
    for t in range(partitions):
        base = t * SIDE * SIDE
        for i in range(SIDE):
            if (t + phase) % 2 == 0:
                groups.append([base + SIDE * i + x for x in range(SIDE)])
            else:
                groups.append([base + SIDE * y + i for y in range(SIDE)])
    return groups


def plane_groups(partitions):
    plane = 2 * SIDE * SIDE
    return [[z * plane + r for r in range(plane)] for z in range(partitions // 2)]


def height_groups(partitions):
    plane = SIDE * SIDE
    return [
        [t * plane + r for t in range(core, partitions, 2)]
        for core in range(2)
        for r in range(plane)
    ]


def state_shift(partitions, steps):
    pairs = []
    for t in range(partitions - 1):
        for y in range(SIDE):
            for x in range(SIDE):
                to = (y, (x + steps) % SIDE) if t % 2 == 0 else ((y + steps) % SIDE, x)
                source = (t + 1) * SIDE * SIDE + SIDE * y + x
                pairs.append((source, t * SIDE * SIDE + SIDE * to[0] + to[1]))
    return pairs


def line_shift(partitions, steps):
    pairs = []
    for t in range(partitions):
        for y in range(SIDE):
            for x in range(SIDE):
                to = ((y + steps) % SIDE, x) if t % 2 == 0 else (y, (x + steps) % SIDE)
                base = t * SIDE * SIDE
                pairs.append((base + SIDE * y + x, base + SIDE * to[0] + to[1]))
    return pairs


def cost(megabytes):
    return pl.CostEstimate(flops=0, bytes_accessed=megabytes * 1_000_000, transcendentals=0)


def exchange(value, groups):
    return lax.all_to_all(value, EVERY, 0, 0, tiled=True, axis_index_groups=groups)


def dot(left, right):
    return jnp.dot(left, right, preferred_element_type=F32)


def dot_t(left, right):
    return lax.dot_general(left, right, (((1,), (1,)), ((), ())), preferred_element_type=F32)


def split(value):
    high = value.astype(BF)
    return high, (value - high.astype(F32)).astype(BF)


def place():
    core = lax.rem(lax.axis_index("tm"), 2)
    y, x = lax.axis_index("y"), lax.axis_index("x")
    first = jnp.where(core == 0, x, y)
    return core, y * SIDE + x, first


def natural(core, second, first):
    return jnp.where(core == 0, SIDE * second + first, SIDE * first + second)


def columns_t(ref, piece, row):
    half = lax.div(row, 8)
    lane = lax.div(lax.rem(row, 8), 2)
    window = ref[
        :,
        pl.ds(pl.multiple_of((piece + half) * ROWS, ROWS), ROWS),
        pl.ds(pl.multiple_of(lane * 128, 128), 128),
    ]
    window = window.reshape(window.shape[0] * ROWS, 128)
    want = lax.broadcasted_iota(jnp.int32, (ROWS, 128), 0) + lax.rem(row, 2) * ROWS
    pick = jnp.where(lax.broadcasted_iota(jnp.int32, (ROWS, 128), 1) == want, 1.0, 0.0)
    return dot_t(pick.astype(BF), window).astype(BF)


def pack_kernel(low, arrow, inverse, sigma, tip, out, start, held, own, sem_in, sem_own, sem_out):
    loads = []
    for k, (ref, j, h) in enumerate(
        [(low, 1, 0), (low, 1, 1), (arrow, 1, 0), (low, 0, 0), (low, 0, 1), (arrow, 0, 0)]
        + [(inverse, 1, 0), (inverse, 1, 1)]
    ):
        loads.append(
            pltpu.make_async_copy(
                ref.at[j, :, pl.ds(h * HALF, HALF)],
                held.at[pl.ds(k * ROWS, ROWS)],
                sem_in.at[k],
            )
        )
    loads_own = [
        pltpu.make_async_copy(sigma.at[0], own.at[:, pl.ds(0, BLOCK)], sem_own.at[0]),
        pltpu.make_async_copy(tip.at[0], own.at[:, pl.ds(BLOCK, HALF)], sem_own.at[1]),
    ]
    for copy in loads + loads_own:
        copy.start()
    for copy in loads + loads_own:
        copy.wait()
    stores = [pltpu.make_async_copy(held, out.at[d], sem_out.at[d]) for d in range(SIDE)]
    stores.append(pltpu.make_async_copy(own, start, sem_out.at[SIDE]))
    for copy in stores:
        copy.start()
    for copy in stores:
        copy.wait()


def state_kernel(steps, *refs):
    count = len(steps)
    owns = refs[:count]
    out, held, sem_in, sem_out = refs[-4:]
    _, _, first = place()
    loads = [pltpu.make_async_copy(owns[i], held.at[i], sem_in.at[i]) for i in range(count)]
    for copy in loads:
        copy.start()
    stores = []
    for i, k in enumerate(steps):
        loads[i].wait()
        j = lax.rem(first + SIDE - k, SIDE)
        here = []
        for d in range(SIDE):
            for h in range(3):
                at = pl.multiple_of(j * EARLY + h * ROWS, ROWS)
                here.append(
                    pltpu.make_async_copy(
                        held.at[i, :, pl.ds(h * HALF, HALF)],
                        out.at[d, pl.ds(at, ROWS)],
                        sem_out.at[(i * SIDE + d) * 3 + h],
                    )
                )
        for copy in here:
            copy.start()
        stores += here
    for copy in stores:
        copy.wait()


def panel_kernel(got, begun, out, out_late, panel, mine, sem_in, sem_out, sem_late, sem_mine):
    del begun
    core, _, first = place()
    loads = [pltpu.make_async_copy(got.at[j], panel.at[j], sem_in.at[j]) for j in range(SIDE)]
    for copy in loads:
        copy.start()
    stores = []
    for j in range(SIDE):
        loads[j].wait()
        here = [
            pltpu.make_async_copy(
                panel.at[j, pl.ds(0, PART)],
                out.at[d, pl.ds(j * EARLY + PART, PART)],
                sem_out.at[d * SIDE + j],
            )
            for d in range(SIDE)
        ]
        here.append(
            pltpu.make_async_copy(
                panel.at[j, pl.ds(PART, PART)],
                out_late.at[pl.ds(j * PART, PART)],
                sem_late.at[j],
            )
        )
        for copy in here:
            copy.start()
        stores += here
    cols = [columns_t(panel, L0, natural(core, d, first)) for d in range(SIDE)]
    for d in range(SIDE):
        mine[d, SHARE:, :] = jnp.concatenate([cols[d][:32], cols[d][32:]], axis=1)
    cols = jnp.concatenate(cols, axis=0)
    for h in range(2):
        at = (X1 + h) * ROWS
        part = dot(cols, panel[:, at : at + ROWS, :].reshape(SIDE * ROWS, HALF))
        for d in range(SIDE):
            mine[d, h * ROWS : (h + 1) * ROWS, :] = part[d * ROWS : (d + 1) * ROWS].astype(BF)
    stores_mine = [
        pltpu.make_async_copy(mine.at[d], out.at[d, pl.ds(SIDE * EARLY, OWN)], sem_mine.at[d])
        for d in range(SIDE)
    ]
    for copy in stores_mine:
        copy.start()
    for copy in stores + stores_mine:
        copy.wait()


class Gathered:
    def __init__(self, mat):
        self.mat = mat

    def piece(self, k):
        return self.mat[:, k * ROWS : (k + 1) * ROWS, :].reshape(BLOCK, HALF)

    def over_rows(self, left, k):
        return dot(left, self.piece(k))

    def over_columns(self, left, k):
        return dot_t(left, self.piece(k))

    def times_factor(self, left_rows, left_tip, k):
        both = jnp.concatenate([self.over_rows(left_rows, k + h) for h in range(2)], axis=1)
        return both + self.over_columns(left_tip, k + 2)


def load_exchanged(got, mat, sem, piece):
    core, _, _ = place()
    return [
        pltpu.make_async_copy(
            got.at[d, pl.ds(j * EARLY + piece * ROWS, PART)],
            mat.at[natural(core, d, j)],
            sem.at[d * SIDE + j],
        )
        for d in range(SIDE)
        for j in range(SIDE)
    ]


def load_shifted(panels, mat, sem):
    core, _, _ = place()
    second = jnp.where(core == 0, lax.axis_index("y"), lax.axis_index("x"))
    return [
        pltpu.make_async_copy(
            panel.at[pl.ds(j * PART, PART)],
            mat.at[natural(core, lax.rem(second + SIDE - k, SIDE), j)],
            sem.at[k * SIDE + j],
        )
        for k, panel in enumerate(panels)
        for j in range(SIDE)
    ]


def sum_shares(shares):
    total = shares[0, :SHARE, :].astype(F32)
    for d in range(1, SIDE):
        total += shares[d, :SHARE, :].astype(F32)
    return jnp.concatenate([total[:ROWS], total[ROWS:]], axis=1)


def trace_kernel(
    got,
    arrow_ref,
    x_ref,
    q_ref,
    weight_ref,
    tip_ref,
    rows_ref,
    rows_tip_ref,
    slope_ref,
    factor,
    state,
    shares,
    arrow,
    x,
    q,
    weight,
    tip,
    rows,
    rows_tip,
    slope,
    sem_factor,
    sem_state,
    sem_in,
    sem_out,
):
    core, row, _ = place()
    load_share = pltpu.make_async_copy(got.at[:, pl.ds(SIDE * EARLY, OWN)], shares, sem_in.at[0])
    load_arrow = pltpu.make_async_copy(arrow_ref, arrow, sem_in.at[1])
    load_x = pltpu.make_async_copy(x_ref, x, sem_in.at[2])
    load_q = pltpu.make_async_copy(q_ref, q, sem_in.at[3])
    load_weight = pltpu.make_async_copy(weight_ref, weight, sem_in.at[4])
    load_factor = load_exchanged(got, factor, sem_factor, 3)
    load_state = load_exchanged(got, state, sem_state, 0)
    at_once = [load_share, load_arrow] + load_factor
    for copy in at_once + load_state + [load_q, load_x, load_weight]:
        copy.start()
    for copy in at_once:
        copy.wait()
    have = Gathered(factor)
    z1 = columns_t(factor, 0, row)
    z1_tip, z0_tip = arrow[1], arrow[0]
    parts = []
    for d in range(SIDE):
        held = shares[d, SHARE:, :]
        parts.append(jnp.concatenate([held[:, :256], held[:, 256:]], axis=0))
    even = jnp.concatenate(parts, axis=1)
    odd = [parts[d][:, j * 64 : (j + 1) * 64] for j in range(SIDE) for d in range(SIDE)]
    z0 = jnp.where(core == 0, even, jnp.concatenate(odd, axis=1))
    u = have.over_columns(z0[:, :HALF], 0) + have.over_columns(z0[:, HALF:], 1)
    u_tip = have.over_rows(z0, 2) - z0_tip.astype(F32)
    uh, ul = split(u)
    uh_tip, ul_tip = split(u_tip)
    rows_in = jnp.concatenate([z1, uh, ul], axis=0)
    tip_in = jnp.concatenate([z1_tip, uh_tip, ul_tip], axis=0)
    for copy in load_state + [load_q]:
        copy.wait()
    have = Gathered(state)
    top = have.times_factor(rows_in, tip_in, 0)
    bottom = have.over_rows(rows_in, 2) + dot(tip_in, q[...])
    p1, a = top[:64], top[64:128] + top[128:]
    p1_tip, a_tip = bottom[:64], bottom[64:128] + bottom[128:]
    tip[1] = -p1_tip
    tip[0] = a_tip
    rows[...] = jnp.concatenate([p1, a], axis=0)
    rows_tip[...] = jnp.concatenate([p1_tip, a_tip], axis=0)
    stores = [
        pltpu.make_async_copy(rows, rows_ref, sem_out.at[0]),
        pltpu.make_async_copy(rows_tip, rows_tip_ref, sem_out.at[1]),
        pltpu.make_async_copy(tip, tip_ref, sem_out.at[2]),
    ]
    for copy in stores:
        copy.start()
    at = lax.broadcasted_iota(jnp.int32, (ROWS, BLOCK), 0) + row * ROWS
    on_diagonal = lax.broadcasted_iota(jnp.int32, (ROWS, BLOCK), 1) == at
    load_x.wait()
    load_weight.wait()
    traced0 = jnp.where(on_diagonal, x[0].astype(F32), 0.0)
    traced0 += z0.astype(F32) * sum_shares(shares) + u * a
    traced1 = jnp.where(on_diagonal, x[1].astype(F32), 0.0) + z1.astype(F32) * p1
    traced = traced0 * weight[0] + traced1 * weight[1]
    tip_traced = u_tip * a_tip * weight[0] + z1_tip.astype(F32) * p1_tip * weight[1]
    slope[...] = jnp.full(slope.shape, jnp.sum(traced) + jnp.sum(tip_traced), F32)
    stores.append(pltpu.make_async_copy(slope, slope_ref, sem_out.at[3]))
    stores[-1].start()
    for copy in stores:
        copy.wait()


def block_kernel(
    got,
    late0,
    late1,
    late2,
    late3,
    start_ref,
    x_ref,
    rows_ref,
    rows_tip_ref,
    diag_ref,
    lower_ref,
    factor1,
    factor0,
    shares,
    start,
    x,
    rows,
    rows_tip,
    diag,
    lower,
    sem_factor1,
    sem_factor0,
    sem_in,
    sem_out,
):
    loads = [
        pltpu.make_async_copy(rows_ref, rows, sem_in.at[0]),
        pltpu.make_async_copy(rows_tip_ref, rows_tip, sem_in.at[1]),
        pltpu.make_async_copy(start_ref, start, sem_in.at[2]),
        pltpu.make_async_copy(x_ref, x, sem_in.at[3]),
        pltpu.make_async_copy(got.at[:, pl.ds(SIDE * EARLY, SHARE)], shares, sem_in.at[4]),
    ]
    loads1 = load_exchanged(got, factor1, sem_factor1, 3)
    loads0 = load_shifted((late0, late1, late2, late3), factor0, sem_factor0)
    for copy in loads[:3] + loads1 + loads[3:] + loads0:
        copy.start()
    for copy in loads[:3]:
        copy.wait()
    p1h, p1l = split(rows[:64])
    ah, al = split(rows[64:])
    p1h_tip, p1l_tip = split(rows_tip[:64])
    ah_tip, al_tip = split(rows_tip[64:])
    for copy in loads1 + loads[3:]:
        copy.wait()
    out = Gathered(factor1).times_factor(
        jnp.concatenate([p1h, p1l, ah, al, start[:, :BLOCK]], axis=0),
        jnp.concatenate([p1h_tip, p1l_tip, ah_tip, al_tip, start[:, BLOCK:]], axis=0),
        0,
    )
    lower[1] = -out[256:]
    sigma1 = x[1].astype(F32) + out[:64] + out[64:128]
    diag[1] = sigma1
    stores = [
        pltpu.make_async_copy(diag.at[1], diag_ref.at[1], sem_out.at[0]),
        pltpu.make_async_copy(lower.at[1], lower_ref.at[1], sem_out.at[1]),
    ]
    for copy in stores:
        copy.start()
    p0h, p0l = split(sum_shares(shares) + out[128:192] + out[192:256])
    for copy in loads0:
        copy.wait()
    out = Gathered(factor0).times_factor(
        jnp.concatenate([p0h, p0l, sigma1.astype(BF)], axis=0),
        jnp.concatenate([-ah_tip, -al_tip, -p1h_tip], axis=0),
        0,
    )
    lower[0] = -out[128:]
    diag[0] = x[0].astype(F32) + out[:64] + out[64:128]
    more = [
        pltpu.make_async_copy(diag.at[0], diag_ref.at[0], sem_out.at[2]),
        pltpu.make_async_copy(lower.at[0], lower_ref.at[0], sem_out.at[3]),
    ]
    for copy in more:
        copy.start()
    for copy in stores + more:
        copy.wait()


def on_device(
    lower_factor,
    arrow_factor,
    block_inverse,
    boundary_sigma,
    boundary_tip,
    tip_inverse,
    slope_weights,
    partitions,
):
    slow = pl.BlockSpec(memory_space=pltpu.HBM)
    params = pltpu.CompilerParams(vmem_limit_bytes=VMEM_BYTES)
    rows, start = pl.pallas_call(
        pack_kernel,
        out_shape=(
            jax.ShapeDtypeStruct((SIDE, SENT, HALF), BF),
            jax.ShapeDtypeStruct((ROWS, BLOCK + HALF), BF),
        ),
        in_specs=[slow] * 5,
        out_specs=(slow,) * 2,
        scratch_shapes=[
            pltpu.VMEM((SENT, HALF), BF),
            pltpu.VMEM((ROWS, BLOCK + HALF), BF),
            pltpu.SemaphoreType.DMA((8,)),
            pltpu.SemaphoreType.DMA((2,)),
            pltpu.SemaphoreType.DMA((SIDE + 1,)),
        ],
        compiler_params=params,
        cost_estimate=cost(4),
    )(lower_factor, arrow_factor, block_inverse, boundary_sigma, boundary_tip)
    got = exchange(rows, line_groups(partitions, 0))
    starts = [lax.ppermute(start, EVERY, state_shift(partitions, k)) for k in range(SIDE)]
    begun = []
    for steps in ((0, 1), (2, 3)):
        count = len(steps)
        begun = [
            pl.pallas_call(
                functools.partial(state_kernel, steps),
                out_shape=jax.ShapeDtypeStruct((SIDE, SIDE * EARLY + OWN, HALF), BF),
                in_specs=[slow] * (count + len(begun)),
                out_specs=slow,
                input_output_aliases={count: 0} if begun else {},
                scratch_shapes=[
                    pltpu.VMEM((count, ROWS, BLOCK + HALF), BF),
                    pltpu.SemaphoreType.DMA((count,)),
                    pltpu.SemaphoreType.DMA((count * SIDE * 3,)),
                ],
                compiler_params=params,
                cost_estimate=cost(8),
            )(*[starts[k] for k in steps], *begun)
        ]
    sent, late = pl.pallas_call(
        panel_kernel,
        out_shape=(
            jax.ShapeDtypeStruct((SIDE, SIDE * EARLY + OWN, HALF), BF),
            jax.ShapeDtypeStruct((SIDE * PART, HALF), BF),
        ),
        in_specs=[slow] * 2,
        out_specs=(slow,) * 2,
        input_output_aliases={1: 0},
        scratch_shapes=[
            pltpu.VMEM((SIDE, SENT, HALF), BF),
            pltpu.VMEM((SIDE, OWN, HALF), BF),
            pltpu.SemaphoreType.DMA((SIDE,)),
            pltpu.SemaphoreType.DMA((16,)),
            pltpu.SemaphoreType.DMA((SIDE,)),
            pltpu.SemaphoreType.DMA((SIDE,)),
        ],
        compiler_params=params,
        cost_estimate=cost(12),
    )(got, *begun)
    lates = [late] + [lax.ppermute(late, EVERY, line_shift(partitions, k)) for k in range(1, SIDE)]
    early = exchange(sent, line_groups(partitions, 1))
    weights = slope_weights[:, :, None]
    outputs = (
        jax.ShapeDtypeStruct((2, ROWS, HALF), F32),
        jax.ShapeDtypeStruct((2 * ROWS, BLOCK), F32),
        jax.ShapeDtypeStruct((2 * ROWS, HALF), F32),
        jax.ShapeDtypeStruct((32, 8, 128), F32),
    )
    tip, rows, rows_tip, slope = pl.pallas_call(
        trace_kernel,
        out_shape=outputs,
        in_specs=[slow] * 5,
        out_specs=(slow,) * 4,
        scratch_shapes=[
            pltpu.VMEM((16, PART, HALF), BF),
            pltpu.VMEM((16, PART, HALF), BF),
            pltpu.VMEM((SIDE, OWN, HALF), BF),
            pltpu.VMEM((2, ROWS, HALF), BF),
            pltpu.VMEM((2, ROWS, BLOCK), BF),
            pltpu.VMEM((HALF, HALF), BF),
            pltpu.VMEM((2, ROWS, 1), F32),
        ]
        + [pltpu.VMEM(leaf.shape, F32) for leaf in outputs]
        + [
            pltpu.SemaphoreType.DMA((16,)),
            pltpu.SemaphoreType.DMA((16,)),
            pltpu.SemaphoreType.DMA((5,)),
            pltpu.SemaphoreType.DMA((4,)),
        ],
        compiler_params=params,
        cost_estimate=cost(20),
    )(early, arrow_factor, block_inverse, tip_inverse, weights)
    total = jnp.sum(exchange(slope, plane_groups(partitions)), axis=0)
    total = jnp.broadcast_to(total[None], (partitions // 2, 8, 128))
    total = jnp.sum(exchange(total, height_groups(partitions)), axis=0)
    diag, lower = pl.pallas_call(
        block_kernel,
        out_shape=(
            jax.ShapeDtypeStruct((2, ROWS, BLOCK), F32),
            jax.ShapeDtypeStruct((2, ROWS, BLOCK), F32),
        ),
        in_specs=[slow] * 9,
        out_specs=(slow,) * 2,
        scratch_shapes=[
            pltpu.VMEM((16, PART, HALF), BF),
            pltpu.VMEM((16, PART, HALF), BF),
            pltpu.VMEM((SIDE, SHARE, HALF), BF),
            pltpu.VMEM((ROWS, BLOCK + HALF), BF),
            pltpu.VMEM((2, ROWS, BLOCK), BF),
            pltpu.VMEM((2 * ROWS, BLOCK), F32),
            pltpu.VMEM((2 * ROWS, HALF), F32),
            pltpu.VMEM((2, ROWS, BLOCK), F32),
            pltpu.VMEM((2, ROWS, BLOCK), F32),
            pltpu.SemaphoreType.DMA((16,)),
            pltpu.SemaphoreType.DMA((16,)),
            pltpu.SemaphoreType.DMA((5,)),
            pltpu.SemaphoreType.DMA((4,)),
        ],
        compiler_params=params,
        cost_estimate=cost(20),
    )(early, *lates, starts[0], block_inverse, rows, rows_tip)
    return diag, lower, tip, total[0, 0]


def solution(mesh):
    partitions = mesh.shape["tm"]
    fine = Mesh(mesh.devices.reshape(partitions, SIDE, SIDE), EVERY)
    rows = P("tm", ("y", "x"), None)

    def program(*args):
        return on_device(*args, partitions=partitions)

    return jax.shard_map(
        program,
        mesh=fine,
        in_specs=(rows, rows, rows, rows, rows, P(), P("tm", ("y", "x"))),
        out_specs=(rows, rows, rows, P()),
        check_vma=False,
    )
```

```python
import jax
import jax.numpy as jnp
from jax import lax
from jax.experimental import pallas as pl
from jax.experimental.pallas import tpu as pltpu
from jax.sharding import Mesh, PartitionSpec as P

SIDE = 4
ROWS = 64
HALF = 512
BLOCK = 1024
BF = jnp.bfloat16
F32 = jnp.float32
EVERY = ("tm", "y", "x")

L1, M1, L0, M0, X1 = 0, 2, 3, 5, 6
PART = 3 * ROWS
SENT = 8 * ROWS
SHARE = 2 * ROWS
PANEL = SIDE * PART
MISC = 2 * ROWS + ROWS + 16
WIDE = BLOCK + HALF
LATER = PANEL + SHARE
VMEM_BYTES = 127 * 512 * 1024


def line_groups(partitions, phase):
    groups = []
    for t in range(partitions):
        base = t * SIDE * SIDE
        for i in range(SIDE):
            if (t + phase) % 2 == 0:
                groups.append([base + SIDE * i + x for x in range(SIDE)])
            else:
                groups.append([base + SIDE * y + i for y in range(SIDE)])
    return groups


def plane_groups(partitions):
    plane = 2 * SIDE * SIDE
    return [[z * plane + r for r in range(plane)] for z in range(partitions // 2)]


def height_groups(partitions):
    plane = SIDE * SIDE
    return [
        [t * plane + r for t in range(core, partitions, 2)]
        for core in range(2)
        for r in range(plane)
    ]


def state_shift(partitions, steps):
    pairs = []
    for t in range(partitions - 1):
        for y in range(SIDE):
            for x in range(SIDE):
                to = (y, (x + steps) % SIDE) if t % 2 == 0 else ((y + steps) % SIDE, x)
                source = (t + 1) * SIDE * SIDE + SIDE * y + x
                pairs.append((source, t * SIDE * SIDE + SIDE * to[0] + to[1]))
    return pairs


def line_shift(partitions, steps):
    pairs = []
    for t in range(partitions):
        for y in range(SIDE):
            for x in range(SIDE):
                to = ((y + steps) % SIDE, x) if t % 2 == 0 else (y, (x + steps) % SIDE)
                base = t * SIDE * SIDE
                pairs.append((base + SIDE * y + x, base + SIDE * to[0] + to[1]))
    return pairs


def cost(megabytes):
    return pl.CostEstimate(flops=0, bytes_accessed=megabytes * 1_000_000, transcendentals=0)


def exchange(value, groups):
    return lax.all_to_all(value, EVERY, 0, 0, tiled=True, axis_index_groups=groups)


def dot(left, right):
    return jnp.dot(left, right, preferred_element_type=F32)


def dot_t(left, right):
    return lax.dot_general(left, right, (((1,), (1,)), ((), ())), preferred_element_type=F32)


def split(value):
    high = value.astype(BF)
    return high, (value - high.astype(F32)).astype(BF)


def place():
    core = lax.rem(lax.axis_index("tm"), 2)
    y, x = lax.axis_index("y"), lax.axis_index("x")
    first = jnp.where(core == 0, x, y)
    return core, y * SIDE + x, first


def natural(core, second, first):
    return jnp.where(core == 0, SIDE * second + first, SIDE * first + second)


def columns_t(ref, piece, row, blocks=None):
    half = lax.div(row, 8)
    lane = lax.div(lax.rem(row, 8), 2)
    rows = pl.ds(pl.multiple_of((piece + half) * ROWS, ROWS), ROWS)
    lanes = pl.ds(pl.multiple_of(lane * 128, 128), 128)
    if blocks is None:
        window = ref[:, rows, lanes]
        window = window.reshape(window.shape[0] * ROWS, 128)
    else:
        window = jnp.concatenate([ref[b, rows, lanes] for b in blocks], axis=0)
    want = lax.broadcasted_iota(jnp.int32, (ROWS, 128), 0) + lax.rem(row, 2) * ROWS
    pick = jnp.where(lax.broadcasted_iota(jnp.int32, (ROWS, 128), 1) == want, 1.0, 0.0)
    return dot_t(pick.astype(BF), window).astype(BF)


def pack_kernel(low, arrow, inverse, sigma, tip, out, start, held, own, sem_in, sem_own, sem_out):
    loads = []
    for k, (ref, j, h) in enumerate(
        [(low, 1, 0), (low, 1, 1), (arrow, 1, 0), (low, 0, 0), (low, 0, 1), (arrow, 0, 0)]
        + [(inverse, 1, 0), (inverse, 1, 1)]
    ):
        loads.append(
            pltpu.make_async_copy(
                ref.at[j, :, pl.ds(h * HALF, HALF)],
                held.at[pl.ds(k * ROWS, ROWS)],
                sem_in.at[k],
            )
        )
    loads_own = [
        pltpu.make_async_copy(sigma.at[0], own.at[:, pl.ds(0, BLOCK)], sem_own.at[0]),
        pltpu.make_async_copy(tip.at[0], own.at[:, pl.ds(BLOCK, HALF)], sem_own.at[1]),
    ]
    for copy in loads + loads_own:
        copy.start()
    for copy in loads + loads_own:
        copy.wait()
    stores = [pltpu.make_async_copy(held, out.at[d], sem_out.at[d]) for d in range(SIDE)]
    stores.append(pltpu.make_async_copy(own, start, sem_out.at[SIDE]))
    for copy in stores:
        copy.start()
    for copy in stores:
        copy.wait()


def panel_kernel(
    got,
    arrow,
    weight,
    own0,
    own1,
    own2,
    own3,
    out,
    late0,
    late1,
    late2,
    late3,
    panel,
    state,
    misc,
    share,
    sem_in,
    sem_out,
    sem_late,
    sem_state,
):
    core, _, first = place()
    second = jnp.where(core == 0, lax.axis_index("y"), lax.axis_index("x"))
    loads = [pltpu.make_async_copy(got.at[j], panel.at[j], sem_in.at[j]) for j in range(SIDE)]
    load_arrow = pltpu.make_async_copy(
        arrow.at[0], misc.at[pl.ds(2 * ROWS, ROWS)], sem_in.at[SIDE]
    )
    loads_state = [
        pltpu.make_async_copy(
            own.at[:, pl.ds(h * HALF, HALF)],
            state.at[pl.ds(k * PART + h * ROWS, ROWS)],
            sem_state.at[k * 3 + h],
        )
        for k, own in enumerate((own0, own1, own2, own3))
        for h in range(3)
    ]
    for copy in loads + [load_arrow] + loads_state:
        copy.start()
    stores = []
    for j in range(SIDE):
        loads[j].wait()
        here = [
            pltpu.make_async_copy(
                panel.at[j, pl.ds(0, PART)],
                out.at[d, pl.ds(j * PART, PART)],
                sem_out.at[d * (SIDE + 1) + j],
            )
            for d in range(SIDE)
        ]
        for copy in here:
            copy.start()
        stores += here
    cols = [columns_t(panel, L0, natural(core, d, first)) for d in range(SIDE)]
    cols = jnp.concatenate(cols, axis=0)
    misc[: 2 * ROWS, :] = jnp.concatenate([cols[: 2 * ROWS], cols[2 * ROWS :]], axis=1)
    rest = weight[...]
    parts = []
    for _ in range(3):
        parts.append(rest.astype(BF).astype(F32))
        rest = rest - parts[-1]
    parts = jnp.concatenate(parts + [jnp.zeros((10, ROWS), F32)], axis=0)
    parts = jnp.concatenate([parts, jnp.zeros((16, HALF - ROWS), F32)], axis=1)
    misc[3 * ROWS :, :] = parts.astype(BF)
    load_arrow.wait()
    here = [
        pltpu.make_async_copy(misc, out.at[d, pl.ds(PANEL, MISC)], sem_out.at[d * (SIDE + 1) + SIDE])
        for d in range(SIDE)
    ]
    lates = (late0, late1, late2, late3)
    for k, late in enumerate(lates):
        here += [
            pltpu.make_async_copy(
                panel.at[j, pl.ds(PART, PART)],
                late.at[pl.ds(j * PART, PART)],
                sem_late.at[k * (SIDE + 1) + j],
            )
            for j in range(SIDE)
        ]
    for copy in loads_state:
        copy.wait()
    here += [
        pltpu.make_async_copy(state, late.at[pl.ds(LATER, PANEL)], sem_state.at[12 + k])
        for k, late in enumerate(lates)
    ]
    for copy in here:
        copy.start()
    stores += here
    for h in range(2):
        at = (X1 + h) * ROWS
        part = dot(cols, panel[:, at : at + ROWS, :].reshape(SIDE * ROWS, HALF))
        for d in range(SIDE):
            share[d, h * ROWS : (h + 1) * ROWS, :] = part[d * ROWS : (d + 1) * ROWS].astype(BF)
    here = [
        pltpu.make_async_copy(
            share.at[lax.rem(second + k, SIDE)],
            late.at[pl.ds(PANEL, SHARE)],
            sem_late.at[k * (SIDE + 1) + SIDE],
        )
        for k, late in enumerate(lates)
    ]
    for copy in here:
        copy.start()
    for copy in stores + here:
        copy.wait()


class Gathered:
    def __init__(self, mat):
        self.mat = mat

    def piece(self, k):
        return self.mat[:, k * ROWS : (k + 1) * ROWS, :].reshape(BLOCK, HALF)

    def over_rows(self, left, k):
        return dot(left, self.piece(k))

    def over_columns(self, left, k):
        return dot_t(left, self.piece(k))

    def times_factor(self, left_rows, left_tip):
        both = jnp.concatenate([self.over_rows(left_rows, h) for h in range(2)], axis=1)
        return both + self.over_columns(left_tip, 2)

    def past(self, left):
        u = self.over_columns(left[:, :HALF], 0) + self.over_columns(left[:, HALF:], 1)
        return u, self.over_rows(left, 2)


def load_exchanged(got, mat, sem):
    core, _, _ = place()
    return [
        pltpu.make_async_copy(
            got.at[d, pl.ds(j * PART, PART)],
            mat.at[natural(core, d, j)],
            sem.at[d * SIDE + j],
        )
        for d in range(SIDE)
        for j in range(SIDE)
    ]


def in_order(core, parts):
    even = jnp.concatenate(parts, axis=1)
    odd = [parts[d][:, j * 64 : (j + 1) * 64] for j in range(SIDE) for d in range(SIDE)]
    return jnp.where(core == 0, even, jnp.concatenate(odd, axis=1))


def sum_all(value):
    return jnp.sum(jnp.sum(value, axis=1, keepdims=True))


def trace_kernel(
    got,
    begun,
    panel_ref,
    arrow_ref,
    x_ref,
    q_ref,
    weight_ref,
    slope,
    factor,
    misc,
    state,
    inverse,
    arrow,
    x,
    q,
    sem_factor,
    sem_in,
):
    core, row, first = place()
    second = jnp.where(core == 0, lax.axis_index("y"), lax.axis_index("x"))
    load_misc = pltpu.make_async_copy(got.at[:, pl.ds(PANEL, MISC)], misc, sem_in.at[0])
    load_factor = load_exchanged(got, factor, sem_factor)
    later = [
        pltpu.make_async_copy(begun.at[pl.ds(LATER, PANEL)], state, sem_in.at[1]),
        pltpu.make_async_copy(
            panel_ref.at[:, pl.ds(X1 * ROWS, 2 * ROWS)], inverse, sem_in.at[2]
        ),
        pltpu.make_async_copy(arrow_ref, arrow, sem_in.at[3]),
        pltpu.make_async_copy(q_ref, q, sem_in.at[4]),
        pltpu.make_async_copy(x_ref, x, sem_in.at[5]),
    ]
    for copy in [load_misc] + load_factor + later:
        copy.start()
    load_misc.wait()
    columns = [natural(core, d, first) for d in range(SIDE)]
    mine = [natural(core, second, lax.rem(first + SIDE - k, SIDE)) for k in range(SIDE)]
    parts = []
    for d in range(SIDE):
        held = misc[d, : 2 * ROWS, :]
        parts.append(jnp.concatenate([held[:, :256], held[:, 256:]], axis=0))
    z0 = in_order(core, parts)
    z0_tip = misc[:, 2 * ROWS : 3 * ROWS, :].reshape(256, HALF)
    eye = lax.broadcasted_iota(jnp.int32, (ROWS, ROWS), 0)
    eye = jnp.where(eye == lax.broadcasted_iota(jnp.int32, (ROWS, ROWS), 1), 1.0, 0.0)
    weights = []
    for block in range(2):
        column = []
        for d in range(SIDE):
            held = misc[d, 3 * ROWS :, :].astype(F32)
            held = held[block : block + 1] + held[block + 2 : block + 3] + held[block + 4 : block + 5]
            column.append(jnp.sum(eye * held[:, :ROWS], axis=1, keepdims=True))
        weights.append(jnp.concatenate(column, axis=0))
    for copy in load_factor:
        copy.wait()
    have = Gathered(factor)
    u, u_tip = have.past(z0)
    u_tip = u_tip - z0_tip.astype(F32)
    u_mine = jnp.zeros((256, 256), F32)
    z1_mine = []
    for h in range(2):
        low = jnp.concatenate([factor[b, h * ROWS : (h + 1) * ROWS, :] for b in mine], axis=0)
        u_mine += dot_t(z0[:, h * HALF : (h + 1) * HALF], low)
    z1 = jnp.concatenate([columns_t(factor, 0, c) for c in columns], axis=0)
    z1_mine = jnp.concatenate([columns_t(factor, 0, c, mine) for c in columns], axis=0)
    z1_tip = jnp.concatenate([factor[c, 2 * ROWS :, :] for c in columns], axis=0)
    for copy in later:
        copy.wait()
    rows_in = jnp.concatenate([u.astype(BF), z1], axis=0)
    tip_in = jnp.concatenate([u_tip.astype(BF), z1_tip], axis=0)
    held = state[...].reshape(SIDE, PART, HALF)
    held = [held[:, h * ROWS : (h + 1) * ROWS, :].reshape(256, HALF) for h in range(3)]
    through = dot_t(rows_in[:, :HALF], held[0]) + dot_t(rows_in[:, HALF:], held[1])
    through += 2.0 * dot_t(tip_in, held[2])
    carried = jnp.zeros((256, 256), F32)
    for h in range(2):
        part = inverse[:, h * ROWS : (h + 1) * ROWS, :].reshape(256, HALF)
        carried += dot_t(z0[:, h * HALF : (h + 1) * HALF], part)
    own_parts = parts[0]
    for d in range(1, SIDE):
        own_parts = jnp.where(second == d, parts[d], own_parts)
    traced = (u_mine * through[:256] + own_parts.astype(F32) * carried) * weights[0]
    traced += z1_mine.astype(F32) * through[256:] * weights[1]
    own_tip = dot(z0_own(misc, second, core), Gathered(factor).piece(2))
    own_tip = own_tip - arrow[0].astype(F32)
    both = jnp.concatenate([own_tip.astype(BF), arrow[1]], axis=0)
    tip_traced = both.astype(F32) * dot(both, q[...])
    at = lax.broadcasted_iota(jnp.int32, (ROWS, BLOCK), 0) + row * ROWS
    on_diagonal = lax.broadcasted_iota(jnp.int32, (ROWS, BLOCK), 1) == at
    total = sum_all(traced)
    for block in range(2):
        total += sum_all(tip_traced[block * ROWS : (block + 1) * ROWS] * weight_ref[block])
        own = jnp.where(on_diagonal, x[block].astype(F32), 0.0)
        total += sum_all(own * weight_ref[block])
    slope[...] = jnp.full(slope.shape, total, F32)


def z0_own(misc, second, core):
    rows = pl.ds(pl.multiple_of(lax.rem(second, 2) * ROWS, ROWS), ROWS)
    lanes = pl.ds(pl.multiple_of(lax.div(second, 2) * 256, 256), 256)
    return in_order(core, [misc[d, rows, lanes] for d in range(SIDE)])


def block_kernel(
    got,
    late0,
    late1,
    late2,
    late3,
    arrow_ref,
    x_ref,
    q_ref,
    total_ref,
    diag_ref,
    lower_ref,
    tip_ref,
    factor1,
    factor0,
    state,
    shares,
    misc,
    arrow,
    x,
    q,
    diag,
    lower,
    tip,
    sem_factor1,
    sem_factor0,
    sem_state,
    sem_share,
    sem_in,
    sem_out,
):
    del total_ref
    core, row, first = place()
    second = jnp.where(core == 0, lax.axis_index("y"), lax.axis_index("x"))
    loads1 = [
        pltpu.make_async_copy(got.at[:, pl.ds(PANEL, MISC)], misc, sem_in.at[0]),
        pltpu.make_async_copy(arrow_ref, arrow, sem_in.at[1]),
    ] + load_exchanged(got, factor1, sem_factor1)
    loads_state = [pltpu.make_async_copy(q_ref, q, sem_in.at[2])]
    loads0 = [pltpu.make_async_copy(x_ref, x, sem_in.at[3])]
    for k, late in enumerate((late0, late1, late2, late3)):
        source = lax.rem(second + SIDE - k, SIDE)
        for j in range(SIDE):
            behind = lax.rem(first + SIDE - j, SIDE)
            loads_state.append(
                pltpu.make_async_copy(
                    late.at[pl.ds(LATER + j * PART, PART)],
                    state.at[natural(core, source, behind)],
                    sem_state.at[k * SIDE + j],
                )
            )
            loads0.append(
                pltpu.make_async_copy(
                    late.at[pl.ds(j * PART, PART)],
                    factor0.at[natural(core, source, j)],
                    sem_factor0.at[k * SIDE + j],
                )
            )
        loads0.append(
            pltpu.make_async_copy(late.at[pl.ds(PANEL, SHARE)], shares.at[k], sem_share.at[k])
        )
    for copy in loads1 + loads_state + loads0:
        copy.start()
    for copy in loads1:
        copy.wait()
    have = Gathered(factor1)
    z1 = columns_t(factor1, 0, row)
    z1_tip, z0_tip = arrow[1], arrow[0]
    u, u_tip = have.past(z0_own(misc, second, core))
    u_tip = u_tip - z0_tip.astype(F32)
    uh, ul = split(u)
    uh_tip, ul_tip = split(u_tip)
    rows_in = jnp.concatenate([z1, uh, ul], axis=0)
    tip_in = jnp.concatenate([z1_tip, uh_tip, ul_tip], axis=0)
    for copy in loads_state:
        copy.wait()
    begun = Gathered(state)
    top = begun.times_factor(rows_in, tip_in)
    bottom = begun.over_rows(rows_in, 2) + dot(tip_in, q[...])
    p1, a = top[:64], top[64:128] + top[128:]
    p1_tip, a_tip = bottom[:64], bottom[64:128] + bottom[128:]
    tip[1] = -p1_tip
    tip[0] = a_tip
    stores = [pltpu.make_async_copy(tip, tip_ref, sem_out.at[0])]
    stores[0].start()
    p1h, p1l = split(p1)
    ah, al = split(a)
    p1h_tip, p1l_tip = split(p1_tip)
    ah_tip, al_tip = split(a_tip)
    own = [state[row, h * ROWS : (h + 1) * ROWS, :] for h in range(3)]
    own_rows = jnp.concatenate(own[:2], axis=1)
    out = have.times_factor(
        jnp.concatenate([p1h, p1l, ah, al, own_rows], axis=0),
        jnp.concatenate([p1h_tip, p1l_tip, ah_tip, al_tip, own[2]], axis=0),
    )
    for copy in loads0:
        copy.wait()
    lower[1] = -out[256:]
    sigma1 = x[1].astype(F32) + out[:64] + out[64:128]
    diag[1] = sigma1
    here = [
        pltpu.make_async_copy(diag.at[1], diag_ref.at[1], sem_out.at[1]),
        pltpu.make_async_copy(lower.at[1], lower_ref.at[1], sem_out.at[2]),
    ]
    for copy in here:
        copy.start()
    stores += here
    carried = shares[0].astype(F32)
    for d in range(1, SIDE):
        carried += shares[d].astype(F32)
    carried = jnp.concatenate([carried[:ROWS], carried[ROWS:]], axis=1)
    p0h, p0l = split(carried + out[128:192] + out[192:256])
    out = Gathered(factor0).times_factor(
        jnp.concatenate([p0h, p0l, sigma1.astype(BF)], axis=0),
        jnp.concatenate([-ah_tip, -al_tip, -p1h_tip], axis=0),
    )
    lower[0] = -out[128:]
    diag[0] = x[0].astype(F32) + out[:64] + out[64:128]
    here = [
        pltpu.make_async_copy(diag.at[0], diag_ref.at[0], sem_out.at[3]),
        pltpu.make_async_copy(lower.at[0], lower_ref.at[0], sem_out.at[4]),
    ]
    for copy in here:
        copy.start()
    for copy in stores + here:
        copy.wait()


def on_device(
    lower_factor,
    arrow_factor,
    block_inverse,
    boundary_sigma,
    boundary_tip,
    tip_inverse,
    slope_weights,
    partitions,
):
    slow = pl.BlockSpec(memory_space=pltpu.HBM)
    fast = pl.BlockSpec(memory_space=pltpu.VMEM)
    params = pltpu.CompilerParams(vmem_limit_bytes=VMEM_BYTES)
    rows, start = pl.pallas_call(
        pack_kernel,
        out_shape=(
            jax.ShapeDtypeStruct((SIDE, SENT, HALF), BF),
            jax.ShapeDtypeStruct((ROWS, BLOCK + HALF), BF),
        ),
        in_specs=[slow] * 5,
        out_specs=(slow,) * 2,
        scratch_shapes=[
            pltpu.VMEM((SENT, HALF), BF),
            pltpu.VMEM((ROWS, BLOCK + HALF), BF),
            pltpu.SemaphoreType.DMA((8,)),
            pltpu.SemaphoreType.DMA((2,)),
            pltpu.SemaphoreType.DMA((SIDE + 1,)),
        ],
        compiler_params=params,
        cost_estimate=cost(4),
    )(lower_factor, arrow_factor, block_inverse, boundary_sigma, boundary_tip)
    got = exchange(rows, line_groups(partitions, 0))
    starts = [lax.ppermute(start, EVERY, state_shift(partitions, k)) for k in range(SIDE)]
    sent, *lates = pl.pallas_call(
        panel_kernel,
        out_shape=(
            jax.ShapeDtypeStruct((SIDE, PANEL + MISC, HALF), BF),
        )
        + (jax.ShapeDtypeStruct((LATER + PANEL, HALF), BF),) * SIDE,
        in_specs=[slow, slow, fast] + [slow] * SIDE,
        out_specs=(slow,) * 5,
        scratch_shapes=[
            pltpu.VMEM((SIDE, SENT, HALF), BF),
            pltpu.VMEM((PANEL, HALF), BF),
            pltpu.VMEM((MISC, HALF), BF),
            pltpu.VMEM((SIDE, SHARE, HALF), BF),
            pltpu.SemaphoreType.DMA((SIDE + 1,)),
            pltpu.SemaphoreType.DMA((SIDE * (SIDE + 1),)),
            pltpu.SemaphoreType.DMA((SIDE * (SIDE + 1),)),
            pltpu.SemaphoreType.DMA((16,)),
        ],
        compiler_params=params,
        cost_estimate=cost(12),
    )(got, arrow_factor, slope_weights, *starts)
    early = exchange(sent, line_groups(partitions, 1))
    for k in range(1, SIDE):
        lates[k] = lax.ppermute(lates[k], EVERY, line_shift(partitions, k))
    slope = pl.pallas_call(
        trace_kernel,
        out_shape=jax.ShapeDtypeStruct((32, 8, 128), F32),
        in_specs=[slow] * 6 + [fast],
        out_specs=fast,
        scratch_shapes=[
            pltpu.VMEM((16, PART, HALF), BF),
            pltpu.VMEM((SIDE, MISC, HALF), BF),
            pltpu.VMEM((PANEL, HALF), BF),
            pltpu.VMEM((SIDE, 2 * ROWS, HALF), BF),
            pltpu.VMEM((2, ROWS, HALF), BF),
            pltpu.VMEM((2, ROWS, BLOCK), BF),
            pltpu.VMEM((HALF, HALF), BF),
            pltpu.SemaphoreType.DMA((16,)),
            pltpu.SemaphoreType.DMA((6,)),
        ],
        compiler_params=params,
        cost_estimate=cost(20),
    )(early, lates[0], got, arrow_factor, block_inverse, tip_inverse, slope_weights[:, :, None])
    total = jnp.sum(exchange(slope, plane_groups(partitions)), axis=0)
    in_plane = total
    total = jnp.broadcast_to(total[None], (partitions // 2, 8, 128))
    total = jnp.sum(exchange(total, height_groups(partitions)), axis=0)
    outputs = (
        jax.ShapeDtypeStruct((2, ROWS, BLOCK), F32),
        jax.ShapeDtypeStruct((2, ROWS, BLOCK), F32),
        jax.ShapeDtypeStruct((2, ROWS, HALF), F32),
    )
    diag, lower, tip = pl.pallas_call(
        block_kernel,
        out_shape=outputs,
        in_specs=[slow] * 9,
        out_specs=(slow,) * 3,
        scratch_shapes=[
            pltpu.VMEM((16, PART, HALF), BF),
            pltpu.VMEM((16, PART, HALF), BF),
            pltpu.VMEM((16, PART, HALF), BF),
            pltpu.VMEM((SIDE, SHARE, HALF), BF),
            pltpu.VMEM((SIDE, MISC, HALF), BF),
            pltpu.VMEM((2, ROWS, HALF), BF),
            pltpu.VMEM((2, ROWS, BLOCK), BF),
            pltpu.VMEM((HALF, HALF), BF),
        ]
        + [pltpu.VMEM(leaf.shape, F32) for leaf in outputs]
        + [
            pltpu.SemaphoreType.DMA((16,)),
            pltpu.SemaphoreType.DMA((16,)),
            pltpu.SemaphoreType.DMA((16,)),
            pltpu.SemaphoreType.DMA((SIDE,)),
            pltpu.SemaphoreType.DMA((4,)),
            pltpu.SemaphoreType.DMA((5,)),
        ],
        compiler_params=params,
        cost_estimate=cost(30),
    )(early, *lates, arrow_factor, block_inverse, tip_inverse, in_plane)
    return diag, lower, tip, total[0, 0]


def solution(mesh):
    partitions = mesh.shape["tm"]
    fine = Mesh(mesh.devices.reshape(partitions, SIDE, SIDE), EVERY)
    rows = P("tm", ("y", "x"), None)

    def program(*args):
        return on_device(*args, partitions=partitions)

    return jax.shard_map(
        program,
        mesh=fine,
        in_specs=(rows, rows, rows, rows, rows, P(), P("tm", ("y", "x"))),
        out_specs=(rows, rows, rows, P()),
        check_vma=False,
    )
```

```python
import jax
import jax.numpy as jnp
from jax import lax
from jax.experimental import pallas as pl
from jax.experimental.pallas import tpu as pltpu
from jax.sharding import Mesh, PartitionSpec as P

SIDE = 4
ROWS = 64
HALF = 512
BLOCK = 1024
BF = jnp.bfloat16
F32 = jnp.float32
EVERY = ("tm", "y", "x")

L1, M1, L0, M0, X1 = 0, 2, 3, 5, 6
PART = 3 * ROWS
SENT = 8 * ROWS
SHARE = 2 * ROWS
PANEL = SIDE * PART
MISC = 2 * ROWS + ROWS + 16
WIDE = BLOCK + HALF
LATER = PANEL + SHARE
VMEM_BYTES = 127 * 512 * 1024


def line_groups(partitions, phase):
    groups = []
    for t in range(partitions):
        base = t * SIDE * SIDE
        for i in range(SIDE):
            if (t + phase) % 2 == 0:
                groups.append([base + SIDE * i + x for x in range(SIDE)])
            else:
                groups.append([base + SIDE * y + i for y in range(SIDE)])
    return groups


def plane_groups(partitions):
    plane = 2 * SIDE * SIDE
    return [[z * plane + r for r in range(plane)] for z in range(partitions // 2)]


def height_groups(partitions):
    plane = SIDE * SIDE
    return [
        [t * plane + r for t in range(core, partitions, 2)]
        for core in range(2)
        for r in range(plane)
    ]


def state_shift(partitions, steps):
    pairs = []
    for t in range(partitions - 1):
        for y in range(SIDE):
            for x in range(SIDE):
                to = (y, (x + steps) % SIDE) if t % 2 == 0 else ((y + steps) % SIDE, x)
                source = (t + 1) * SIDE * SIDE + SIDE * y + x
                pairs.append((source, t * SIDE * SIDE + SIDE * to[0] + to[1]))
    return pairs


def line_shift(partitions, steps):
    pairs = []
    for t in range(partitions):
        for y in range(SIDE):
            for x in range(SIDE):
                to = ((y + steps) % SIDE, x) if t % 2 == 0 else (y, (x + steps) % SIDE)
                base = t * SIDE * SIDE
                pairs.append((base + SIDE * y + x, base + SIDE * to[0] + to[1]))
    return pairs


def cost(megabytes):
    return pl.CostEstimate(flops=0, bytes_accessed=megabytes * 1_000_000, transcendentals=0)


def exchange(value, groups):
    return lax.all_to_all(value, EVERY, 0, 0, tiled=True, axis_index_groups=groups)


def dot(left, right):
    return jnp.dot(left, right, preferred_element_type=F32)


def dot_t(left, right):
    return lax.dot_general(left, right, (((1,), (1,)), ((), ())), preferred_element_type=F32)


def split(value):
    high = value.astype(BF)
    return high, (value - high.astype(F32)).astype(BF)


def place():
    core = lax.rem(lax.axis_index("tm"), 2)
    y, x = lax.axis_index("y"), lax.axis_index("x")
    first = jnp.where(core == 0, x, y)
    return core, y * SIDE + x, first


def natural(core, second, first):
    return jnp.where(core == 0, SIDE * second + first, SIDE * first + second)


def columns_t(ref, piece, row, blocks=None):
    half = lax.div(row, 8)
    lane = lax.div(lax.rem(row, 8), 2)
    rows = pl.ds(pl.multiple_of((piece + half) * ROWS, ROWS), ROWS)
    lanes = pl.ds(pl.multiple_of(lane * 128, 128), 128)
    if blocks is None:
        window = ref[:, rows, lanes]
        window = window.reshape(window.shape[0] * ROWS, 128)
    else:
        window = jnp.concatenate([ref[b, rows, lanes] for b in blocks], axis=0)
    want = lax.broadcasted_iota(jnp.int32, (ROWS, 128), 0) + lax.rem(row, 2) * ROWS
    pick = jnp.where(lax.broadcasted_iota(jnp.int32, (ROWS, 128), 1) == want, 1.0, 0.0)
    return dot_t(pick.astype(BF), window).astype(BF)


def pack_kernel(low, arrow, inverse, sigma, tip, out, start, held, own, sem_in, sem_own, sem_out):
    loads = []
    for k, (ref, j, h) in enumerate(
        [(low, 1, 0), (low, 1, 1), (arrow, 1, 0), (low, 0, 0), (low, 0, 1), (arrow, 0, 0)]
        + [(inverse, 1, 0), (inverse, 1, 1)]
    ):
        loads.append(
            pltpu.make_async_copy(
                ref.at[j, :, pl.ds(h * HALF, HALF)],
                held.at[pl.ds(k * ROWS, ROWS)],
                sem_in.at[k],
            )
        )
    loads_own = [
        pltpu.make_async_copy(sigma.at[0], own.at[:, pl.ds(0, BLOCK)], sem_own.at[0]),
        pltpu.make_async_copy(tip.at[0], own.at[:, pl.ds(BLOCK, HALF)], sem_own.at[1]),
    ]
    for copy in loads + loads_own:
        copy.start()
    for copy in loads + loads_own:
        copy.wait()
    stores = [pltpu.make_async_copy(held, out.at[d], sem_out.at[d]) for d in range(SIDE)]
    stores.append(pltpu.make_async_copy(own, start, sem_out.at[SIDE]))
    for copy in stores:
        copy.start()
    for copy in stores:
        copy.wait()


def panel_kernel(
    got, arrow, weight, own0, own1, own2, own3, out, panel, misc, sem_in, sem_out
):
    del own0, own1, own2, own3
    core, _, first = place()
    loads = [
        pltpu.make_async_copy(got.at[j, pl.ds(0, 2 * PART)], panel.at[j], sem_in.at[j])
        for j in range(SIDE)
    ]
    load_arrow = pltpu.make_async_copy(
        arrow.at[0], misc.at[pl.ds(2 * ROWS, ROWS)], sem_in.at[SIDE]
    )
    for copy in loads + [load_arrow]:
        copy.start()
    stores = []
    for j in range(SIDE):
        loads[j].wait()
        here = [
            pltpu.make_async_copy(
                panel.at[j, pl.ds(0, PART)],
                out.at[d, pl.ds(j * PART, PART)],
                sem_out.at[d * (SIDE + 1) + j],
            )
            for d in range(SIDE)
        ]
        for copy in here:
            copy.start()
        stores += here
    cols = [columns_t(panel, L0, natural(core, d, first)) for d in range(SIDE)]
    cols = jnp.concatenate(cols, axis=0)
    misc[: 2 * ROWS, :] = jnp.concatenate([cols[: 2 * ROWS], cols[2 * ROWS :]], axis=1)
    rest = weight[...]
    parts = []
    for _ in range(3):
        parts.append(rest.astype(BF).astype(F32))
        rest = rest - parts[-1]
    parts = jnp.concatenate(parts + [jnp.zeros((10, ROWS), F32)], axis=0)
    parts = jnp.concatenate([parts, jnp.zeros((16, HALF - ROWS), F32)], axis=1)
    misc[3 * ROWS :, :] = parts.astype(BF)
    load_arrow.wait()
    here = [
        pltpu.make_async_copy(misc, out.at[d, pl.ds(PANEL, MISC)], sem_out.at[d * (SIDE + 1) + SIDE])
        for d in range(SIDE)
    ]
    for copy in here:
        copy.start()
    for copy in stores + here:
        copy.wait()


def later_kernel(
    got,
    own0,
    own1,
    own2,
    own3,
    late0,
    late1,
    late2,
    late3,
    panel,
    state,
    share,
    sem_in,
    sem_out,
    sem_state,
):
    core, _, first = place()
    second = jnp.where(core == 0, lax.axis_index("y"), lax.axis_index("x"))
    lates = (late0, late1, late2, late3)
    loads = [
        pltpu.make_async_copy(got.at[j, pl.ds(PART, SENT - PART)], panel.at[j], sem_in.at[j])
        for j in range(SIDE)
    ]
    loads_state = [
        pltpu.make_async_copy(
            own.at[:, pl.ds(h * HALF, HALF)],
            state.at[pl.ds(k * PART + h * ROWS, ROWS)],
            sem_state.at[k * 3 + h],
        )
        for k, own in enumerate((own0, own1, own2, own3))
        for h in range(3)
    ]
    for copy in loads + loads_state:
        copy.start()
    for copy in loads + loads_state:
        copy.wait()
    stores = []
    for k, late in enumerate(lates):
        stores += [
            pltpu.make_async_copy(
                panel.at[j, pl.ds(0, PART)],
                late.at[pl.ds(j * PART, PART)],
                sem_out.at[k * (SIDE + 1) + j],
            )
            for j in range(SIDE)
        ]
        stores.append(
            pltpu.make_async_copy(state, late.at[pl.ds(LATER, PANEL)], sem_state.at[12 + k])
        )
    for copy in stores:
        copy.start()
    cols = [columns_t(panel, 0, natural(core, d, first)) for d in range(SIDE)]
    cols = jnp.concatenate(cols, axis=0)
    for h in range(2):
        at = PART + h * ROWS
        part = dot(cols, panel[:, at : at + ROWS, :].reshape(SIDE * ROWS, HALF))
        for d in range(SIDE):
            share[d, h * ROWS : (h + 1) * ROWS, :] = part[d * ROWS : (d + 1) * ROWS].astype(BF)
    here = [
        pltpu.make_async_copy(
            share.at[lax.rem(second + k, SIDE)],
            late.at[pl.ds(PANEL, SHARE)],
            sem_out.at[k * (SIDE + 1) + SIDE],
        )
        for k, late in enumerate(lates)
    ]
    for copy in here:
        copy.start()
    for copy in stores + here:
        copy.wait()


class Gathered:
    def __init__(self, mat):
        self.mat = mat

    def piece(self, k):
        return self.mat[:, k * ROWS : (k + 1) * ROWS, :].reshape(BLOCK, HALF)

    def over_rows(self, left, k):
        return dot(left, self.piece(k))

    def over_columns(self, left, k):
        return dot_t(left, self.piece(k))

    def times_factor(self, left_rows, left_tip):
        both = jnp.concatenate([self.over_rows(left_rows, h) for h in range(2)], axis=1)
        return both + self.over_columns(left_tip, 2)

    def past(self, left):
        u = self.over_columns(left[:, :HALF], 0) + self.over_columns(left[:, HALF:], 1)
        return u, self.over_rows(left, 2)


def load_exchanged(got, mat, sem):
    core, _, _ = place()
    return [
        pltpu.make_async_copy(
            got.at[d, pl.ds(j * PART, PART)],
            mat.at[natural(core, d, j)],
            sem.at[d * SIDE + j],
        )
        for d in range(SIDE)
        for j in range(SIDE)
    ]


def in_order(core, parts):
    even = jnp.concatenate(parts, axis=1)
    odd = [parts[d][:, j * 64 : (j + 1) * 64] for j in range(SIDE) for d in range(SIDE)]
    return jnp.where(core == 0, even, jnp.concatenate(odd, axis=1))


def sum_all(value):
    return jnp.sum(jnp.sum(value, axis=1, keepdims=True))


def trace_kernel(
    got,
    begun,
    panel_ref,
    arrow_ref,
    x_ref,
    q_ref,
    weight_ref,
    slope,
    factor,
    misc,
    state,
    inverse,
    arrow,
    x,
    q,
    sem_factor,
    sem_in,
):
    core, row, first = place()
    second = jnp.where(core == 0, lax.axis_index("y"), lax.axis_index("x"))
    load_misc = pltpu.make_async_copy(got.at[:, pl.ds(PANEL, MISC)], misc, sem_in.at[0])
    load_factor = load_exchanged(got, factor, sem_factor)
    later = [
        pltpu.make_async_copy(begun.at[pl.ds(LATER, PANEL)], state, sem_in.at[1]),
        pltpu.make_async_copy(
            panel_ref.at[:, pl.ds(X1 * ROWS, 2 * ROWS)], inverse, sem_in.at[2]
        ),
        pltpu.make_async_copy(arrow_ref, arrow, sem_in.at[3]),
        pltpu.make_async_copy(q_ref, q, sem_in.at[4]),
        pltpu.make_async_copy(x_ref, x, sem_in.at[5]),
    ]
    for copy in [load_misc] + load_factor + later:
        copy.start()
    load_misc.wait()
    columns = [natural(core, d, first) for d in range(SIDE)]
    mine = [natural(core, second, lax.rem(first + SIDE - k, SIDE)) for k in range(SIDE)]
    parts = []
    for d in range(SIDE):
        held = misc[d, : 2 * ROWS, :]
        parts.append(jnp.concatenate([held[:, :256], held[:, 256:]], axis=0))
    z0 = in_order(core, parts)
    z0_tip = misc[:, 2 * ROWS : 3 * ROWS, :].reshape(256, HALF)
    eye = lax.broadcasted_iota(jnp.int32, (ROWS, ROWS), 0)
    eye = jnp.where(eye == lax.broadcasted_iota(jnp.int32, (ROWS, ROWS), 1), 1.0, 0.0)
    weights = []
    for block in range(2):
        column = []
        for d in range(SIDE):
            held = misc[d, 3 * ROWS :, :].astype(F32)
            held = held[block : block + 1] + held[block + 2 : block + 3] + held[block + 4 : block + 5]
            column.append(jnp.sum(eye * held[:, :ROWS], axis=1, keepdims=True))
        weights.append(jnp.concatenate(column, axis=0))
    for copy in load_factor:
        copy.wait()
    have = Gathered(factor)
    u, u_tip = have.past(z0)
    u_tip = u_tip - z0_tip.astype(F32)
    u_mine = jnp.zeros((256, 256), F32)
    z1_mine = []
    for h in range(2):
        low = jnp.concatenate([factor[b, h * ROWS : (h + 1) * ROWS, :] for b in mine], axis=0)
        u_mine += dot_t(z0[:, h * HALF : (h + 1) * HALF], low)
    z1 = jnp.concatenate([columns_t(factor, 0, c) for c in columns], axis=0)
    z1_mine = jnp.concatenate([columns_t(factor, 0, c, mine) for c in columns], axis=0)
    z1_tip = jnp.concatenate([factor[c, 2 * ROWS :, :] for c in columns], axis=0)
    for copy in later:
        copy.wait()
    rows_in = jnp.concatenate([u.astype(BF), z1], axis=0)
    tip_in = jnp.concatenate([u_tip.astype(BF), z1_tip], axis=0)
    held = state[...].reshape(SIDE, PART, HALF)
    held = [held[:, h * ROWS : (h + 1) * ROWS, :].reshape(256, HALF) for h in range(3)]
    through = dot_t(rows_in[:, :HALF], held[0]) + dot_t(rows_in[:, HALF:], held[1])
    through += 2.0 * dot_t(tip_in, held[2])
    carried = jnp.zeros((256, 256), F32)
    for h in range(2):
        part = inverse[:, h * ROWS : (h + 1) * ROWS, :].reshape(256, HALF)
        carried += dot_t(z0[:, h * HALF : (h + 1) * HALF], part)
    own_parts = parts[0]
    for d in range(1, SIDE):
        own_parts = jnp.where(second == d, parts[d], own_parts)
    traced = (u_mine * through[:256] + own_parts.astype(F32) * carried) * weights[0]
    traced += z1_mine.astype(F32) * through[256:] * weights[1]
    own_tip = dot(z0_own(misc, second, core), Gathered(factor).piece(2))
    own_tip = own_tip - arrow[0].astype(F32)
    both = jnp.concatenate([own_tip.astype(BF), arrow[1]], axis=0)
    tip_traced = both.astype(F32) * dot(both, q[...])
    at = lax.broadcasted_iota(jnp.int32, (ROWS, BLOCK), 0) + row * ROWS
    on_diagonal = lax.broadcasted_iota(jnp.int32, (ROWS, BLOCK), 1) == at
    total = sum_all(traced)
    for block in range(2):
        total += sum_all(tip_traced[block * ROWS : (block + 1) * ROWS] * weight_ref[block])
        own = jnp.where(on_diagonal, x[block].astype(F32), 0.0)
        total += sum_all(own * weight_ref[block])
    slope[...] = jnp.full(slope.shape, total, F32)


def z0_own(misc, second, core):
    rows = pl.ds(pl.multiple_of(lax.rem(second, 2) * ROWS, ROWS), ROWS)
    lanes = pl.ds(pl.multiple_of(lax.div(second, 2) * 256, 256), 256)
    return in_order(core, [misc[d, rows, lanes] for d in range(SIDE)])


def block_kernel(
    got,
    late0,
    late1,
    late2,
    late3,
    arrow_ref,
    x_ref,
    q_ref,
    diag_ref,
    lower_ref,
    tip_ref,
    factor1,
    factor0,
    state,
    shares,
    misc,
    arrow,
    x,
    q,
    diag,
    lower,
    tip,
    sem_factor1,
    sem_factor0,
    sem_state,
    sem_share,
    sem_in,
    sem_out,
):
    core, row, first = place()
    second = jnp.where(core == 0, lax.axis_index("y"), lax.axis_index("x"))
    loads1 = [
        pltpu.make_async_copy(got.at[:, pl.ds(PANEL, MISC)], misc, sem_in.at[0]),
        pltpu.make_async_copy(arrow_ref, arrow, sem_in.at[1]),
    ] + load_exchanged(got, factor1, sem_factor1)
    loads_state = [pltpu.make_async_copy(q_ref, q, sem_in.at[2])]
    loads0 = [pltpu.make_async_copy(x_ref, x, sem_in.at[3])]
    for k, late in enumerate((late0, late1, late2, late3)):
        source = lax.rem(second + SIDE - k, SIDE)
        for j in range(SIDE):
            behind = lax.rem(first + SIDE - j, SIDE)
            loads_state.append(
                pltpu.make_async_copy(
                    late.at[pl.ds(LATER + j * PART, PART)],
                    state.at[natural(core, source, behind)],
                    sem_state.at[k * SIDE + j],
                )
            )
            loads0.append(
                pltpu.make_async_copy(
                    late.at[pl.ds(j * PART, PART)],
                    factor0.at[natural(core, source, j)],
                    sem_factor0.at[k * SIDE + j],
                )
            )
        loads0.append(
            pltpu.make_async_copy(late.at[pl.ds(PANEL, SHARE)], shares.at[k], sem_share.at[k])
        )
    for copy in loads1 + loads_state + loads0:
        copy.start()
    for copy in loads1:
        copy.wait()
    have = Gathered(factor1)
    z1 = columns_t(factor1, 0, row)
    z1_tip, z0_tip = arrow[1], arrow[0]
    u, u_tip = have.past(z0_own(misc, second, core))
    u_tip = u_tip - z0_tip.astype(F32)
    uh, ul = split(u)
    uh_tip, ul_tip = split(u_tip)
    rows_in = jnp.concatenate([z1, uh, ul], axis=0)
    tip_in = jnp.concatenate([z1_tip, uh_tip, ul_tip], axis=0)
    for copy in loads_state:
        copy.wait()
    begun = Gathered(state)
    top = begun.times_factor(rows_in, tip_in)
    bottom = begun.over_rows(rows_in, 2) + dot(tip_in, q[...])
    p1, a = top[:64], top[64:128] + top[128:]
    p1_tip, a_tip = bottom[:64], bottom[64:128] + bottom[128:]
    tip[1] = -p1_tip
    tip[0] = a_tip
    stores = [pltpu.make_async_copy(tip, tip_ref, sem_out.at[0])]
    stores[0].start()
    p1h, p1l = split(p1)
    ah, al = split(a)
    p1h_tip, p1l_tip = split(p1_tip)
    ah_tip, al_tip = split(a_tip)
    own = [state[row, h * ROWS : (h + 1) * ROWS, :] for h in range(3)]
    own_rows = jnp.concatenate(own[:2], axis=1)
    out = have.times_factor(
        jnp.concatenate([p1h, p1l, ah, al, own_rows], axis=0),
        jnp.concatenate([p1h_tip, p1l_tip, ah_tip, al_tip, own[2]], axis=0),
    )
    for copy in loads0:
        copy.wait()
    lower[1] = -out[256:]
    sigma1 = x[1].astype(F32) + out[:64] + out[64:128]
    diag[1] = sigma1
    here = [
        pltpu.make_async_copy(diag.at[1], diag_ref.at[1], sem_out.at[1]),
        pltpu.make_async_copy(lower.at[1], lower_ref.at[1], sem_out.at[2]),
    ]
    for copy in here:
        copy.start()
    stores += here
    carried = shares[0].astype(F32)
    for d in range(1, SIDE):
        carried += shares[d].astype(F32)
    carried = jnp.concatenate([carried[:ROWS], carried[ROWS:]], axis=1)
    p0h, p0l = split(carried + out[128:192] + out[192:256])
    out = Gathered(factor0).times_factor(
        jnp.concatenate([p0h, p0l, sigma1.astype(BF)], axis=0),
        jnp.concatenate([-ah_tip, -al_tip, -p1h_tip], axis=0),
    )
    lower[0] = -out[128:]
    diag[0] = x[0].astype(F32) + out[:64] + out[64:128]
    here = [
        pltpu.make_async_copy(diag.at[0], diag_ref.at[0], sem_out.at[3]),
        pltpu.make_async_copy(lower.at[0], lower_ref.at[0], sem_out.at[4]),
    ]
    for copy in here:
        copy.start()
    for copy in stores + here:
        copy.wait()


def on_device(
    lower_factor,
    arrow_factor,
    block_inverse,
    boundary_sigma,
    boundary_tip,
    tip_inverse,
    slope_weights,
    partitions,
):
    slow = pl.BlockSpec(memory_space=pltpu.HBM)
    fast = pl.BlockSpec(memory_space=pltpu.VMEM)
    params = pltpu.CompilerParams(vmem_limit_bytes=VMEM_BYTES)
    rows, start = pl.pallas_call(
        pack_kernel,
        out_shape=(
            jax.ShapeDtypeStruct((SIDE, SENT, HALF), BF),
            jax.ShapeDtypeStruct((ROWS, BLOCK + HALF), BF),
        ),
        in_specs=[slow] * 5,
        out_specs=(slow,) * 2,
        scratch_shapes=[
            pltpu.VMEM((SENT, HALF), BF),
            pltpu.VMEM((ROWS, BLOCK + HALF), BF),
            pltpu.SemaphoreType.DMA((8,)),
            pltpu.SemaphoreType.DMA((2,)),
            pltpu.SemaphoreType.DMA((SIDE + 1,)),
        ],
        compiler_params=params,
        cost_estimate=cost(4),
    )(lower_factor, arrow_factor, block_inverse, boundary_sigma, boundary_tip)
    got = exchange(rows, line_groups(partitions, 0))
    starts = [lax.ppermute(start, EVERY, state_shift(partitions, k)) for k in range(SIDE)]
    sent = pl.pallas_call(
        panel_kernel,
        out_shape=jax.ShapeDtypeStruct((SIDE, PANEL + MISC, HALF), BF),
        in_specs=[slow, slow, fast] + [slow] * SIDE,
        out_specs=slow,
        scratch_shapes=[
            pltpu.VMEM((SIDE, 2 * PART, HALF), BF),
            pltpu.VMEM((MISC, HALF), BF),
            pltpu.SemaphoreType.DMA((SIDE + 1,)),
            pltpu.SemaphoreType.DMA((SIDE * (SIDE + 1),)),
        ],
        compiler_params=params,
        cost_estimate=cost(12),
    )(got, arrow_factor, slope_weights, *starts)
    lates = pl.pallas_call(
        later_kernel,
        out_shape=(jax.ShapeDtypeStruct((LATER + PANEL, HALF), BF),) * SIDE,
        in_specs=[slow] * 5,
        out_specs=(slow,) * 4,
        scratch_shapes=[
            pltpu.VMEM((SIDE, SENT - PART, HALF), BF),
            pltpu.VMEM((PANEL, HALF), BF),
            pltpu.VMEM((SIDE, SHARE, HALF), BF),
            pltpu.SemaphoreType.DMA((SIDE,)),
            pltpu.SemaphoreType.DMA((SIDE * (SIDE + 1),)),
            pltpu.SemaphoreType.DMA((16,)),
        ],
        compiler_params=params,
        cost_estimate=cost(12),
    )(got, *starts)
    lates = list(lates)
    early = exchange(sent, line_groups(partitions, 1))
    for k in range(1, SIDE):
        lates[k] = lax.ppermute(lates[k], EVERY, line_shift(partitions, k))
    slope = pl.pallas_call(
        trace_kernel,
        out_shape=jax.ShapeDtypeStruct((partitions // 2, 8, 128), F32),
        in_specs=[slow] * 6 + [fast],
        out_specs=fast,
        scratch_shapes=[
            pltpu.VMEM((16, PART, HALF), BF),
            pltpu.VMEM((SIDE, MISC, HALF), BF),
            pltpu.VMEM((PANEL, HALF), BF),
            pltpu.VMEM((SIDE, 2 * ROWS, HALF), BF),
            pltpu.VMEM((2, ROWS, HALF), BF),
            pltpu.VMEM((2, ROWS, BLOCK), BF),
            pltpu.VMEM((HALF, HALF), BF),
            pltpu.SemaphoreType.DMA((16,)),
            pltpu.SemaphoreType.DMA((6,)),
        ],
        compiler_params=params,
        cost_estimate=cost(20),
    )(early, lates[0], got, arrow_factor, block_inverse, tip_inverse, slope_weights[:, :, None])
    total = jnp.sum(exchange(slope, height_groups(partitions)), axis=0)
    total = jnp.broadcast_to(total[None], (2 * SIDE * SIDE, 8, 128))
    total = jnp.sum(exchange(total, plane_groups(partitions)), axis=0)
    outputs = (
        jax.ShapeDtypeStruct((2, ROWS, BLOCK), F32),
        jax.ShapeDtypeStruct((2, ROWS, BLOCK), F32),
        jax.ShapeDtypeStruct((2, ROWS, HALF), F32),
    )
    diag, lower, tip = pl.pallas_call(
        block_kernel,
        out_shape=outputs,
        in_specs=[slow] * 8,
        out_specs=(slow,) * 3,
        scratch_shapes=[
            pltpu.VMEM((16, PART, HALF), BF),
            pltpu.VMEM((16, PART, HALF), BF),
            pltpu.VMEM((16, PART, HALF), BF),
            pltpu.VMEM((SIDE, SHARE, HALF), BF),
            pltpu.VMEM((SIDE, MISC, HALF), BF),
            pltpu.VMEM((2, ROWS, HALF), BF),
            pltpu.VMEM((2, ROWS, BLOCK), BF),
            pltpu.VMEM((HALF, HALF), BF),
        ]
        + [pltpu.VMEM(leaf.shape, F32) for leaf in outputs]
        + [
            pltpu.SemaphoreType.DMA((16,)),
            pltpu.SemaphoreType.DMA((16,)),
            pltpu.SemaphoreType.DMA((16,)),
            pltpu.SemaphoreType.DMA((SIDE,)),
            pltpu.SemaphoreType.DMA((4,)),
            pltpu.SemaphoreType.DMA((5,)),
        ],
        compiler_params=params,
        cost_estimate=cost(30),
    )(early, *lates, arrow_factor, block_inverse, tip_inverse)
    return diag, lower, tip, total[0, 0]


def solution(mesh):
    partitions = mesh.shape["tm"]
    fine = Mesh(mesh.devices.reshape(partitions, SIDE, SIDE), EVERY)
    rows = P("tm", ("y", "x"), None)

    def program(*args):
        return on_device(*args, partitions=partitions)

    return jax.shard_map(
        program,
        mesh=fine,
        in_specs=(rows, rows, rows, rows, rows, P(), P("tm", ("y", "x"))),
        out_specs=(rows, rows, rows, P()),
        check_vma=False,
    )
```

```python
import jax
import jax.numpy as jnp
from jax import lax
from jax.experimental import pallas as pl
from jax.experimental.pallas import tpu as pltpu
from jax.sharding import Mesh, PartitionSpec as P

SIDE = 4
ROWS = 64
HALF = 512
BLOCK = 1024
BF = jnp.bfloat16
F32 = jnp.float32
EVERY = ("tm", "y", "x")

L1, M1, L0, M0, X1 = 0, 2, 3, 5, 6
PART = 3 * ROWS
SENT = 8 * ROWS
SHARE = 2 * ROWS
PANEL = SIDE * PART
MISC = 2 * ROWS + ROWS + 16
WIDE = BLOCK + HALF
LATER = PANEL + SHARE
VMEM_BYTES = 127 * 512 * 1024


def line_groups(partitions, phase):
    groups = []
    for t in range(partitions):
        base = t * SIDE * SIDE
        for i in range(SIDE):
            if (t + phase) % 2 == 0:
                groups.append([base + SIDE * i + x for x in range(SIDE)])
            else:
                groups.append([base + SIDE * y + i for y in range(SIDE)])
    return groups


def plane_groups(partitions):
    plane = 2 * SIDE * SIDE
    return [[z * plane + r for r in range(plane)] for z in range(partitions // 2)]


def height_groups(partitions):
    plane = SIDE * SIDE
    return [
        [t * plane + r for t in range(core, partitions, 2)]
        for core in range(2)
        for r in range(plane)
    ]


def state_shift(partitions, steps):
    pairs = []
    for t in range(partitions - 1):
        for y in range(SIDE):
            for x in range(SIDE):
                to = (y, (x + steps) % SIDE) if t % 2 == 0 else ((y + steps) % SIDE, x)
                source = (t + 1) * SIDE * SIDE + SIDE * y + x
                pairs.append((source, t * SIDE * SIDE + SIDE * to[0] + to[1]))
    return pairs


def line_shift(partitions, steps):
    pairs = []
    for t in range(partitions):
        for y in range(SIDE):
            for x in range(SIDE):
                to = ((y + steps) % SIDE, x) if t % 2 == 0 else (y, (x + steps) % SIDE)
                base = t * SIDE * SIDE
                pairs.append((base + SIDE * y + x, base + SIDE * to[0] + to[1]))
    return pairs


def cost(megabytes):
    return pl.CostEstimate(flops=0, bytes_accessed=megabytes * 1_000_000, transcendentals=0)


def exchange(value, groups):
    return lax.all_to_all(value, EVERY, 0, 0, tiled=True, axis_index_groups=groups)


def dot(left, right):
    return jnp.dot(left, right, preferred_element_type=F32)


def dot_t(left, right):
    return lax.dot_general(left, right, (((1,), (1,)), ((), ())), preferred_element_type=F32)


def split(value):
    high = value.astype(BF)
    return high, (value - high.astype(F32)).astype(BF)


def place():
    core = lax.rem(lax.axis_index("tm"), 2)
    y, x = lax.axis_index("y"), lax.axis_index("x")
    first = jnp.where(core == 0, x, y)
    return core, y * SIDE + x, first


def natural(core, second, first):
    return jnp.where(core == 0, SIDE * second + first, SIDE * first + second)


def columns_t(ref, piece, row, blocks=None):
    half = lax.div(row, 8)
    lane = lax.div(lax.rem(row, 8), 2)
    rows = pl.ds(pl.multiple_of((piece + half) * ROWS, ROWS), ROWS)
    lanes = pl.ds(pl.multiple_of(lane * 128, 128), 128)
    if blocks is None:
        window = ref[:, rows, lanes]
        window = window.reshape(window.shape[0] * ROWS, 128)
    else:
        window = jnp.concatenate([ref[b, rows, lanes] for b in blocks], axis=0)
    want = lax.broadcasted_iota(jnp.int32, (ROWS, 128), 0) + lax.rem(row, 2) * ROWS
    pick = jnp.where(lax.broadcasted_iota(jnp.int32, (ROWS, 128), 1) == want, 1.0, 0.0)
    return dot_t(pick.astype(BF), window).astype(BF)


def pack_kernel(low, arrow, inverse, sigma, tip, out, start, held, own, sem_in, sem_own, sem_out):
    loads = []
    for k, (ref, j, h) in enumerate(
        [(low, 1, 0), (low, 1, 1), (arrow, 1, 0), (low, 0, 0), (low, 0, 1), (arrow, 0, 0)]
        + [(inverse, 1, 0), (inverse, 1, 1)]
    ):
        loads.append(
            pltpu.make_async_copy(
                ref.at[j, :, pl.ds(h * HALF, HALF)],
                held.at[pl.ds(k * ROWS, ROWS)],
                sem_in.at[k],
            )
        )
    loads_own = [
        pltpu.make_async_copy(sigma.at[0], own.at[:, pl.ds(0, BLOCK)], sem_own.at[0]),
        pltpu.make_async_copy(tip.at[0], own.at[:, pl.ds(BLOCK, HALF)], sem_own.at[1]),
    ]
    for copy in loads + loads_own:
        copy.start()
    stores = []
    for h in range(2):
        for copy in loads[4 * h : 4 * h + 4]:
            copy.wait()
        rows = pl.ds(h * SENT // 2, SENT // 2)
        here = [
            pltpu.make_async_copy(held.at[rows], out.at[d, rows], sem_out.at[d * 2 + h])
            for d in range(SIDE)
        ]
        for copy in here:
            copy.start()
        stores += here
    for copy in loads_own:
        copy.wait()
    stores.append(pltpu.make_async_copy(own, start, sem_out.at[2 * SIDE]))
    stores[-1].start()
    for copy in stores:
        copy.wait()


def panel_kernel(
    got, arrow, weight, own0, own1, own2, own3, out, panel, misc, sem_in, sem_out
):
    del own0, own1, own2, own3
    core, _, first = place()
    loads = [
        pltpu.make_async_copy(got.at[j, pl.ds(0, 5 * ROWS)], panel.at[j], sem_in.at[j])
        for j in range(SIDE)
    ]
    load_arrow = pltpu.make_async_copy(
        arrow.at[0], misc.at[pl.ds(2 * ROWS, ROWS)], sem_in.at[SIDE]
    )
    for copy in loads + [load_arrow]:
        copy.start()
    stores = []
    for j in range(SIDE):
        loads[j].wait()
        here = [
            pltpu.make_async_copy(
                panel.at[j, pl.ds(0, PART)],
                out.at[d, pl.ds(j * PART, PART)],
                sem_out.at[d * (SIDE + 1) + j],
            )
            for d in range(SIDE)
        ]
        for copy in here:
            copy.start()
        stores += here
    cols = [columns_t(panel, L0, natural(core, d, first)) for d in range(SIDE)]
    cols = jnp.concatenate(cols, axis=0)
    misc[: 2 * ROWS, :] = jnp.concatenate([cols[: 2 * ROWS], cols[2 * ROWS :]], axis=1)
    rest = weight[...]
    parts = []
    for _ in range(3):
        parts.append(rest.astype(BF).astype(F32))
        rest = rest - parts[-1]
    parts = jnp.concatenate(parts + [jnp.zeros((10, ROWS), F32)], axis=0)
    parts = jnp.concatenate([parts, jnp.zeros((16, HALF - ROWS), F32)], axis=1)
    misc[3 * ROWS :, :] = parts.astype(BF)
    load_arrow.wait()
    here = [
        pltpu.make_async_copy(misc, out.at[d, pl.ds(PANEL, MISC)], sem_out.at[d * (SIDE + 1) + SIDE])
        for d in range(SIDE)
    ]
    for copy in here:
        copy.start()
    for copy in stores + here:
        copy.wait()


def later_kernel(
    got,
    own0,
    own1,
    own2,
    own3,
    begun0,
    begun1,
    begun2,
    begun3,
    late,
    panel,
    state,
    share,
    sem_in,
    sem_out,
    sem_state,
):
    core, _, first = place()
    second = jnp.where(core == 0, lax.axis_index("y"), lax.axis_index("x"))
    all_begun = (begun0, begun1, begun2, begun3)
    loads = [
        pltpu.make_async_copy(got.at[j, pl.ds(PART, SENT - PART)], panel.at[j], sem_in.at[j])
        for j in range(SIDE)
    ]
    loads_state = [
        pltpu.make_async_copy(
            own.at[:, pl.ds(h * HALF, HALF)],
            state.at[pl.ds(k * PART + h * ROWS, ROWS)],
            sem_state.at[k * 3 + h],
        )
        for k, own in enumerate((own0, own1, own2, own3))
        for h in range(3)
    ]
    for copy in loads + loads_state:
        copy.start()
    for copy in loads + loads_state:
        copy.wait()
    stores = [
        pltpu.make_async_copy(state, begun.at[pl.ds(0, PANEL)], sem_state.at[12 + k])
        for k, begun in enumerate(all_begun)
    ]
    for k, (ref, at) in enumerate(((late, 0), (begun2, LATER))):
        stores += [
            pltpu.make_async_copy(
                panel.at[j, pl.ds(0, PART)],
                ref.at[pl.ds(at + j * PART, PART)],
                sem_out.at[k * SIDE + j],
            )
            for j in range(SIDE)
        ]
    for copy in stores:
        copy.start()
    cols = [columns_t(panel, 0, natural(core, d, first)) for d in range(SIDE)]
    cols = jnp.concatenate(cols, axis=0)
    for h in range(2):
        at = PART + h * ROWS
        part = dot(cols, panel[:, at : at + ROWS, :].reshape(SIDE * ROWS, HALF))
        for d in range(SIDE):
            share[d, h * ROWS : (h + 1) * ROWS, :] = part[d * ROWS : (d + 1) * ROWS].astype(BF)
    here = [
        pltpu.make_async_copy(
            share.at[lax.rem(second + k, SIDE)],
            begun.at[pl.ds(PANEL, SHARE)],
            sem_out.at[2 * SIDE + k],
        )
        for k, begun in enumerate(all_begun)
    ]
    for copy in here:
        copy.start()
    for copy in stores + here:
        copy.wait()


class Gathered:
    def __init__(self, mat):
        self.mat = mat

    def piece(self, k):
        return self.mat[:, k * ROWS : (k + 1) * ROWS, :].reshape(BLOCK, HALF)

    def over_rows(self, left, k):
        return dot(left, self.piece(k))

    def over_columns(self, left, k):
        return dot_t(left, self.piece(k))

    def times_factor(self, left_rows, left_tip):
        both = jnp.concatenate([self.over_rows(left_rows, h) for h in range(2)], axis=1)
        return both + self.over_columns(left_tip, 2)

    def past(self, left):
        u = self.over_columns(left[:, :HALF], 0) + self.over_columns(left[:, HALF:], 1)
        return u, self.over_rows(left, 2)


def load_exchanged(got, mat, sem):
    core, _, _ = place()
    return [
        pltpu.make_async_copy(
            got.at[d, pl.ds(j * PART, PART)],
            mat.at[natural(core, d, j)],
            sem.at[d * SIDE + j],
        )
        for d in range(SIDE)
        for j in range(SIDE)
    ]


def in_order(core, parts):
    even = jnp.concatenate(parts, axis=1)
    odd = [parts[d][:, j * 64 : (j + 1) * 64] for j in range(SIDE) for d in range(SIDE)]
    return jnp.where(core == 0, even, jnp.concatenate(odd, axis=1))


def sum_all(value):
    return jnp.sum(jnp.sum(value, axis=1, keepdims=True))


def trace_kernel(
    got,
    begun,
    panel_ref,
    arrow_ref,
    x_ref,
    q_ref,
    weight_ref,
    slope,
    factor,
    misc,
    state,
    inverse,
    arrow,
    x,
    q,
    sem_factor,
    sem_in,
):
    core, row, first = place()
    second = jnp.where(core == 0, lax.axis_index("y"), lax.axis_index("x"))
    load_misc = pltpu.make_async_copy(got.at[:, pl.ds(PANEL, MISC)], misc, sem_in.at[0])
    load_factor = load_exchanged(got, factor, sem_factor)
    later = [
        pltpu.make_async_copy(begun.at[pl.ds(0, PANEL)], state, sem_in.at[1]),
        pltpu.make_async_copy(
            panel_ref.at[:, pl.ds(X1 * ROWS, 2 * ROWS)], inverse, sem_in.at[2]
        ),
        pltpu.make_async_copy(arrow_ref, arrow, sem_in.at[3]),
        pltpu.make_async_copy(q_ref, q, sem_in.at[4]),
        pltpu.make_async_copy(x_ref, x, sem_in.at[5]),
    ]
    for copy in [load_misc] + load_factor + later:
        copy.start()
    load_misc.wait()
    columns = [natural(core, d, first) for d in range(SIDE)]
    mine = [natural(core, second, lax.rem(first + SIDE - k, SIDE)) for k in range(SIDE)]
    parts = []
    for d in range(SIDE):
        held = misc[d, : 2 * ROWS, :]
        parts.append(jnp.concatenate([held[:, :256], held[:, 256:]], axis=0))
    z0 = in_order(core, parts)
    z0_tip = misc[:, 2 * ROWS : 3 * ROWS, :].reshape(256, HALF)
    eye = lax.broadcasted_iota(jnp.int32, (ROWS, ROWS), 0)
    eye = jnp.where(eye == lax.broadcasted_iota(jnp.int32, (ROWS, ROWS), 1), 1.0, 0.0)
    weights = []
    for block in range(2):
        column = []
        for d in range(SIDE):
            held = misc[d, 3 * ROWS :, :].astype(F32)
            held = held[block : block + 1] + held[block + 2 : block + 3] + held[block + 4 : block + 5]
            column.append(jnp.sum(eye * held[:, :ROWS], axis=1, keepdims=True))
        weights.append(jnp.concatenate(column, axis=0))
    for copy in load_factor:
        copy.wait()
    have = Gathered(factor)
    u, u_tip = have.past(z0)
    u_tip = u_tip - z0_tip.astype(F32)
    u_mine = jnp.zeros((256, 256), F32)
    z1_mine = []
    for h in range(2):
        low = jnp.concatenate([factor[b, h * ROWS : (h + 1) * ROWS, :] for b in mine], axis=0)
        u_mine += dot_t(z0[:, h * HALF : (h + 1) * HALF], low)
    z1 = jnp.concatenate([columns_t(factor, 0, c) for c in columns], axis=0)
    z1_mine = jnp.concatenate([columns_t(factor, 0, c, mine) for c in columns], axis=0)
    z1_tip = jnp.concatenate([factor[c, 2 * ROWS :, :] for c in columns], axis=0)
    for copy in later:
        copy.wait()
    rows_in = jnp.concatenate([u.astype(BF), z1], axis=0)
    tip_in = jnp.concatenate([u_tip.astype(BF), z1_tip], axis=0)
    held = state[...].reshape(SIDE, PART, HALF)
    held = [held[:, h * ROWS : (h + 1) * ROWS, :].reshape(256, HALF) for h in range(3)]
    through = dot_t(rows_in[:, :HALF], held[0]) + dot_t(rows_in[:, HALF:], held[1])
    through += 2.0 * dot_t(tip_in, held[2])
    carried = jnp.zeros((256, 256), F32)
    for h in range(2):
        part = inverse[:, h * ROWS : (h + 1) * ROWS, :].reshape(256, HALF)
        carried += dot_t(z0[:, h * HALF : (h + 1) * HALF], part)
    own_parts = parts[0]
    for d in range(1, SIDE):
        own_parts = jnp.where(second == d, parts[d], own_parts)
    traced = (u_mine * through[:256] + own_parts.astype(F32) * carried) * weights[0]
    traced += z1_mine.astype(F32) * through[256:] * weights[1]
    own_tip = u_tip[:ROWS]
    for d in range(1, SIDE):
        own_tip = jnp.where(second == d, u_tip[d * ROWS : (d + 1) * ROWS], own_tip)
    both = jnp.concatenate([own_tip.astype(BF), arrow[1]], axis=0)
    tip_traced = both.astype(F32) * dot(both, q[...])
    at = lax.broadcasted_iota(jnp.int32, (ROWS, BLOCK), 0) + row * ROWS
    on_diagonal = lax.broadcasted_iota(jnp.int32, (ROWS, BLOCK), 1) == at
    total = sum_all(traced)
    for block in range(2):
        total += sum_all(tip_traced[block * ROWS : (block + 1) * ROWS] * weight_ref[block])
        own = jnp.where(on_diagonal, x[block].astype(F32), 0.0)
        total += sum_all(own * weight_ref[block])
    slope[...] = jnp.full(slope.shape, total, F32)


def z0_own(misc, second, core):
    rows = pl.ds(pl.multiple_of(lax.rem(second, 2) * ROWS, ROWS), ROWS)
    lanes = pl.ds(pl.multiple_of(lax.div(second, 2) * 256, 256), 256)
    return in_order(core, [misc[d, rows, lanes] for d in range(SIDE)])


def sum_kernel(parts, after, out):
    del after
    out[...] = jnp.broadcast_to(jnp.sum(parts[...], axis=0)[None], out.shape)


def own_kernel(
    got,
    begun,
    arrow_ref,
    lower_ref,
    rows_ref,
    rows_tip_ref,
    factor,
    misc,
    own,
    arrow,
    lower,
    rows,
    rows_tip,
    sem_factor,
    sem_in,
    sem_out,
):
    core, row, _ = place()
    second = jnp.where(core == 0, lax.axis_index("y"), lax.axis_index("x"))
    loads = [
        pltpu.make_async_copy(got.at[:, pl.ds(PANEL, MISC)], misc, sem_in.at[0]),
        pltpu.make_async_copy(arrow_ref, arrow, sem_in.at[1]),
        pltpu.make_async_copy(begun.at[pl.ds(0, PART)], own, sem_in.at[2]),
    ] + load_exchanged(got, factor, sem_factor)
    for copy in loads:
        copy.start()
    for copy in loads:
        copy.wait()
    have = Gathered(factor)
    u, u_tip = have.past(z0_own(misc, second, core))
    uh, ul = split(u)
    uh_tip, ul_tip = split(u_tip - arrow[0].astype(F32))
    rows[...] = jnp.concatenate([columns_t(factor, 0, row), uh, ul], axis=0)
    rows_tip[...] = jnp.concatenate([arrow[1], uh_tip, ul_tip], axis=0)
    stores = [
        pltpu.make_async_copy(rows, rows_ref, sem_out.at[0]),
        pltpu.make_async_copy(rows_tip, rows_tip_ref, sem_out.at[1]),
    ]
    for copy in stores:
        copy.start()
    own_rows = jnp.concatenate([own[:ROWS], own[ROWS : 2 * ROWS]], axis=1)
    lower[...] = -have.times_factor(own_rows, own[2 * ROWS :])
    stores.append(pltpu.make_async_copy(lower, lower_ref, sem_out.at[2]))
    stores[-1].start()
    for copy in stores:
        copy.wait()


def first_kernel(
    got,
    begun0,
    begun1,
    begun2,
    begun3,
    x_ref,
    q_ref,
    own_ref,
    own_tip_ref,
    diag_ref,
    tip_ref,
    rows_ref,
    rows_tip_ref,
    factor,
    state,
    shares,
    x,
    q,
    own,
    own_tip,
    diag,
    tip,
    rows,
    rows_tip,
    sem_factor,
    sem_state,
    sem_share,
    sem_in,
    sem_out,
):
    core, _, first = place()
    second = jnp.where(core == 0, lax.axis_index("y"), lax.axis_index("x"))
    loads_state = [
        pltpu.make_async_copy(own_ref, own, sem_in.at[0]),
        pltpu.make_async_copy(own_tip_ref, own_tip, sem_in.at[1]),
        pltpu.make_async_copy(q_ref, q, sem_in.at[2]),
    ]
    loads = load_exchanged(got, factor, sem_factor)
    loads.append(pltpu.make_async_copy(x_ref.at[1], x, sem_in.at[3]))
    for k, begun in enumerate((begun0, begun1, begun2, begun3)):
        loads.append(
            pltpu.make_async_copy(begun.at[pl.ds(PANEL, SHARE)], shares.at[k], sem_share.at[k])
        )
        source = lax.rem(second + SIDE - k, SIDE)
        for j in range(SIDE):
            behind = lax.rem(first + SIDE - j, SIDE)
            loads_state.append(
                pltpu.make_async_copy(
                    begun.at[pl.ds(j * PART, PART)],
                    state.at[natural(core, source, behind)],
                    sem_state.at[k * SIDE + j],
                )
            )
    for copy in loads_state + loads:
        copy.start()
    for copy in loads_state:
        copy.wait()
    begun = Gathered(state)
    top = begun.times_factor(own[...], own_tip[...])
    bottom = begun.over_rows(own[...], 2) + dot(own_tip[...], q[...])
    p1, a = top[:64], top[64:128] + top[128:]
    p1_tip, a_tip = bottom[:64], bottom[64:128] + bottom[128:]
    tip[1] = -p1_tip
    tip[0] = a_tip
    p1h, p1l = split(p1)
    ah, al = split(a)
    p1h_tip, p1l_tip = split(p1_tip)
    ah_tip, al_tip = split(a_tip)
    rows_tip[...] = jnp.concatenate([-ah_tip, -al_tip, -p1h_tip], axis=0)
    stores = [
        pltpu.make_async_copy(tip, tip_ref, sem_out.at[0]),
        pltpu.make_async_copy(rows_tip, rows_tip_ref, sem_out.at[1]),
    ]
    for copy in stores:
        copy.start()
    for copy in loads:
        copy.wait()
    out = Gathered(factor).times_factor(
        jnp.concatenate([p1h, p1l, ah, al], axis=0),
        jnp.concatenate([p1h_tip, p1l_tip, ah_tip, al_tip], axis=0),
    )
    sigma1 = x[...].astype(F32) + out[:64] + out[64:128]
    diag[...] = sigma1
    carried = shares[0].astype(F32)
    for d in range(1, SIDE):
        carried += shares[d].astype(F32)
    carried = jnp.concatenate([carried[:ROWS], carried[ROWS:]], axis=1)
    p0h, p0l = split(carried + out[128:192] + out[192:])
    rows[...] = jnp.concatenate([p0h, p0l, sigma1.astype(BF)], axis=0)
    here = [
        pltpu.make_async_copy(diag, diag_ref, sem_out.at[2]),
        pltpu.make_async_copy(rows, rows_ref, sem_out.at[3]),
    ]
    for copy in here:
        copy.start()
    for copy in stores + here:
        copy.wait()


def last_kernel(
    late0,
    late1,
    late2,
    late3,
    x_ref,
    diag1_ref,
    lower1_ref,
    rows_ref,
    rows_tip_ref,
    diag_ref,
    lower_ref,
    factor,
    x,
    diag,
    lower,
    rows,
    rows_tip,
    sem_factor,
    sem_in,
    sem_out,
):
    core, _, first = place()
    second = jnp.where(core == 0, lax.axis_index("y"), lax.axis_index("x"))
    loads = [
        pltpu.make_async_copy(diag1_ref, diag.at[1], sem_in.at[0]),
        pltpu.make_async_copy(rows_ref, rows, sem_in.at[1]),
        pltpu.make_async_copy(rows_tip_ref, rows_tip, sem_in.at[2]),
        pltpu.make_async_copy(x_ref.at[0], x, sem_in.at[3]),
    ]
    load_lower = pltpu.make_async_copy(lower1_ref, lower.at[1], sem_in.at[4])
    loads0 = []
    for k, (late, at) in enumerate(((late0, 0), (late1, 0), (late2, LATER), (late3, 0))):
        source = lax.rem(second + SIDE - k, SIDE)
        loads0 += [
            pltpu.make_async_copy(
                late.at[pl.ds(at + j * PART, PART)],
                factor.at[natural(core, source, j)],
                sem_factor.at[k * SIDE + j],
            )
            for j in range(SIDE)
        ]
    for copy in loads + loads0 + [load_lower]:
        copy.start()
    for copy in loads:
        copy.wait()
    load_lower.wait()
    stores = [
        pltpu.make_async_copy(diag.at[1], diag_ref.at[1], sem_out.at[0]),
        pltpu.make_async_copy(lower.at[1], lower_ref.at[1], sem_out.at[1]),
    ]
    for copy in stores:
        copy.start()
    for copy in loads0:
        copy.wait()
    out = Gathered(factor).times_factor(rows[...], rows_tip[...])
    lower[0] = -out[128:]
    diag[0] = x[...].astype(F32) + out[:64] + out[64:128]
    here = [
        pltpu.make_async_copy(diag.at[0], diag_ref.at[0], sem_out.at[2]),
        pltpu.make_async_copy(lower.at[0], lower_ref.at[0], sem_out.at[3]),
    ]
    for copy in here:
        copy.start()
    for copy in stores + here:
        copy.wait()


def on_device(
    lower_factor,
    arrow_factor,
    block_inverse,
    boundary_sigma,
    boundary_tip,
    tip_inverse,
    slope_weights,
    partitions,
):
    slow = pl.BlockSpec(memory_space=pltpu.HBM)
    fast = pl.BlockSpec(memory_space=pltpu.VMEM)
    params = pltpu.CompilerParams(vmem_limit_bytes=VMEM_BYTES)
    rows, start = pl.pallas_call(
        pack_kernel,
        out_shape=(
            jax.ShapeDtypeStruct((SIDE, SENT, HALF), BF),
            jax.ShapeDtypeStruct((ROWS, BLOCK + HALF), BF),
        ),
        in_specs=[slow] * 5,
        out_specs=(slow,) * 2,
        scratch_shapes=[
            pltpu.VMEM((SENT, HALF), BF),
            pltpu.VMEM((ROWS, BLOCK + HALF), BF),
            pltpu.SemaphoreType.DMA((8,)),
            pltpu.SemaphoreType.DMA((2,)),
            pltpu.SemaphoreType.DMA((2 * SIDE + 1,)),
        ],
        compiler_params=params,
        cost_estimate=cost(4),
    )(lower_factor, arrow_factor, block_inverse, boundary_sigma, boundary_tip)
    got = exchange(rows, line_groups(partitions, 0))
    starts = [lax.ppermute(start, EVERY, state_shift(partitions, k)) for k in range(SIDE)]
    sent = pl.pallas_call(
        panel_kernel,
        out_shape=jax.ShapeDtypeStruct((SIDE, PANEL + MISC, HALF), BF),
        in_specs=[slow, slow, fast] + [slow] * SIDE,
        out_specs=slow,
        scratch_shapes=[
            pltpu.VMEM((SIDE, 5 * ROWS, HALF), BF),
            pltpu.VMEM((MISC, HALF), BF),
            pltpu.SemaphoreType.DMA((SIDE + 1,)),
            pltpu.SemaphoreType.DMA((SIDE * (SIDE + 1),)),
        ],
        compiler_params=params,
        cost_estimate=cost(12),
    )(got, arrow_factor, slope_weights, *starts)
    short = jax.ShapeDtypeStruct((LATER, HALF), BF)
    long = jax.ShapeDtypeStruct((LATER + PANEL, HALF), BF)
    *begun, late = pl.pallas_call(
        later_kernel,
        out_shape=(short, short, long, short, jax.ShapeDtypeStruct((PANEL, HALF), BF)),
        in_specs=[slow] * 5,
        out_specs=(slow,) * 5,
        scratch_shapes=[
            pltpu.VMEM((SIDE, SENT - PART, HALF), BF),
            pltpu.VMEM((PANEL, HALF), BF),
            pltpu.VMEM((SIDE, SHARE, HALF), BF),
            pltpu.SemaphoreType.DMA((SIDE,)),
            pltpu.SemaphoreType.DMA((3 * SIDE,)),
            pltpu.SemaphoreType.DMA((16,)),
        ],
        compiler_params=params,
        cost_estimate=cost(12),
    )(got, *starts)
    early = exchange(sent, line_groups(partitions, 1))
    shifts = [line_shift(partitions, k) for k in range(SIDE)]
    begun[1:] = [lax.ppermute(begun[k], EVERY, shifts[k]) for k in range(1, SIDE)]
    lates = [lax.ppermute(late, EVERY, shifts[k]) for k in (1, 3)]
    lates = [late, lates[0], begun[2], lates[1]]
    slope = pl.pallas_call(
        trace_kernel,
        out_shape=jax.ShapeDtypeStruct((partitions // 2, 8, 128), F32),
        in_specs=[slow] * 6 + [fast],
        out_specs=fast,
        scratch_shapes=[
            pltpu.VMEM((16, PART, HALF), BF),
            pltpu.VMEM((SIDE, MISC, HALF), BF),
            pltpu.VMEM((PANEL, HALF), BF),
            pltpu.VMEM((SIDE, 2 * ROWS, HALF), BF),
            pltpu.VMEM((2, ROWS, HALF), BF),
            pltpu.VMEM((2, ROWS, BLOCK), BF),
            pltpu.VMEM((HALF, HALF), BF),
            pltpu.SemaphoreType.DMA((16,)),
            pltpu.SemaphoreType.DMA((6,)),
        ],
        compiler_params=params,
        cost_estimate=cost(20),
    )(early, begun[0], got, arrow_factor, block_inverse, tip_inverse, slope_weights[:, :, None])
    total = exchange(slope, height_groups(partitions))
    outputs = (
        jax.ShapeDtypeStruct((ROWS, BLOCK), F32),
        jax.ShapeDtypeStruct((3 * ROWS, BLOCK), BF),
        jax.ShapeDtypeStruct((3 * ROWS, HALF), BF),
    )
    lower1, own, own_tip = pl.pallas_call(
        own_kernel,
        out_shape=outputs,
        in_specs=[slow] * 3,
        out_specs=(slow,) * 3,
        scratch_shapes=[
            pltpu.VMEM((16, PART, HALF), BF),
            pltpu.VMEM((SIDE, MISC, HALF), BF),
            pltpu.VMEM((PART, HALF), BF),
            pltpu.VMEM((2, ROWS, HALF), BF),
        ]
        + [pltpu.VMEM(leaf.shape, leaf.dtype) for leaf in outputs]
        + [
            pltpu.SemaphoreType.DMA((16,)),
            pltpu.SemaphoreType.DMA((3,)),
            pltpu.SemaphoreType.DMA((3,)),
        ],
        compiler_params=params,
        cost_estimate=cost(15),
    )(early, begun[0], arrow_factor)
    outputs = (
        jax.ShapeDtypeStruct((ROWS, BLOCK), F32),
        jax.ShapeDtypeStruct((2, ROWS, HALF), F32),
        jax.ShapeDtypeStruct((3 * ROWS, BLOCK), BF),
        jax.ShapeDtypeStruct((3 * ROWS, HALF), BF),
    )
    diag1, tip, rows, rows_tip = pl.pallas_call(
        first_kernel,
        out_shape=outputs,
        in_specs=[slow] * 9,
        out_specs=(slow,) * 4,
        scratch_shapes=[
            pltpu.VMEM((16, PART, HALF), BF),
            pltpu.VMEM((16, PART, HALF), BF),
            pltpu.VMEM((SIDE, SHARE, HALF), BF),
            pltpu.VMEM((ROWS, BLOCK), BF),
            pltpu.VMEM((HALF, HALF), BF),
            pltpu.VMEM((3 * ROWS, BLOCK), BF),
            pltpu.VMEM((3 * ROWS, HALF), BF),
        ]
        + [pltpu.VMEM(leaf.shape, leaf.dtype) for leaf in outputs]
        + [
            pltpu.SemaphoreType.DMA((16,)),
            pltpu.SemaphoreType.DMA((16,)),
            pltpu.SemaphoreType.DMA((SIDE,)),
            pltpu.SemaphoreType.DMA((4,)),
            pltpu.SemaphoreType.DMA((4,)),
        ],
        compiler_params=params,
        cost_estimate=cost(25),
    )(early, *begun, block_inverse, tip_inverse, own, own_tip)
    total = pl.pallas_call(
        sum_kernel,
        out_shape=jax.ShapeDtypeStruct((2 * SIDE * SIDE, 8, 128), F32),
        in_specs=[fast, slow],
        out_specs=fast,
        compiler_params=params,
        cost_estimate=cost(1),
    )(total, rows_tip)
    total = jnp.sum(exchange(total, plane_groups(partitions)), axis=0)
    outputs = (
        jax.ShapeDtypeStruct((2, ROWS, BLOCK), F32),
        jax.ShapeDtypeStruct((2, ROWS, BLOCK), F32),
    )
    diag, lower = pl.pallas_call(
        last_kernel,
        out_shape=outputs,
        in_specs=[slow] * 9,
        out_specs=(slow,) * 2,
        scratch_shapes=[
            pltpu.VMEM((16, PART, HALF), BF),
            pltpu.VMEM((ROWS, BLOCK), BF),
            pltpu.VMEM((2, ROWS, BLOCK), F32),
            pltpu.VMEM((2, ROWS, BLOCK), F32),
            pltpu.VMEM((3 * ROWS, BLOCK), BF),
            pltpu.VMEM((3 * ROWS, HALF), BF),
            pltpu.SemaphoreType.DMA((16,)),
            pltpu.SemaphoreType.DMA((5,)),
            pltpu.SemaphoreType.DMA((4,)),
        ],
        compiler_params=params,
        cost_estimate=cost(15),
    )(*lates, block_inverse, diag1, lower1, rows, rows_tip)
    return diag, lower, tip, total[0, 0]


def solution(mesh):
    partitions = mesh.shape["tm"]
    fine = Mesh(mesh.devices.reshape(partitions, SIDE, SIDE), EVERY)
    rows = P("tm", ("y", "x"), None)

    def program(*args):
        return on_device(*args, partitions=partitions)

    return jax.shard_map(
        program,
        mesh=fine,
        in_specs=(rows, rows, rows, rows, rows, P(), P("tm", ("y", "x"))),
        out_specs=(rows, rows, rows, P()),
        check_vma=False,
    )
```

```python
import jax
import jax.numpy as jnp
from jax import lax
from jax.experimental import pallas as pl
from jax.experimental.pallas import tpu as pltpu
from jax.sharding import Mesh, PartitionSpec as P

SIDE = 4
ROWS = 64
HALF = 512
BLOCK = 1024
BF = jnp.bfloat16
F32 = jnp.float32
EVERY = ("tm", "y", "x")

L1, M1, L0, M0, X1 = 0, 2, 3, 5, 6
PART = 3 * ROWS
SENT = 8 * ROWS
SHARE = 2 * ROWS
PANEL = SIDE * PART
MISC = 2 * ROWS + ROWS + 16
WIDE = BLOCK + HALF
LATER = PANEL + SHARE
VMEM_BYTES = 127 * 512 * 1024


def line_groups(partitions, phase):
    groups = []
    for t in range(partitions):
        base = t * SIDE * SIDE
        for i in range(SIDE):
            if (t + phase) % 2 == 0:
                groups.append([base + SIDE * i + x for x in range(SIDE)])
            else:
                groups.append([base + SIDE * y + i for y in range(SIDE)])
    return groups


def plane_groups(partitions):
    plane = 2 * SIDE * SIDE
    return [[z * plane + r for r in range(plane)] for z in range(partitions // 2)]


def height_groups(partitions):
    plane = SIDE * SIDE
    return [
        [t * plane + r for t in range(core, partitions, 2)]
        for core in range(2)
        for r in range(plane)
    ]


def state_shift(partitions, steps):
    pairs = []
    for t in range(partitions - 1):
        for y in range(SIDE):
            for x in range(SIDE):
                to = (y, (x + steps) % SIDE) if t % 2 == 0 else ((y + steps) % SIDE, x)
                source = (t + 1) * SIDE * SIDE + SIDE * y + x
                pairs.append((source, t * SIDE * SIDE + SIDE * to[0] + to[1]))
    return pairs


def line_shift(partitions, steps):
    pairs = []
    for t in range(partitions):
        for y in range(SIDE):
            for x in range(SIDE):
                to = ((y + steps) % SIDE, x) if t % 2 == 0 else (y, (x + steps) % SIDE)
                base = t * SIDE * SIDE
                pairs.append((base + SIDE * y + x, base + SIDE * to[0] + to[1]))
    return pairs


def cost(megabytes):
    return pl.CostEstimate(flops=0, bytes_accessed=megabytes * 1_000_000, transcendentals=0)


def exchange(value, groups):
    return lax.all_to_all(value, EVERY, 0, 0, tiled=True, axis_index_groups=groups)


def dot(left, right):
    return jnp.dot(left, right, preferred_element_type=F32)


def dot_t(left, right):
    return lax.dot_general(left, right, (((1,), (1,)), ((), ())), preferred_element_type=F32)


def split(value):
    high = value.astype(BF)
    return high, (value - high.astype(F32)).astype(BF)


def place():
    core = lax.rem(lax.axis_index("tm"), 2)
    y, x = lax.axis_index("y"), lax.axis_index("x")
    first = jnp.where(core == 0, x, y)
    return core, y * SIDE + x, first


def natural(core, second, first):
    return jnp.where(core == 0, SIDE * second + first, SIDE * first + second)


def columns_t(ref, piece, row, blocks=None):
    half = lax.div(row, 8)
    lane = lax.div(lax.rem(row, 8), 2)
    rows = pl.ds(pl.multiple_of((piece + half) * ROWS, ROWS), ROWS)
    lanes = pl.ds(pl.multiple_of(lane * 128, 128), 128)
    if blocks is None:
        window = ref[:, rows, lanes]
        window = window.reshape(window.shape[0] * ROWS, 128)
    else:
        window = jnp.concatenate([ref[b, rows, lanes] for b in blocks], axis=0)
    want = lax.broadcasted_iota(jnp.int32, (ROWS, 128), 0) + lax.rem(row, 2) * ROWS
    pick = jnp.where(lax.broadcasted_iota(jnp.int32, (ROWS, 128), 1) == want, 1.0, 0.0)
    return dot_t(pick.astype(BF), window).astype(BF)


def pack_kernel(low, arrow, inverse, sigma, tip, out, start, held, own, sem_in, sem_own, sem_out):
    loads = []
    for k, (ref, j, h) in enumerate(
        [(low, 1, 0), (low, 1, 1), (arrow, 1, 0), (low, 0, 0), (low, 0, 1), (arrow, 0, 0)]
        + [(inverse, 1, 0), (inverse, 1, 1)]
    ):
        loads.append(
            pltpu.make_async_copy(
                ref.at[j, :, pl.ds(h * HALF, HALF)],
                held.at[pl.ds(k * ROWS, ROWS)],
                sem_in.at[k],
            )
        )
    loads_own = [
        pltpu.make_async_copy(sigma.at[0], own.at[:, pl.ds(0, BLOCK)], sem_own.at[0]),
        pltpu.make_async_copy(tip.at[0], own.at[:, pl.ds(BLOCK, HALF)], sem_own.at[1]),
    ]
    for copy in loads + loads_own:
        copy.start()
    stores = []
    for h in range(2):
        for copy in loads[4 * h : 4 * h + 4]:
            copy.wait()
        rows = pl.ds(h * SENT // 2, SENT // 2)
        here = [
            pltpu.make_async_copy(held.at[rows], out.at[d, rows], sem_out.at[d * 2 + h])
            for d in range(SIDE)
        ]
        for copy in here:
            copy.start()
        stores += here
    for copy in loads_own:
        copy.wait()
    stores.append(pltpu.make_async_copy(own, start, sem_out.at[2 * SIDE]))
    stores[-1].start()
    for copy in stores:
        copy.wait()


def panel_kernel(
    got, arrow, weight, own0, own1, own2, own3, out, panel, misc, sem_in, sem_out
):
    del own0, own1, own2, own3
    core, _, first = place()
    loads = [
        pltpu.make_async_copy(got.at[j, pl.ds(0, 5 * ROWS)], panel.at[j], sem_in.at[j])
        for j in range(SIDE)
    ]
    load_arrow = pltpu.make_async_copy(
        arrow.at[0], misc.at[pl.ds(2 * ROWS, ROWS)], sem_in.at[SIDE]
    )
    for copy in loads + [load_arrow]:
        copy.start()
    stores = []
    for j in range(SIDE):
        loads[j].wait()
        here = [
            pltpu.make_async_copy(
                panel.at[j, pl.ds(0, PART)],
                out.at[d, pl.ds(j * PART, PART)],
                sem_out.at[d * (SIDE + 1) + j],
            )
            for d in range(SIDE)
        ]
        for copy in here:
            copy.start()
        stores += here
    cols = [columns_t(panel, L0, natural(core, d, first)) for d in range(SIDE)]
    cols = jnp.concatenate(cols, axis=0)
    misc[: 2 * ROWS, :] = jnp.concatenate([cols[: 2 * ROWS], cols[2 * ROWS :]], axis=1)
    rest = weight[...]
    parts = []
    for _ in range(3):
        parts.append(rest.astype(BF).astype(F32))
        rest = rest - parts[-1]
    parts = jnp.concatenate(parts + [jnp.zeros((10, ROWS), F32)], axis=0)
    parts = jnp.concatenate([parts, jnp.zeros((16, HALF - ROWS), F32)], axis=1)
    misc[3 * ROWS :, :] = parts.astype(BF)
    load_arrow.wait()
    here = [
        pltpu.make_async_copy(misc, out.at[d, pl.ds(PANEL, MISC)], sem_out.at[d * (SIDE + 1) + SIDE])
        for d in range(SIDE)
    ]
    for copy in here:
        copy.start()
    for copy in stores + here:
        copy.wait()


def later_kernel(
    got,
    own0,
    own1,
    own2,
    own3,
    late0,
    late1,
    late2,
    late3,
    panel,
    state,
    share,
    sem_in,
    sem_out,
    sem_state,
):
    core, _, first = place()
    second = jnp.where(core == 0, lax.axis_index("y"), lax.axis_index("x"))
    lates = (late0, late1, late2, late3)
    loads = [
        pltpu.make_async_copy(got.at[j, pl.ds(PART, SENT - PART)], panel.at[j], sem_in.at[j])
        for j in range(SIDE)
    ]
    loads_state = [
        pltpu.make_async_copy(
            own.at[:, pl.ds(h * HALF, HALF)],
            state.at[pl.ds(k * PART + h * ROWS, ROWS)],
            sem_state.at[k * 3 + h],
        )
        for k, own in enumerate((own0, own1, own2, own3))
        for h in range(3)
    ]
    for copy in loads + loads_state:
        copy.start()
    for copy in loads + loads_state:
        copy.wait()
    stores = []
    for k, late in enumerate(lates):
        stores += [
            pltpu.make_async_copy(
                panel.at[j, pl.ds(0, PART)],
                late.at[pl.ds(j * PART, PART)],
                sem_out.at[k * (SIDE + 1) + j],
            )
            for j in range(SIDE)
        ]
        stores.append(
            pltpu.make_async_copy(state, late.at[pl.ds(LATER, PANEL)], sem_state.at[12 + k])
        )
    for copy in stores:
        copy.start()
    cols = [columns_t(panel, 0, natural(core, d, first)) for d in range(SIDE)]
    cols = jnp.concatenate(cols, axis=0)
    for h in range(2):
        at = PART + h * ROWS
        part = dot(cols, panel[:, at : at + ROWS, :].reshape(SIDE * ROWS, HALF))
        for d in range(SIDE):
            share[d, h * ROWS : (h + 1) * ROWS, :] = part[d * ROWS : (d + 1) * ROWS].astype(BF)
    here = [
        pltpu.make_async_copy(
            share.at[lax.rem(second + k, SIDE)],
            late.at[pl.ds(PANEL, SHARE)],
            sem_out.at[k * (SIDE + 1) + SIDE],
        )
        for k, late in enumerate(lates)
    ]
    for copy in here:
        copy.start()
    for copy in stores + here:
        copy.wait()


class Gathered:
    def __init__(self, mat):
        self.mat = mat

    def piece(self, k):
        return self.mat[:, k * ROWS : (k + 1) * ROWS, :].reshape(BLOCK, HALF)

    def over_rows(self, left, k):
        return dot(left, self.piece(k))

    def over_columns(self, left, k):
        return dot_t(left, self.piece(k))

    def times_factor(self, left_rows, left_tip):
        both = jnp.concatenate([self.over_rows(left_rows, h) for h in range(2)], axis=1)
        return both + self.over_columns(left_tip, 2)

    def past(self, left):
        u = self.over_columns(left[:, :HALF], 0) + self.over_columns(left[:, HALF:], 1)
        return u, self.over_rows(left, 2)


def load_exchanged(got, mat, sem):
    core, _, _ = place()
    return [
        pltpu.make_async_copy(
            got.at[d, pl.ds(j * PART, PART)],
            mat.at[natural(core, d, j)],
            sem.at[d * SIDE + j],
        )
        for d in range(SIDE)
        for j in range(SIDE)
    ]


def in_order(core, parts):
    even = jnp.concatenate(parts, axis=1)
    odd = [parts[d][:, j * 64 : (j + 1) * 64] for j in range(SIDE) for d in range(SIDE)]
    return jnp.where(core == 0, even, jnp.concatenate(odd, axis=1))


def sum_all(value):
    return jnp.sum(jnp.sum(value, axis=1, keepdims=True))


def trace_kernel(
    got,
    begun,
    panel_ref,
    arrow_ref,
    x_ref,
    q_ref,
    weight_ref,
    slope,
    factor,
    misc,
    state,
    inverse,
    arrow,
    x,
    q,
    sem_factor,
    sem_in,
):
    core, row, first = place()
    second = jnp.where(core == 0, lax.axis_index("y"), lax.axis_index("x"))
    load_misc = pltpu.make_async_copy(got.at[:, pl.ds(PANEL, MISC)], misc, sem_in.at[0])
    load_factor = load_exchanged(got, factor, sem_factor)
    later = [
        pltpu.make_async_copy(begun.at[pl.ds(LATER, PANEL)], state, sem_in.at[1]),
        pltpu.make_async_copy(
            panel_ref.at[:, pl.ds(X1 * ROWS, 2 * ROWS)], inverse, sem_in.at[2]
        ),
        pltpu.make_async_copy(arrow_ref, arrow, sem_in.at[3]),
        pltpu.make_async_copy(q_ref, q, sem_in.at[4]),
        pltpu.make_async_copy(x_ref, x, sem_in.at[5]),
    ]
    for copy in [load_misc] + load_factor + later:
        copy.start()
    load_misc.wait()
    columns = [natural(core, d, first) for d in range(SIDE)]
    mine = [natural(core, second, lax.rem(first + SIDE - k, SIDE)) for k in range(SIDE)]
    parts = []
    for d in range(SIDE):
        held = misc[d, : 2 * ROWS, :]
        parts.append(jnp.concatenate([held[:, :256], held[:, 256:]], axis=0))
    z0 = in_order(core, parts)
    z0_tip = misc[:, 2 * ROWS : 3 * ROWS, :].reshape(256, HALF)
    eye = lax.broadcasted_iota(jnp.int32, (ROWS, ROWS), 0)
    eye = jnp.where(eye == lax.broadcasted_iota(jnp.int32, (ROWS, ROWS), 1), 1.0, 0.0)
    weights = []
    for block in range(2):
        column = []
        for d in range(SIDE):
            held = misc[d, 3 * ROWS :, :].astype(F32)
            held = held[block : block + 1] + held[block + 2 : block + 3] + held[block + 4 : block + 5]
            column.append(jnp.sum(eye * held[:, :ROWS], axis=1, keepdims=True))
        weights.append(jnp.concatenate(column, axis=0))
    for copy in load_factor:
        copy.wait()
    have = Gathered(factor)
    u, u_tip = have.past(z0)
    u_tip = u_tip - z0_tip.astype(F32)
    u_mine = jnp.zeros((256, 256), F32)
    z1_mine = []
    for h in range(2):
        low = jnp.concatenate([factor[b, h * ROWS : (h + 1) * ROWS, :] for b in mine], axis=0)
        u_mine += dot_t(z0[:, h * HALF : (h + 1) * HALF], low)
    z1 = jnp.concatenate([columns_t(factor, 0, c) for c in columns], axis=0)
    z1_mine = jnp.concatenate([columns_t(factor, 0, c, mine) for c in columns], axis=0)
    z1_tip = jnp.concatenate([factor[c, 2 * ROWS :, :] for c in columns], axis=0)
    for copy in later:
        copy.wait()
    rows_in = jnp.concatenate([u.astype(BF), z1], axis=0)
    tip_in = jnp.concatenate([u_tip.astype(BF), z1_tip], axis=0)
    held = state[...].reshape(SIDE, PART, HALF)
    held = [held[:, h * ROWS : (h + 1) * ROWS, :].reshape(256, HALF) for h in range(3)]
    through = dot_t(rows_in[:, :HALF], held[0]) + dot_t(rows_in[:, HALF:], held[1])
    through += 2.0 * dot_t(tip_in, held[2])
    carried = jnp.zeros((256, 256), F32)
    for h in range(2):
        part = inverse[:, h * ROWS : (h + 1) * ROWS, :].reshape(256, HALF)
        carried += dot_t(z0[:, h * HALF : (h + 1) * HALF], part)
    own_parts = parts[0]
    for d in range(1, SIDE):
        own_parts = jnp.where(second == d, parts[d], own_parts)
    traced = (u_mine * through[:256] + own_parts.astype(F32) * carried) * weights[0]
    traced += z1_mine.astype(F32) * through[256:] * weights[1]
    own_tip = u_tip[:ROWS]
    for d in range(1, SIDE):
        own_tip = jnp.where(second == d, u_tip[d * ROWS : (d + 1) * ROWS], own_tip)
    both = jnp.concatenate([own_tip.astype(BF), arrow[1]], axis=0)
    tip_traced = both.astype(F32) * dot(both, q[...])
    at = lax.broadcasted_iota(jnp.int32, (ROWS, BLOCK), 0) + row * ROWS
    on_diagonal = lax.broadcasted_iota(jnp.int32, (ROWS, BLOCK), 1) == at
    total = sum_all(traced)
    for block in range(2):
        total += sum_all(tip_traced[block * ROWS : (block + 1) * ROWS] * weight_ref[block])
        own = jnp.where(on_diagonal, x[block].astype(F32), 0.0)
        total += sum_all(own * weight_ref[block])
    slope[...] = jnp.full(slope.shape, total, F32)


def z0_own(misc, second, core):
    rows = pl.ds(pl.multiple_of(lax.rem(second, 2) * ROWS, ROWS), ROWS)
    lanes = pl.ds(pl.multiple_of(lax.div(second, 2) * 256, 256), 256)
    return in_order(core, [misc[d, rows, lanes] for d in range(SIDE)])


def block_kernel(
    got,
    late0,
    late1,
    late2,
    late3,
    arrow_ref,
    x_ref,
    q_ref,
    diag_ref,
    lower_ref,
    tip_ref,
    factor1,
    factor0,
    state,
    shares,
    misc,
    arrow,
    x,
    q,
    diag,
    lower,
    tip,
    sem_factor1,
    sem_factor0,
    sem_state,
    sem_share,
    sem_in,
    sem_out,
):
    core, row, first = place()
    second = jnp.where(core == 0, lax.axis_index("y"), lax.axis_index("x"))
    loads1 = [
        pltpu.make_async_copy(got.at[:, pl.ds(PANEL, MISC)], misc, sem_in.at[0]),
        pltpu.make_async_copy(arrow_ref, arrow, sem_in.at[1]),
    ] + load_exchanged(got, factor1, sem_factor1)
    loads_state = [pltpu.make_async_copy(q_ref, q, sem_in.at[2])]
    loads0 = [pltpu.make_async_copy(x_ref, x, sem_in.at[3])]
    for k, late in enumerate((late0, late1, late2, late3)):
        source = lax.rem(second + SIDE - k, SIDE)
        for j in range(SIDE):
            behind = lax.rem(first + SIDE - j, SIDE)
            loads_state.append(
                pltpu.make_async_copy(
                    late.at[pl.ds(LATER + j * PART, PART)],
                    state.at[natural(core, source, behind)],
                    sem_state.at[k * SIDE + j],
                )
            )
            loads0.append(
                pltpu.make_async_copy(
                    late.at[pl.ds(j * PART, PART)],
                    factor0.at[natural(core, source, j)],
                    sem_factor0.at[k * SIDE + j],
                )
            )
        loads0.append(
            pltpu.make_async_copy(late.at[pl.ds(PANEL, SHARE)], shares.at[k], sem_share.at[k])
        )
    for copy in loads1 + loads_state + loads0:
        copy.start()
    for copy in loads1:
        copy.wait()
    have = Gathered(factor1)
    z1 = columns_t(factor1, 0, row)
    z1_tip, z0_tip = arrow[1], arrow[0]
    u, u_tip = have.past(z0_own(misc, second, core))
    u_tip = u_tip - z0_tip.astype(F32)
    uh, ul = split(u)
    uh_tip, ul_tip = split(u_tip)
    rows_in = jnp.concatenate([z1, uh, ul], axis=0)
    tip_in = jnp.concatenate([z1_tip, uh_tip, ul_tip], axis=0)
    for copy in loads_state:
        copy.wait()
    begun = Gathered(state)
    top = begun.times_factor(rows_in, tip_in)
    bottom = begun.over_rows(rows_in, 2) + dot(tip_in, q[...])
    p1, a = top[:64], top[64:128] + top[128:]
    p1_tip, a_tip = bottom[:64], bottom[64:128] + bottom[128:]
    tip[1] = -p1_tip
    tip[0] = a_tip
    stores = [pltpu.make_async_copy(tip, tip_ref, sem_out.at[0])]
    stores[0].start()
    p1h, p1l = split(p1)
    ah, al = split(a)
    p1h_tip, p1l_tip = split(p1_tip)
    ah_tip, al_tip = split(a_tip)
    own = [state[row, h * ROWS : (h + 1) * ROWS, :] for h in range(3)]
    own_rows = jnp.concatenate(own[:2], axis=1)
    out = have.times_factor(
        jnp.concatenate([p1h, p1l, ah, al, own_rows], axis=0),
        jnp.concatenate([p1h_tip, p1l_tip, ah_tip, al_tip, own[2]], axis=0),
    )
    for copy in loads0:
        copy.wait()
    lower[1] = -out[256:]
    sigma1 = x[1].astype(F32) + out[:64] + out[64:128]
    diag[1] = sigma1
    here = [
        pltpu.make_async_copy(diag.at[1], diag_ref.at[1], sem_out.at[1]),
        pltpu.make_async_copy(lower.at[1], lower_ref.at[1], sem_out.at[2]),
    ]
    for copy in here:
        copy.start()
    stores += here
    carried = shares[0].astype(F32)
    for d in range(1, SIDE):
        carried += shares[d].astype(F32)
    carried = jnp.concatenate([carried[:ROWS], carried[ROWS:]], axis=1)
    p0h, p0l = split(carried + out[128:192] + out[192:256])
    out = Gathered(factor0).times_factor(
        jnp.concatenate([p0h, p0l, sigma1.astype(BF)], axis=0),
        jnp.concatenate([-ah_tip, -al_tip, -p1h_tip], axis=0),
    )
    lower[0] = -out[128:]
    diag[0] = x[0].astype(F32) + out[:64] + out[64:128]
    here = [
        pltpu.make_async_copy(diag.at[0], diag_ref.at[0], sem_out.at[3]),
        pltpu.make_async_copy(lower.at[0], lower_ref.at[0], sem_out.at[4]),
    ]
    for copy in here:
        copy.start()
    for copy in stores + here:
        copy.wait()


def on_device(
    lower_factor,
    arrow_factor,
    block_inverse,
    boundary_sigma,
    boundary_tip,
    tip_inverse,
    slope_weights,
    partitions,
):
    slow = pl.BlockSpec(memory_space=pltpu.HBM)
    fast = pl.BlockSpec(memory_space=pltpu.VMEM)
    params = pltpu.CompilerParams(vmem_limit_bytes=VMEM_BYTES)
    rows, start = pl.pallas_call(
        pack_kernel,
        out_shape=(
            jax.ShapeDtypeStruct((SIDE, SENT, HALF), BF),
            jax.ShapeDtypeStruct((ROWS, BLOCK + HALF), BF),
        ),
        in_specs=[slow] * 5,
        out_specs=(slow,) * 2,
        scratch_shapes=[
            pltpu.VMEM((SENT, HALF), BF),
            pltpu.VMEM((ROWS, BLOCK + HALF), BF),
            pltpu.SemaphoreType.DMA((8,)),
            pltpu.SemaphoreType.DMA((2,)),
            pltpu.SemaphoreType.DMA((2 * SIDE + 1,)),
        ],
        compiler_params=params,
        cost_estimate=cost(4),
    )(lower_factor, arrow_factor, block_inverse, boundary_sigma, boundary_tip)
    got = exchange(rows, line_groups(partitions, 0))
    starts = [lax.ppermute(start, EVERY, state_shift(partitions, k)) for k in range(SIDE)]
    sent = pl.pallas_call(
        panel_kernel,
        out_shape=jax.ShapeDtypeStruct((SIDE, PANEL + MISC, HALF), BF),
        in_specs=[slow, slow, fast] + [slow] * SIDE,
        out_specs=slow,
        scratch_shapes=[
            pltpu.VMEM((SIDE, 5 * ROWS, HALF), BF),
            pltpu.VMEM((MISC, HALF), BF),
            pltpu.SemaphoreType.DMA((SIDE + 1,)),
            pltpu.SemaphoreType.DMA((SIDE * (SIDE + 1),)),
        ],
        compiler_params=params,
        cost_estimate=cost(12),
    )(got, arrow_factor, slope_weights, *starts)
    lates = pl.pallas_call(
        later_kernel,
        out_shape=(jax.ShapeDtypeStruct((LATER + PANEL, HALF), BF),) * SIDE,
        in_specs=[slow] * 5,
        out_specs=(slow,) * 4,
        scratch_shapes=[
            pltpu.VMEM((SIDE, SENT - PART, HALF), BF),
            pltpu.VMEM((PANEL, HALF), BF),
            pltpu.VMEM((SIDE, SHARE, HALF), BF),
            pltpu.SemaphoreType.DMA((SIDE,)),
            pltpu.SemaphoreType.DMA((SIDE * (SIDE + 1),)),
            pltpu.SemaphoreType.DMA((16,)),
        ],
        compiler_params=params,
        cost_estimate=cost(12),
    )(got, *starts)
    lates = list(lates)
    early = exchange(sent, line_groups(partitions, 1))
    for k in range(1, SIDE):
        lates[k] = lax.ppermute(lates[k], EVERY, line_shift(partitions, k))
    slope = pl.pallas_call(
        trace_kernel,
        out_shape=jax.ShapeDtypeStruct((partitions // 2, 8, 128), F32),
        in_specs=[slow] * 6 + [fast],
        out_specs=fast,
        scratch_shapes=[
            pltpu.VMEM((16, PART, HALF), BF),
            pltpu.VMEM((SIDE, MISC, HALF), BF),
            pltpu.VMEM((PANEL, HALF), BF),
            pltpu.VMEM((SIDE, 2 * ROWS, HALF), BF),
            pltpu.VMEM((2, ROWS, HALF), BF),
            pltpu.VMEM((2, ROWS, BLOCK), BF),
            pltpu.VMEM((HALF, HALF), BF),
            pltpu.SemaphoreType.DMA((16,)),
            pltpu.SemaphoreType.DMA((6,)),
        ],
        compiler_params=params,
        cost_estimate=cost(20),
    )(early, lates[0], got, arrow_factor, block_inverse, tip_inverse, slope_weights[:, :, None])
    total = jnp.sum(exchange(slope, height_groups(partitions)), axis=0)
    total = jnp.broadcast_to(total[None], (2 * SIDE * SIDE, 8, 128))
    total = jnp.sum(exchange(total, plane_groups(partitions)), axis=0)
    outputs = (
        jax.ShapeDtypeStruct((2, ROWS, BLOCK), F32),
        jax.ShapeDtypeStruct((2, ROWS, BLOCK), F32),
        jax.ShapeDtypeStruct((2, ROWS, HALF), F32),
    )
    diag, lower, tip = pl.pallas_call(
        block_kernel,
        out_shape=outputs,
        in_specs=[slow] * 8,
        out_specs=(slow,) * 3,
        scratch_shapes=[
            pltpu.VMEM((16, PART, HALF), BF),
            pltpu.VMEM((16, PART, HALF), BF),
            pltpu.VMEM((16, PART, HALF), BF),
            pltpu.VMEM((SIDE, SHARE, HALF), BF),
            pltpu.VMEM((SIDE, MISC, HALF), BF),
            pltpu.VMEM((2, ROWS, HALF), BF),
            pltpu.VMEM((2, ROWS, BLOCK), BF),
            pltpu.VMEM((HALF, HALF), BF),
        ]
        + [pltpu.VMEM(leaf.shape, F32) for leaf in outputs]
        + [
            pltpu.SemaphoreType.DMA((16,)),
            pltpu.SemaphoreType.DMA((16,)),
            pltpu.SemaphoreType.DMA((16,)),
            pltpu.SemaphoreType.DMA((SIDE,)),
            pltpu.SemaphoreType.DMA((4,)),
            pltpu.SemaphoreType.DMA((5,)),
        ],
        compiler_params=params,
        cost_estimate=cost(30),
    )(early, *lates, arrow_factor, block_inverse, tip_inverse)
    return diag, lower, tip, total[0, 0]


def solution(mesh):
    partitions = mesh.shape["tm"]
    fine = Mesh(mesh.devices.reshape(partitions, SIDE, SIDE), EVERY)
    rows = P("tm", ("y", "x"), None)

    def program(*args):
        return on_device(*args, partitions=partitions)

    return jax.shard_map(
        program,
        mesh=fine,
        in_specs=(rows, rows, rows, rows, rows, P(), P("tm", ("y", "x"))),
        out_specs=(rows, rows, rows, P()),
        check_vma=False,
    )
```

```python
import jax
import jax.numpy as jnp
from jax import lax
from jax.experimental import pallas as pl
from jax.experimental.pallas import tpu as pltpu
from jax.sharding import Mesh, PartitionSpec as P

SIDE = 4
ROWS = 64
HALF = 512
BLOCK = 1024
BF = jnp.bfloat16
F32 = jnp.float32
EVERY = ("tm", "y", "x")

L1, M1, L0, M0, X1 = 0, 2, 3, 5, 6
PART = 3 * ROWS
SENT = 8 * ROWS
SHARE = 2 * ROWS
PANEL = SIDE * PART
MISC = 2 * ROWS + ROWS + 16
WIDE = BLOCK + HALF
LATER = PANEL + SHARE
VMEM_BYTES = 127 * 512 * 1024


def line_groups(partitions, phase):
    groups = []
    for t in range(partitions):
        base = t * SIDE * SIDE
        for i in range(SIDE):
            if (t + phase) % 2 == 0:
                groups.append([base + SIDE * i + x for x in range(SIDE)])
            else:
                groups.append([base + SIDE * y + i for y in range(SIDE)])
    return groups


def plane_groups(partitions):
    plane = 2 * SIDE * SIDE
    return [[z * plane + r for r in range(plane)] for z in range(partitions // 2)]


def height_groups(partitions):
    plane = SIDE * SIDE
    return [
        [t * plane + r for t in range(core, partitions, 2)]
        for core in range(2)
        for r in range(plane)
    ]


def state_shift(partitions, steps):
    pairs = []
    for t in range(partitions - 1):
        for y in range(SIDE):
            for x in range(SIDE):
                to = (y, (x + steps) % SIDE) if t % 2 == 0 else ((y + steps) % SIDE, x)
                source = (t + 1) * SIDE * SIDE + SIDE * y + x
                pairs.append((source, t * SIDE * SIDE + SIDE * to[0] + to[1]))
    return pairs


def line_shift(partitions, steps):
    pairs = []
    for t in range(partitions):
        for y in range(SIDE):
            for x in range(SIDE):
                to = ((y + steps) % SIDE, x) if t % 2 == 0 else (y, (x + steps) % SIDE)
                base = t * SIDE * SIDE
                pairs.append((base + SIDE * y + x, base + SIDE * to[0] + to[1]))
    return pairs


def cost(megabytes):
    return pl.CostEstimate(flops=0, bytes_accessed=megabytes * 1_000_000, transcendentals=0)


def exchange(value, groups):
    return lax.all_to_all(value, EVERY, 0, 0, tiled=True, axis_index_groups=groups)


def dot(left, right):
    return jnp.dot(left, right, preferred_element_type=F32)


def dot_t(left, right):
    return lax.dot_general(left, right, (((1,), (1,)), ((), ())), preferred_element_type=F32)


def split(value):
    high = value.astype(BF)
    return high, (value - high.astype(F32)).astype(BF)


def place():
    core = lax.rem(lax.axis_index("tm"), 2)
    y, x = lax.axis_index("y"), lax.axis_index("x")
    first = jnp.where(core == 0, x, y)
    return core, y * SIDE + x, first


def natural(core, second, first):
    return jnp.where(core == 0, SIDE * second + first, SIDE * first + second)


def columns_t(ref, piece, row, blocks=None):
    half = lax.div(row, 8)
    lane = lax.div(lax.rem(row, 8), 2)
    rows = pl.ds(pl.multiple_of((piece + half) * ROWS, ROWS), ROWS)
    lanes = pl.ds(pl.multiple_of(lane * 128, 128), 128)
    if blocks is None:
        window = ref[:, rows, lanes]
        window = window.reshape(window.shape[0] * ROWS, 128)
    else:
        window = jnp.concatenate([ref[b, rows, lanes] for b in blocks], axis=0)
    want = lax.broadcasted_iota(jnp.int32, (ROWS, 128), 0) + lax.rem(row, 2) * ROWS
    pick = jnp.where(lax.broadcasted_iota(jnp.int32, (ROWS, 128), 1) == want, 1.0, 0.0)
    return dot_t(pick.astype(BF), window).astype(BF)


def pack_kernel(low, arrow, inverse, sigma, tip, out, start, held, own, sem_in, sem_own, sem_out):
    loads = []
    for k, (ref, j, h) in enumerate(
        [(low, 1, 0), (low, 1, 1), (arrow, 1, 0), (low, 0, 0), (low, 0, 1), (arrow, 0, 0)]
        + [(inverse, 1, 0), (inverse, 1, 1)]
    ):
        loads.append(
            pltpu.make_async_copy(
                ref.at[j, :, pl.ds(h * HALF, HALF)],
                held.at[pl.ds(k * ROWS, ROWS)],
                sem_in.at[k],
            )
        )
    loads_own = [
        pltpu.make_async_copy(sigma.at[0], own.at[:, pl.ds(0, BLOCK)], sem_own.at[0]),
        pltpu.make_async_copy(tip.at[0], own.at[:, pl.ds(BLOCK, HALF)], sem_own.at[1]),
    ]
    for copy in loads + loads_own:
        copy.start()
    stores = []
    for h in range(2):
        for copy in loads[4 * h : 4 * h + 4]:
            copy.wait()
        rows = pl.ds(h * SENT // 2, SENT // 2)
        here = [
            pltpu.make_async_copy(held.at[rows], out.at[d, rows], sem_out.at[d * 2 + h])
            for d in range(SIDE)
        ]
        for copy in here:
            copy.start()
        stores += here
    for copy in loads_own:
        copy.wait()
    stores.append(pltpu.make_async_copy(own, start, sem_out.at[2 * SIDE]))
    stores[-1].start()
    for copy in stores:
        copy.wait()


def panel_kernel(
    got, arrow, weight, own0, own1, own2, own3, out, panel, misc, sem_in, sem_out
):
    del own0, own1, own2, own3
    core, _, first = place()
    loads = [
        pltpu.make_async_copy(got.at[j, pl.ds(0, 5 * ROWS)], panel.at[j], sem_in.at[j])
        for j in range(SIDE)
    ]
    load_arrow = pltpu.make_async_copy(
        arrow.at[0], misc.at[pl.ds(2 * ROWS, ROWS)], sem_in.at[SIDE]
    )
    for copy in loads + [load_arrow]:
        copy.start()
    stores = []
    for j in range(SIDE):
        loads[j].wait()
        here = [
            pltpu.make_async_copy(
                panel.at[j, pl.ds(0, PART)],
                out.at[d, pl.ds(j * PART, PART)],
                sem_out.at[d * (SIDE + 1) + j],
            )
            for d in range(SIDE)
        ]
        for copy in here:
            copy.start()
        stores += here
    cols = [columns_t(panel, L0, natural(core, d, first)) for d in range(SIDE)]
    cols = jnp.concatenate(cols, axis=0)
    misc[: 2 * ROWS, :] = jnp.concatenate([cols[: 2 * ROWS], cols[2 * ROWS :]], axis=1)
    rest = weight[...]
    parts = []
    for _ in range(3):
        parts.append(rest.astype(BF).astype(F32))
        rest = rest - parts[-1]
    parts = jnp.concatenate(parts + [jnp.zeros((10, ROWS), F32)], axis=0)
    parts = jnp.concatenate([parts, jnp.zeros((16, HALF - ROWS), F32)], axis=1)
    misc[3 * ROWS :, :] = parts.astype(BF)
    load_arrow.wait()
    here = [
        pltpu.make_async_copy(misc, out.at[d, pl.ds(PANEL, MISC)], sem_out.at[d * (SIDE + 1) + SIDE])
        for d in range(SIDE)
    ]
    for copy in here:
        copy.start()
    for copy in stores + here:
        copy.wait()


def later_kernel(
    got,
    own0,
    own1,
    own2,
    own3,
    late0,
    late1,
    late2,
    late3,
    panel,
    state,
    share,
    sem_in,
    sem_out,
    sem_state,
):
    core, _, first = place()
    second = jnp.where(core == 0, lax.axis_index("y"), lax.axis_index("x"))
    lates = (late0, late1, late2, late3)
    loads = [
        pltpu.make_async_copy(got.at[j, pl.ds(PART, SENT - PART)], panel.at[j], sem_in.at[j])
        for j in range(SIDE)
    ]
    loads_state = [
        pltpu.make_async_copy(
            own.at[:, pl.ds(h * HALF, HALF)],
            state.at[pl.ds(k * PART + h * ROWS, ROWS)],
            sem_state.at[k * 3 + h],
        )
        for k, own in enumerate((own0, own1, own2, own3))
        for h in range(3)
    ]
    for copy in loads + loads_state:
        copy.start()
    for copy in loads + loads_state:
        copy.wait()
    stores = []
    for k, late in enumerate(lates):
        stores += [
            pltpu.make_async_copy(
                panel.at[j, pl.ds(0, PART)],
                late.at[pl.ds(j * PART, PART)],
                sem_out.at[k * (SIDE + 1) + j],
            )
            for j in range(SIDE)
        ]
        stores.append(
            pltpu.make_async_copy(state, late.at[pl.ds(LATER, PANEL)], sem_state.at[12 + k])
        )
    for copy in stores:
        copy.start()
    cols = [columns_t(panel, 0, natural(core, d, first)) for d in range(SIDE)]
    cols = jnp.concatenate(cols, axis=0)
    for h in range(2):
        at = PART + h * ROWS
        part = dot(cols, panel[:, at : at + ROWS, :].reshape(SIDE * ROWS, HALF))
        for d in range(SIDE):
            share[d, h * ROWS : (h + 1) * ROWS, :] = part[d * ROWS : (d + 1) * ROWS].astype(BF)
    here = [
        pltpu.make_async_copy(
            share.at[lax.rem(second + k, SIDE)],
            late.at[pl.ds(PANEL, SHARE)],
            sem_out.at[k * (SIDE + 1) + SIDE],
        )
        for k, late in enumerate(lates)
    ]
    for copy in here:
        copy.start()
    for copy in stores + here:
        copy.wait()


class Gathered:
    def __init__(self, mat):
        self.mat = mat

    def piece(self, k):
        return self.mat[:, k * ROWS : (k + 1) * ROWS, :].reshape(BLOCK, HALF)

    def over_rows(self, left, k):
        return dot(left, self.piece(k))

    def over_columns(self, left, k):
        return dot_t(left, self.piece(k))

    def times_factor(self, left_rows, left_tip):
        both = jnp.concatenate([self.over_rows(left_rows, h) for h in range(2)], axis=1)
        return both + self.over_columns(left_tip, 2)

    def past(self, left):
        u = self.over_columns(left[:, :HALF], 0) + self.over_columns(left[:, HALF:], 1)
        return u, self.over_rows(left, 2)


def load_exchanged(got, mat, sem):
    core, _, _ = place()
    return [
        pltpu.make_async_copy(
            got.at[d, pl.ds(j * PART, PART)],
            mat.at[natural(core, d, j)],
            sem.at[d * SIDE + j],
        )
        for d in range(SIDE)
        for j in range(SIDE)
    ]


def in_order(core, parts):
    even = jnp.concatenate(parts, axis=1)
    odd = [parts[d][:, j * 64 : (j + 1) * 64] for j in range(SIDE) for d in range(SIDE)]
    return jnp.where(core == 0, even, jnp.concatenate(odd, axis=1))


def sum_all(value):
    return jnp.sum(jnp.sum(value, axis=1, keepdims=True))


def trace_kernel(
    got,
    begun,
    panel_ref,
    arrow_ref,
    x_ref,
    q_ref,
    weight_ref,
    slope,
    factor,
    misc,
    state,
    inverse,
    arrow,
    x,
    q,
    sem_factor,
    sem_in,
):
    core, row, first = place()
    second = jnp.where(core == 0, lax.axis_index("y"), lax.axis_index("x"))
    near = pl.ds(pl.multiple_of(lax.div(row, 2) * 128, 128), 128)
    load_misc = pltpu.make_async_copy(got.at[:, pl.ds(PANEL, MISC)], misc, sem_in.at[0])
    load_factor = load_exchanged(got, factor, sem_factor)
    later = [
        pltpu.make_async_copy(begun.at[pl.ds(LATER, PANEL)], state, sem_in.at[1]),
        pltpu.make_async_copy(
            panel_ref.at[:, pl.ds(X1 * ROWS, 2 * ROWS)], inverse, sem_in.at[2]
        ),
        pltpu.make_async_copy(arrow_ref, arrow, sem_in.at[3]),
        pltpu.make_async_copy(q_ref, q, sem_in.at[4]),
        pltpu.make_async_copy(x_ref.at[:, :, near], x, sem_in.at[5]),
    ]
    for copy in [load_misc] + load_factor + later:
        copy.start()
    load_misc.wait()
    columns = [natural(core, d, first) for d in range(SIDE)]
    mine = [natural(core, second, lax.rem(first + SIDE - k, SIDE)) for k in range(SIDE)]
    parts = []
    for d in range(SIDE):
        held = misc[d, : 2 * ROWS, :]
        parts.append(jnp.concatenate([held[:, :256], held[:, 256:]], axis=0))
    z0 = in_order(core, parts)
    z0_tip = misc[:, 2 * ROWS : 3 * ROWS, :].reshape(256, HALF)
    eye = lax.broadcasted_iota(jnp.int32, (ROWS, ROWS), 0)
    eye = jnp.where(eye == lax.broadcasted_iota(jnp.int32, (ROWS, ROWS), 1), 1.0, 0.0)
    weights = []
    for block in range(2):
        column = []
        for d in range(SIDE):
            held = misc[d, 3 * ROWS :, :].astype(F32)
            held = held[block : block + 1] + held[block + 2 : block + 3] + held[block + 4 : block + 5]
            column.append(jnp.sum(eye * held[:, :ROWS], axis=1, keepdims=True))
        weights.append(jnp.concatenate(column, axis=0))
    for copy in load_factor:
        copy.wait()
    have = Gathered(factor)
    whole = jnp.concatenate([have.piece(0), have.piece(1)], axis=1)
    u = dot_t(z0, whole)
    u_tip = have.over_rows(z0, 2) - z0_tip.astype(F32)
    u_mine = jnp.zeros((256, 256), F32)
    z1_mine = []
    for h in range(2):
        low = jnp.concatenate([factor[b, h * ROWS : (h + 1) * ROWS, :] for b in mine], axis=0)
        u_mine += dot_t(z0[:, h * HALF : (h + 1) * HALF], low)
    z1 = jnp.concatenate([columns_t(factor, 0, c) for c in columns], axis=0)
    z1_mine = jnp.concatenate([columns_t(factor, 0, c, mine) for c in columns], axis=0)
    z1_tip = jnp.concatenate([factor[c, 2 * ROWS :, :] for c in columns], axis=0)
    for copy in later:
        copy.wait()
    rows_in = jnp.concatenate([u.astype(BF), z1], axis=0)
    tip_in = jnp.concatenate([u_tip.astype(BF), z1_tip], axis=0)
    held = state[...].reshape(SIDE, PART, HALF)
    held = [held[:, h * ROWS : (h + 1) * ROWS, :].reshape(256, HALF) for h in range(3)]
    through = dot_t(rows_in[:, :HALF], held[0]) + dot_t(rows_in[:, HALF:], held[1])
    through += 2.0 * dot_t(tip_in, held[2])
    carried = jnp.zeros((256, 256), F32)
    for h in range(2):
        part = inverse[:, h * ROWS : (h + 1) * ROWS, :].reshape(256, HALF)
        carried += dot_t(z0[:, h * HALF : (h + 1) * HALF], part)
    own_parts = parts[0]
    for d in range(1, SIDE):
        own_parts = jnp.where(second == d, parts[d], own_parts)
    traced = (u_mine * through[:256] + own_parts.astype(F32) * carried) * weights[0]
    traced += z1_mine.astype(F32) * through[256:] * weights[1]
    own_tip = u_tip[:ROWS]
    for d in range(1, SIDE):
        own_tip = jnp.where(second == d, u_tip[d * ROWS : (d + 1) * ROWS], own_tip)
    both = jnp.concatenate([own_tip.astype(BF), arrow[1]], axis=0)
    tip_traced = both.astype(F32) * dot(both, q[...])
    at = lax.broadcasted_iota(jnp.int32, (ROWS, 128), 0) + lax.rem(row, 2) * ROWS
    on_diagonal = lax.broadcasted_iota(jnp.int32, (ROWS, 128), 1) == at
    total = sum_all(traced)
    for block in range(2):
        total += sum_all(tip_traced[block * ROWS : (block + 1) * ROWS] * weight_ref[block])
        own = jnp.where(on_diagonal, x[block].astype(F32), 0.0)
        total += sum_all(own * weight_ref[block])
    slope[...] = jnp.full(slope.shape, total, F32)


def z0_own(misc, second, core):
    rows = pl.ds(pl.multiple_of(lax.rem(second, 2) * ROWS, ROWS), ROWS)
    lanes = pl.ds(pl.multiple_of(lax.div(second, 2) * 256, 256), 256)
    return in_order(core, [misc[d, rows, lanes] for d in range(SIDE)])


def block_kernel(
    got,
    late0,
    late1,
    late2,
    late3,
    arrow_ref,
    x_ref,
    q_ref,
    diag_ref,
    lower_ref,
    tip_ref,
    factor1,
    factor0,
    state,
    shares,
    misc,
    arrow,
    x,
    q,
    diag,
    lower,
    tip,
    sem_factor1,
    sem_factor0,
    sem_state,
    sem_share,
    sem_in,
    sem_out,
):
    core, row, first = place()
    second = jnp.where(core == 0, lax.axis_index("y"), lax.axis_index("x"))
    loads1 = [
        pltpu.make_async_copy(got.at[:, pl.ds(PANEL, MISC)], misc, sem_in.at[0]),
        pltpu.make_async_copy(arrow_ref, arrow, sem_in.at[1]),
    ] + load_exchanged(got, factor1, sem_factor1)
    loads_state = [pltpu.make_async_copy(q_ref, q, sem_in.at[2])]
    loads0 = [pltpu.make_async_copy(x_ref, x, sem_in.at[3])]
    for k, late in enumerate((late0, late1, late2, late3)):
        source = lax.rem(second + SIDE - k, SIDE)
        for j in range(SIDE):
            behind = lax.rem(first + SIDE - j, SIDE)
            loads_state.append(
                pltpu.make_async_copy(
                    late.at[pl.ds(LATER + j * PART, PART)],
                    state.at[natural(core, source, behind)],
                    sem_state.at[k * SIDE + j],
                )
            )
            loads0.append(
                pltpu.make_async_copy(
                    late.at[pl.ds(j * PART, PART)],
                    factor0.at[natural(core, source, j)],
                    sem_factor0.at[k * SIDE + j],
                )
            )
        loads0.append(
            pltpu.make_async_copy(late.at[pl.ds(PANEL, SHARE)], shares.at[k], sem_share.at[k])
        )
    for copy in loads1 + loads_state + loads0:
        copy.start()
    for copy in loads1:
        copy.wait()
    have = Gathered(factor1)
    z1 = columns_t(factor1, 0, row)
    z1_tip, z0_tip = arrow[1], arrow[0]
    u, u_tip = have.past(z0_own(misc, second, core))
    u_tip = u_tip - z0_tip.astype(F32)
    uh, ul = split(u)
    uh_tip, ul_tip = split(u_tip)
    rows_in = jnp.concatenate([z1, uh, ul], axis=0)
    tip_in = jnp.concatenate([z1_tip, uh_tip, ul_tip], axis=0)
    for copy in loads_state:
        copy.wait()
    begun = Gathered(state)
    top = begun.times_factor(rows_in, tip_in)
    bottom = begun.over_rows(rows_in, 2) + dot(tip_in, q[...])
    p1, a = top[:64], top[64:128] + top[128:]
    p1_tip, a_tip = bottom[:64], bottom[64:128] + bottom[128:]
    tip[1] = -p1_tip
    tip[0] = a_tip
    stores = [pltpu.make_async_copy(tip, tip_ref, sem_out.at[0])]
    stores[0].start()
    p1h, p1l = split(p1)
    ah, al = split(a)
    p1h_tip, p1l_tip = split(p1_tip)
    ah_tip, al_tip = split(a_tip)
    own = [state[row, h * ROWS : (h + 1) * ROWS, :] for h in range(3)]
    own_rows = jnp.concatenate(own[:2], axis=1)
    out = have.times_factor(
        jnp.concatenate([p1h, p1l, ah, al, own_rows], axis=0),
        jnp.concatenate([p1h_tip, p1l_tip, ah_tip, al_tip, own[2]], axis=0),
    )
    for copy in loads0:
        copy.wait()
    lower[1] = -out[256:]
    sigma1 = x[1].astype(F32) + out[:64] + out[64:128]
    diag[1] = sigma1
    here = [
        pltpu.make_async_copy(diag.at[1], diag_ref.at[1], sem_out.at[1]),
        pltpu.make_async_copy(lower.at[1], lower_ref.at[1], sem_out.at[2]),
    ]
    for copy in here:
        copy.start()
    stores += here
    carried = shares[0].astype(F32)
    for d in range(1, SIDE):
        carried += shares[d].astype(F32)
    carried = jnp.concatenate([carried[:ROWS], carried[ROWS:]], axis=1)
    p0h, p0l = split(carried + out[128:192] + out[192:256])
    out = Gathered(factor0).times_factor(
        jnp.concatenate([p0h, p0l, sigma1.astype(BF)], axis=0),
        jnp.concatenate([-ah_tip, -al_tip, -p1h_tip], axis=0),
    )
    lower[0] = -out[128:]
    diag[0] = x[0].astype(F32) + out[:64] + out[64:128]
    here = [
        pltpu.make_async_copy(diag.at[0], diag_ref.at[0], sem_out.at[3]),
        pltpu.make_async_copy(lower.at[0], lower_ref.at[0], sem_out.at[4]),
    ]
    for copy in here:
        copy.start()
    for copy in stores + here:
        copy.wait()


def on_device(
    lower_factor,
    arrow_factor,
    block_inverse,
    boundary_sigma,
    boundary_tip,
    tip_inverse,
    slope_weights,
    partitions,
):
    slow = pl.BlockSpec(memory_space=pltpu.HBM)
    fast = pl.BlockSpec(memory_space=pltpu.VMEM)
    params = pltpu.CompilerParams(vmem_limit_bytes=VMEM_BYTES)
    rows, start = pl.pallas_call(
        pack_kernel,
        out_shape=(
            jax.ShapeDtypeStruct((SIDE, SENT, HALF), BF),
            jax.ShapeDtypeStruct((ROWS, BLOCK + HALF), BF),
        ),
        in_specs=[slow] * 5,
        out_specs=(slow,) * 2,
        scratch_shapes=[
            pltpu.VMEM((SENT, HALF), BF),
            pltpu.VMEM((ROWS, BLOCK + HALF), BF),
            pltpu.SemaphoreType.DMA((8,)),
            pltpu.SemaphoreType.DMA((2,)),
            pltpu.SemaphoreType.DMA((2 * SIDE + 1,)),
        ],
        compiler_params=params,
        cost_estimate=cost(4),
    )(lower_factor, arrow_factor, block_inverse, boundary_sigma, boundary_tip)
    got = exchange(rows, line_groups(partitions, 0))
    starts = [lax.ppermute(start, EVERY, state_shift(partitions, k)) for k in range(SIDE)]
    sent = pl.pallas_call(
        panel_kernel,
        out_shape=jax.ShapeDtypeStruct((SIDE, PANEL + MISC, HALF), BF),
        in_specs=[slow, slow, fast] + [slow] * SIDE,
        out_specs=slow,
        scratch_shapes=[
            pltpu.VMEM((SIDE, 5 * ROWS, HALF), BF),
            pltpu.VMEM((MISC, HALF), BF),
            pltpu.SemaphoreType.DMA((SIDE + 1,)),
            pltpu.SemaphoreType.DMA((SIDE * (SIDE + 1),)),
        ],
        compiler_params=params,
        cost_estimate=cost(12),
    )(got, arrow_factor, slope_weights, *starts)
    lates = pl.pallas_call(
        later_kernel,
        out_shape=(jax.ShapeDtypeStruct((LATER + PANEL, HALF), BF),) * SIDE,
        in_specs=[slow] * 5,
        out_specs=(slow,) * 4,
        scratch_shapes=[
            pltpu.VMEM((SIDE, SENT - PART, HALF), BF),
            pltpu.VMEM((PANEL, HALF), BF),
            pltpu.VMEM((SIDE, SHARE, HALF), BF),
            pltpu.SemaphoreType.DMA((SIDE,)),
            pltpu.SemaphoreType.DMA((SIDE * (SIDE + 1),)),
            pltpu.SemaphoreType.DMA((16,)),
        ],
        compiler_params=params,
        cost_estimate=cost(12),
    )(got, *starts)
    lates = list(lates)
    early = exchange(sent, line_groups(partitions, 1))
    for k in range(1, SIDE):
        lates[k] = lax.ppermute(lates[k], EVERY, line_shift(partitions, k))
    slope = pl.pallas_call(
        trace_kernel,
        out_shape=jax.ShapeDtypeStruct((partitions // 2, 8, 128), F32),
        in_specs=[slow] * 6 + [fast],
        out_specs=fast,
        scratch_shapes=[
            pltpu.VMEM((16, PART, HALF), BF),
            pltpu.VMEM((SIDE, MISC, HALF), BF),
            pltpu.VMEM((PANEL, HALF), BF),
            pltpu.VMEM((SIDE, 2 * ROWS, HALF), BF),
            pltpu.VMEM((2, ROWS, HALF), BF),
            pltpu.VMEM((2, ROWS, 128), BF),
            pltpu.VMEM((HALF, HALF), BF),
            pltpu.SemaphoreType.DMA((16,)),
            pltpu.SemaphoreType.DMA((6,)),
        ],
        compiler_params=params,
        cost_estimate=cost(20),
    )(early, lates[0], got, arrow_factor, block_inverse, tip_inverse, slope_weights[:, :, None])
    total = jnp.sum(exchange(slope, height_groups(partitions)), axis=0)
    total = jnp.broadcast_to(total[None], (2 * SIDE * SIDE, 8, 128))
    total = jnp.sum(exchange(total, plane_groups(partitions)), axis=0)
    outputs = (
        jax.ShapeDtypeStruct((2, ROWS, BLOCK), F32),
        jax.ShapeDtypeStruct((2, ROWS, BLOCK), F32),
        jax.ShapeDtypeStruct((2, ROWS, HALF), F32),
    )
    diag, lower, tip = pl.pallas_call(
        block_kernel,
        out_shape=outputs,
        in_specs=[slow] * 8,
        out_specs=(slow,) * 3,
        scratch_shapes=[
            pltpu.VMEM((16, PART, HALF), BF),
            pltpu.VMEM((16, PART, HALF), BF),
            pltpu.VMEM((16, PART, HALF), BF),
            pltpu.VMEM((SIDE, SHARE, HALF), BF),
            pltpu.VMEM((SIDE, MISC, HALF), BF),
            pltpu.VMEM((2, ROWS, HALF), BF),
            pltpu.VMEM((2, ROWS, BLOCK), BF),
            pltpu.VMEM((HALF, HALF), BF),
        ]
        + [pltpu.VMEM(leaf.shape, F32) for leaf in outputs]
        + [
            pltpu.SemaphoreType.DMA((16,)),
            pltpu.SemaphoreType.DMA((16,)),
            pltpu.SemaphoreType.DMA((16,)),
            pltpu.SemaphoreType.DMA((SIDE,)),
            pltpu.SemaphoreType.DMA((4,)),
            pltpu.SemaphoreType.DMA((5,)),
        ],
        compiler_params=params,
        cost_estimate=cost(30),
    )(early, *lates, arrow_factor, block_inverse, tip_inverse)
    return diag, lower, tip, total[0, 0]


def solution(mesh):
    partitions = mesh.shape["tm"]
    fine = Mesh(mesh.devices.reshape(partitions, SIDE, SIDE), EVERY)
    rows = P("tm", ("y", "x"), None)

    def program(*args):
        return on_device(*args, partitions=partitions)

    return jax.shard_map(
        program,
        mesh=fine,
        in_specs=(rows, rows, rows, rows, rows, P(), P("tm", ("y", "x"))),
        out_specs=(rows, rows, rows, P()),
        check_vma=False,
    )
```
